32 devices in a mesh: rep: 8 (over z, y), shard: 4 (over x, core).
Axes of the slice: x: 2, y: 2, z: 4, core: 2. Of those that a mesh axis runs over, the one named last changes fastest.
Arguments:
- token_ids: int32 [16, 512], P('rep'), may hold values from 0 to 50271
- positions: int32 [16, 512], P('rep'), may hold values from 0 to 510, as said below
- segment_ids: int32 [16, 512], P('rep'), may hold values from 0 to 15, as said below
- pair_index: int32 [16, 8, 2], P('rep'), may hold values from -1 to 15, as said below
- embed_table: bfloat16 [50272, 1024], P('shard'), may hold values from -6 to 6
- pos_table: bfloat16 [2050, 1024], replicated, may hold values from -3 to 3
- base_qkv: bfloat16 [1024, 3072], P('rep'), may hold values from -0.1875 to 0.1875
- base_out: bfloat16 [1024, 1024], P('rep'), may hold values from -0.75 to 0.75
- base_up: bfloat16 [1024, 4096], P('rep'), may hold values from -0.1875 to 0.1875
- base_down: bfloat16 [4096, 1024], P('rep'), may hold values from -0.125 to 0.125
- base_gains: float32 [3, 1024], replicated, may hold values from 0.5 to 1.5
- base_bias: float32 [12288], replicated, may hold values from -1.75 to 1.75
- adapt_d: float32 [4, 1024, 2, 40], P('shard', 'rep'), may hold values from -0.1875 to 0.1875
- adapt_f: float32 [4, 4096, 16], P('shard', 'rep'), may hold values from -0.1875 to 0.1875
- head: float32 [4, 1024], P('shard', 'rep'), may hold values from -0.1875 to 0.1875
- mom_d: float32 [4, 1024, 2, 40], P('shard', 'rep'), may hold values from -7.6293945e-05 to 7.6293945e-05
- mom_f: float32 [4, 4096, 16], P('shard', 'rep'), may hold values from -7.6293945e-05 to 7.6293945e-05
- mom_head: float32 [4, 1024], P('shard', 'rep'), may hold values from -0.00024414062 to 0.00024414062
- err_d: float32 [4, 8, 1024, 2, 40], P('shard', 'rep'), may hold values from -0.046875 to 0.046875
- err_f: float32 [4, 8, 4096, 16], P('shard', 'rep'), may hold values from -0.046875 to 0.046875
- qstart_d: float32 [4, 2, 40, 8], P('shard'), may hold values from -6 to 6
- qstart_f: float32 [4, 16, 8], P('shard'), may hold values from -6 to 6
Outputs:
- loss_sum: float32 [], replicated
- pair_count: float32 [], replicated
- grad_norm: float32 [], replicated
- new_d: float32 [4, 1024, 2, 40], P('shard', 'rep')
- new_f: float32 [4, 4096, 16], P('shard', 'rep')
- new_head: float32 [4, 1024], P('shard', 'rep')
- new_mom_d: float32 [4, 1024, 2, 40], P('shard', 'rep')
- new_mom_f: float32 [4, 4096, 16], P('shard', 'rep')
- new_mom_head: float32 [4, 1024], P('shard', 'rep')
- new_err_d: float32 [4, 8, 1024, 2, 40], P('shard', 'rep')
- new_err_f: float32 [4, 8, 4096, 16], P('shard', 'rep')
- new_q_d: float32 [4, 2, 40, 8], P('shard')
- new_q_f: float32 [4, 16, 8], P('shard')
The draws below stay inside these ranges and needn't reach their ends.
Inputs may be any that keep to these rules, and one draw needn't show every extreme that they name: `segment_ids`: segment ids start at 0, rise by one at each segment start, every segment holds one token or more; a sequence has an even number of segments. `positions`: positions count from 0 at each segment's first token. `pair_index`: the live slots come first; a live slot names two distinct segments of its own sequence, each segment in exactly one live slot; every sequence has one live slot or more.
All inputs are finite; a program needn't handle non-finite values.
Results may differ from the reference program's by a relative error of at most 0.0033.
Values may be sent and summed in bfloat16 or wider, within the bound.
No kernel may reach another device: no remote copies, remote signals or barrier semaphores. Data moves between devices by JAX's collectives and lax.ppermute only.
A program may use at most 160 MiB of HBM per device.

```python
import math
import jax
import jax.numpy as jnp
import numpy as np
from jax import lax

MODEL_DIM = 1024
FEEDFORWARD_DIM = 4096
HEAD_DIM = 64
VOCAB = 50272
POS_ROWS = 2050
ADAPTER_RANK = 8
MICRO = 2
SEQUENCE_TOKENS = 512
PAIRS = 8
MEMBERS = 4
NSEQ = 16
N_REP = 8


def packing_layout(source):
    keys = jax.random.split(source, 3)
    seq_index = jnp.arange(NSEQ)
    live = jnp.clip(1 + seq_index * PAIRS // max(NSEQ - 1, 1) + jax.random.randint(keys[0], (NSEQ,), -1, 2), 1, PAIRS)
    single_seq = jax.random.randint(jax.random.fold_in(source, 7), (), 0, max(NSEQ - 1, 1))
    live = jnp.where(seq_index == single_seq, 1, live)
    orders = jax.vmap(lambda single: jax.random.permutation(single, SEQUENCE_TOKENS - 1))(jax.random.split(keys[1], NSEQ)) + 1
    cutoff = orders[:, :2 * PAIRS - 1]
    valid = jnp.arange(2 * PAIRS - 1)[None, :] < (2 * live - 1)[:, None]
    cutoff = jnp.where(valid, cutoff, SEQUENCE_TOKENS)
    first_cut = (seq_index[:, None] == single_seq) & (jnp.arange(2 * PAIRS - 1)[None, :] == 0)
    cutoff = jnp.where(first_cut, 1, cutoff)
    places = jnp.arange(SEQUENCE_TOKENS)
    below = cutoff[:, None, :] <= places[None, :, None]
    segment = jnp.sum(below, -1).astype(jnp.int32)
    starts = jnp.max(jnp.where(below, cutoff[:, None, :], 0), -1)
    position = (places[None, :] - starts).astype(jnp.int32)
    flips = jax.random.randint(keys[2], (NSEQ, PAIRS), 0, 2)
    slot_index = jnp.arange(PAIRS)[None, :]
    chosen = 2 * slot_index + flips
    rejected = 2 * slot_index + 1 - flips
    alive = slot_index < live[:, None]
    pairs = jnp.stack([jnp.where(alive, chosen, -1), jnp.where(alive, rejected, -1)], -1).astype(jnp.int32)
    return (segment, position, pairs)


def draw_positions(key, part):
    layout = packing_layout(key)
    return layout[1]


def draw_segment_ids(key, part):
    layout = packing_layout(key)
    return layout[0]


def draw_pair_index(key, part):
    layout = packing_layout(key)
    return layout[2]


def with_ends(drawn, rng, least, top_value):
    longest = drawn.shape.index(max(drawn.shape))
    spots = []
    for shift in (0, 1):
        where = [jax.random.randint(jax.random.fold_in(rng, axis), (), 0, length) for axis, length in enumerate(drawn.shape)]
        where[longest] = (where[longest] + shift) % drawn.shape[longest]
        spots.append(tuple(where))
    return drawn.at[spots[0]].set(least).at[spots[1]].set(top_value)


def levels(own_key, extent, cuts, smallest, high):
    level, own = 1.0, jax.random.fold_in(own_key, 6)
    for dim, shards_of in cuts:
        heights = jnp.exp(jax.random.uniform(jax.random.fold_in(own, dim), (shards_of,), jnp.float32, smallest / len(cuts), high / len(cuts)))
        level = level * jnp.repeat(heights, extent[dim] // shards_of).reshape([-1 if axis == dim else 1 for axis in range(len(extent))])
    return level


def rank_bounds(count, slope):
    weights = [(1 << 20) // math.isqrt(standing ** slope) + 1 for standing in range(1, count + 1)]
    width = 1 + sum(weights) // (1 << 30)
    return np.cumsum(np.array([max(1, weight // width) for weight in weights]))


def ranked(own_key, dims, count, lean):
    listing = rank_bounds(count, lean)
    lot = jax.random.randint(jax.random.fold_in(own_key, 1), dims, 0, int(listing[count - 1]))
    rank = jnp.searchsorted(jnp.asarray(listing, jnp.int32), lot, side="right")
    return jax.random.permutation(jax.random.fold_in(own_key, 2), count)[rank].astype(jnp.int32)


def centred(key, extent, width, reach, shards=(), held_as=jnp.bfloat16):
    loudness = levels(key, extent, shards, -0.22, 0.18) if shards else 1.0
    drawn = jax.random.normal(key, extent, jnp.float32) * width * loudness
    return jnp.minimum(jnp.maximum(drawn, -reach), reach).astype(held_as)


def setup_inputs(seed: int = 0) -> dict:
    arg_keys = jax.random.split(jax.random.key(seed), 23)
    return {
        "token_ids": with_ends(ranked(arg_keys[0], (NSEQ, SEQUENCE_TOKENS), VOCAB, 2), jax.random.fold_in(arg_keys[0], 3), 0, VOCAB - 1).astype(jnp.int32),
        "positions": draw_positions(jax.random.fold_in(arg_keys[22], 71), 0),
        "segment_ids": draw_segment_ids(jax.random.fold_in(arg_keys[22], 71), 0),
        "pair_index": draw_pair_index(jax.random.fold_in(arg_keys[22], 71), 0),
        "embed_table": centred(arg_keys[4], (VOCAB, MODEL_DIM), 1.0, 6.0, ((0, 4),)),
        "pos_table": centred(arg_keys[5], (POS_ROWS, MODEL_DIM), 0.5, 3.0),
        "base_qkv": centred(arg_keys[6], (MODEL_DIM, 3 * MODEL_DIM), MODEL_DIM ** -0.5, 0.1875, ((0, 8),)),
        "base_out": centred(arg_keys[7], (MODEL_DIM, MODEL_DIM), (MODEL_DIM // 16) ** -0.5, 0.75, ((0, 8),)),
        "base_up": centred(arg_keys[8], (MODEL_DIM, FEEDFORWARD_DIM), MODEL_DIM ** -0.5, 0.1875, ((0, 8),)),
        "base_down": centred(arg_keys[9], (FEEDFORWARD_DIM, MODEL_DIM), (FEEDFORWARD_DIM // 2) ** -0.5, 0.125, ((0, 8),)),
        "base_gains": jnp.clip(1.0 + 0.1 * jax.random.normal(arg_keys[10], (3, MODEL_DIM), jnp.float32), 0.5, 1.5),
        "base_bias": centred(arg_keys[11], (8 * MODEL_DIM + FEEDFORWARD_DIM,), 0.3, 1.75, (), jnp.float32),
        "adapt_d": centred(arg_keys[12], (MEMBERS, MODEL_DIM, 2, 5 * ADAPTER_RANK), MODEL_DIM ** -0.5, 0.1875, ((0, 4), (1, 8)), jnp.float32),
        "adapt_f": centred(arg_keys[13], (MEMBERS, FEEDFORWARD_DIM, 2 * ADAPTER_RANK), MODEL_DIM ** -0.5, 0.1875, ((0, 4), (1, 8)), jnp.float32),
        "head": centred(arg_keys[14], (MEMBERS, MODEL_DIM), MODEL_DIM ** -0.5, 0.1875, ((0, 4), (1, 8)), jnp.float32),
        "mom_d": centred(arg_keys[15], (MEMBERS, MODEL_DIM, 2, 5 * ADAPTER_RANK), (0.01 / (MEMBERS * (10 * MODEL_DIM * ADAPTER_RANK + 2 * FEEDFORWARD_DIM * ADAPTER_RANK + MODEL_DIM)) ** 0.5), 7.62939453125e-05, ((0, 4), (1, 8)), jnp.float32),
        "mom_f": centred(arg_keys[16], (MEMBERS, FEEDFORWARD_DIM, 2 * ADAPTER_RANK), (0.01 / (MEMBERS * (10 * MODEL_DIM * ADAPTER_RANK + 2 * FEEDFORWARD_DIM * ADAPTER_RANK + MODEL_DIM)) ** 0.5), 7.62939453125e-05, ((0, 4), (1, 8)), jnp.float32),
        "mom_head": centred(arg_keys[17], (MEMBERS, MODEL_DIM), (0.03 / (MEMBERS * (10 * MODEL_DIM * ADAPTER_RANK + 2 * FEEDFORWARD_DIM * ADAPTER_RANK + MODEL_DIM)) ** 0.5), 0.00024414062, ((0, 4), (1, 8)), jnp.float32),
        "err_d": centred(arg_keys[18], (MEMBERS, N_REP, MODEL_DIM, 2, 5 * ADAPTER_RANK), (0.5 / (NSEQ * MEMBERS)), 0.046875, ((0, 4), (1, 8)), jnp.float32),
        "err_f": centred(arg_keys[19], (MEMBERS, N_REP, FEEDFORWARD_DIM, 2 * ADAPTER_RANK), (0.5 / (NSEQ * MEMBERS)), 0.046875, ((0, 4), (1, 8)), jnp.float32),
        "qstart_d": centred(arg_keys[20], (MEMBERS, 2, 5 * ADAPTER_RANK, ADAPTER_RANK), 1.0, 6.0, ((0, 4),), jnp.float32),
        "qstart_f": centred(arg_keys[21], (MEMBERS, 2 * ADAPTER_RANK, ADAPTER_RANK), 1.0, 6.0, ((0, 4),), jnp.float32),
    }


FULL_PRECISION = lax.Precision.HIGHEST
CLIP = 0.01
MOMENTUM = 0.9
RATE = 1000.0
ADAPTER_SCALE = 2.0

@jax.custom_vjp
def low_precision_cast(v):
    return lax.optimization_barrier(v.astype(jnp.bfloat16)).astype(jnp.float32)

@jax.custom_vjp
def low_precision_return(v):
    return v

def low_keep(v):
    return (low_precision_cast(v), None)

def low_pass(kept, grad):
    return (grad,)

def back_keep(v):
    return (v, None)

def back_low(kept, grad):
    return (low_precision_cast(grad),)
low_precision_cast.defvjp(low_keep, low_pass)
low_precision_return.defvjp(back_keep, back_low)

def matrix_multiply(left, right):
    return jnp.matmul(left, right, precision=FULL_PRECISION)

def layer_norm(values, gain, shift):
    average = lax.optimization_barrier(jnp.mean(values, -1, keepdims=True))
    centered = values - average
    return centered * lax.rsqrt(lax.optimization_barrier(jnp.mean(centered * centered, -1, keepdims=True)) + 1e-05) * gain + shift

def orthonormal(matrix):
    columns = []
    for index in range(matrix.shape[-1]):
        vector = matrix[..., index]
        for basis in columns:
            vector = vector - lax.optimization_barrier(jnp.sum(basis * vector, -1, keepdims=True)) * basis
        vector = vector * lax.rsqrt(lax.optimization_barrier(jnp.sum(vector * vector, -1, keepdims=True)) + 1e-06)
        columns.append(vector)
    return jnp.stack(columns, -1)

def seq_reward(residual_initial, segment, member_d, member_feedforward, head_vec, base):
    query_key_value_weight, output_weight, up_weight, down_weight, gains, bias_vector = base
    adapter_input = member_d[:, 0]
    adapter_output = member_d[:, 1]
    first_layer_norm = low_precision_cast(layer_norm(residual_initial, gains[0], bias_vector[:MODEL_DIM]))
    adapter_triple = low_precision_return(low_precision_cast(matrix_multiply(first_layer_norm, adapter_input[:, :3 * ADAPTER_RANK])))
    adapter_terms = jnp.einsum('bvo,hvo->bvh', adapter_triple.reshape(SEQUENCE_TOKENS, 3, ADAPTER_RANK), adapter_output[:, :3 * ADAPTER_RANK].reshape(MODEL_DIM, 3, ADAPTER_RANK), precision=FULL_PRECISION).reshape(SEQUENCE_TOKENS, 3 * MODEL_DIM)
    projected_rows = low_precision_return(low_precision_cast(matrix_multiply(first_layer_norm, query_key_value_weight) + bias_vector[3 * MODEL_DIM:6 * MODEL_DIM] + ADAPTER_SCALE * adapter_terms))
    query_rows = projected_rows[:, :MODEL_DIM].reshape(SEQUENCE_TOKENS, -1, HEAD_DIM)
    key_rows = projected_rows[:, MODEL_DIM:2 * MODEL_DIM].reshape(SEQUENCE_TOKENS, -1, HEAD_DIM)
    value_rows = projected_rows[:, 2 * MODEL_DIM:].reshape(SEQUENCE_TOKENS, -1, HEAD_DIM)
    scores = low_precision_return(HEAD_DIM ** (-0.5) * jnp.einsum('qhd,khd->hqk', query_rows, key_rows, precision=FULL_PRECISION))
    places = jnp.arange(SEQUENCE_TOKENS)
    allowed = (segment[:, None] == segment[None, :]) & (places[None, :] <= places[:, None])
    scores = jnp.where(allowed[None], scores, -1000000000.0)
    attention = jax.nn.softmax(scores, -1)
    attended_values = low_precision_return(low_precision_cast(jnp.einsum('hqk,khd->qhd', low_precision_cast(attention), value_rows, precision=FULL_PRECISION).reshape(SEQUENCE_TOKENS, MODEL_DIM)))
    adapter_projection_output = low_precision_return(low_precision_cast(matrix_multiply(attended_values, adapter_input[:, 3 * ADAPTER_RANK:4 * ADAPTER_RANK])))
    residual_middle = residual_initial + low_precision_return(matrix_multiply(attended_values, output_weight) + bias_vector[6 * MODEL_DIM:7 * MODEL_DIM] + ADAPTER_SCALE * matrix_multiply(adapter_projection_output, adapter_output[:, 3 * ADAPTER_RANK:4 * ADAPTER_RANK].T))
    second_layer_norm = low_precision_return(low_precision_cast(layer_norm(residual_middle, gains[1], bias_vector[MODEL_DIM:2 * MODEL_DIM])))
    adapter_up = low_precision_return(low_precision_cast(matrix_multiply(second_layer_norm, adapter_input[:, 4 * ADAPTER_RANK:])))
    preactivation_hidden = low_precision_return(matrix_multiply(second_layer_norm, up_weight) + bias_vector[7 * MODEL_DIM:7 * MODEL_DIM + FEEDFORWARD_DIM] + ADAPTER_SCALE * matrix_multiply(adapter_up, member_feedforward[:, ADAPTER_RANK:].T))
    activated_hidden = low_precision_return(low_precision_cast(jax.nn.gelu(preactivation_hidden, approximate=True)))
    adapter_down = low_precision_return(low_precision_cast(matrix_multiply(activated_hidden, member_feedforward[:, :ADAPTER_RANK])))
    residual_final = residual_middle + low_precision_return(matrix_multiply(activated_hidden, down_weight) + bias_vector[7 * MODEL_DIM + FEEDFORWARD_DIM:] + ADAPTER_SCALE * matrix_multiply(adapter_down, adapter_output[:, 4 * ADAPTER_RANK:].T))
    final_norm = layer_norm(residual_final, gains[2], bias_vector[2 * MODEL_DIM:3 * MODEL_DIM])
    token_score = lax.optimization_barrier(jnp.sum(final_norm * head_vec, -1))
    is_last = jnp.concatenate([segment[1:] != segment[:-1], jnp.ones((1,), bool)])
    onehot = (segment[:, None] == jnp.arange(2 * PAIRS)[None, :]).astype(jnp.float32)
    return lax.optimization_barrier(jnp.sum(onehot * (token_score * is_last)[:, None], 0))

def reference(token_ids, positions, segment_ids, pair_index, embed_table, pos_table, base_qkv, base_out, base_up, base_down, base_gains, base_bias, adapt_d, adapt_f, head, mom_d, mom_f, mom_head, err_d, err_f, qstart_d, qstart_f):
    wide = jnp.float32
    resid_all = embed_table[token_ids].astype(wide) + pos_table[positions].astype(wide)
    resid_all = resid_all.reshape(N_REP, MICRO, SEQUENCE_TOKENS, MODEL_DIM)
    segments = segment_ids.reshape(N_REP, MICRO, SEQUENCE_TOKENS)
    base = (base_qkv.astype(wide), base_out.astype(wide), base_up.astype(wide), base_down.astype(wide), base_gains, base_bias)
    one_seq = jax.checkpoint(lambda resid, segment, member_d, member_feedforward, head_vec: seq_reward(resid, segment, member_d, member_feedforward, head_vec, base))

    def replica(item):
        rep_d, rep_f, rep_head, resid_rep, segment_rep = item
        low_d = low_precision_cast(rep_d)
        low_f = low_precision_cast(rep_f)
        low_head = low_precision_cast(rep_head)
        rows = []
        for member in range(MEMBERS):
            rows.append(jnp.stack([one_seq(resid_rep[batch], segment_rep[batch], low_d[member], low_f[member], low_head[member]) for batch in range(MICRO)]))
        return jnp.stack(rows)

    def loss_fn(all_d, all_f, all_head):
        rewards = lax.map(replica, (all_d, all_f, all_head, resid_all, segments))
        mean_reward = lax.optimization_barrier(jnp.mean(rewards, axis=1)).reshape(NSEQ, 2 * PAIRS)
        slots = jnp.arange(2 * PAIRS)
        pick_chosen = (pair_index[..., 0][..., None] == slots).astype(wide)
        pick_rejected = (pair_index[..., 1][..., None] == slots).astype(wide)
        reward_chosen = lax.optimization_barrier(jnp.sum(pick_chosen * mean_reward[:, None, :], -1))
        reward_rejected = lax.optimization_barrier(jnp.sum(pick_rejected * mean_reward[:, None, :], -1))
        live = (pair_index[..., 0] >= 0).astype(wide)
        total = jnp.sum(live * jax.nn.softplus(reward_rejected - reward_chosen))
        count = jnp.sum(live)
        return (total / count, (total, count))
    rep_d = jnp.broadcast_to(adapt_d[None], (N_REP,) + adapt_d.shape)
    rep_f = jnp.broadcast_to(adapt_f[None], (N_REP,) + adapt_f.shape)
    rep_head = jnp.broadcast_to(head[None], (N_REP,) + head.shape)
    loss_value, pullback, extras = jax.vjp(loss_fn, rep_d, rep_f, rep_head, has_aux=True)
    loss_sum, pair_count = extras
    grad_d, grad_f, grad_head = pullback(jnp.ones((), wide))
    mat_d = grad_d + err_d.transpose(1, 0, 2, 3, 4)
    mat_f = grad_f + err_f.transpose(1, 0, 2, 3)
    left_d = orthonormal(jnp.einsum('nmdjc,mjck->mjdk', mat_d, qstart_d, precision=FULL_PRECISION))
    left_f = orthonormal(jnp.einsum('nmfc,mck->mfk', mat_f, qstart_f, precision=FULL_PRECISION))
    new_q_d = jnp.einsum('nmdjc,mjdk->mjck', mat_d, left_d, precision=FULL_PRECISION)
    new_q_f = jnp.einsum('nmfc,mfk->mck', mat_f, left_f, precision=FULL_PRECISION)
    comp_d = jnp.einsum('mjdk,mjck->mdjc', left_d, new_q_d, precision=FULL_PRECISION)
    comp_f = jnp.einsum('mfk,mck->mfc', left_f, new_q_f, precision=FULL_PRECISION)
    comp_head = lax.optimization_barrier(jnp.sum(grad_head, 0))
    new_err_d = (mat_d - comp_d[None] / N_REP).transpose(1, 0, 2, 3, 4)
    new_err_f = (mat_f - comp_f[None] / N_REP).transpose(1, 0, 2, 3)
    grad_norm = jnp.sqrt(jnp.sum(comp_d * comp_d) + jnp.sum(comp_f * comp_f) + jnp.sum(comp_head * comp_head))
    clip = jnp.minimum(1.0, CLIP / (grad_norm + 1e-06))
    new_mom_d = MOMENTUM * mom_d + clip * comp_d
    new_mom_f = MOMENTUM * mom_f + clip * comp_f
    new_mom_head = MOMENTUM * mom_head + clip * comp_head
    return (loss_sum, pair_count, grad_norm, adapt_d - RATE * new_mom_d, adapt_f - RATE * new_mom_f, head - RATE * new_mom_head, new_mom_d, new_mom_f, new_mom_head, new_err_d, new_err_f, new_q_d, new_q_f)
```

```python
import functools
import math

import jax
import jax.numpy as jnp
import numpy as np
from jax import lax
from jax.experimental import pallas as pl
from jax.experimental.pallas import tpu as pltpu
from jax.sharding import PartitionSpec as P

HEAD_DIM = 64
F32 = jnp.float32
BF16 = jnp.bfloat16
EXACT = lax.Precision.HIGHEST
CLIP = 0.01
MOMENTUM = 0.9
RATE = 1000.0
SCALE = 2.0
AXES = ("rep", "shard")
PIECE_ROWS = 160


def nn(a, b, precision=None):
    return lax.dot_general(
        a, b, (((1,), (0,)), ((), ())), precision=precision, preferred_element_type=F32
    )


def nt(a, b, precision=None):
    return lax.dot_general(
        a, b, (((1,), (1,)), ((), ())), precision=precision, preferred_element_type=F32
    )


def tn(a, b, precision=None):
    return lax.dot_general(
        a, b, (((0,), (0,)), ((), ())), precision=precision, preferred_element_type=F32
    )


def iota(shape, dim):
    return lax.broadcasted_iota(jnp.int32, shape, dim)


def lanes(x, low, high):
    at = iota(x.shape, x.ndim - 1)
    return jnp.where((at >= low) & (at < high), x, jnp.zeros_like(x))


def norm_parts(x):
    centered = x - jnp.mean(x, -1, keepdims=True)
    rstd = lax.rsqrt(jnp.mean(centered * centered, -1, keepdims=True) + 1e-05)
    return centered * rstd, rstd


def norm_back(grad, gain, unit, rstd):
    g = grad * gain
    return rstd * (
        g - jnp.mean(g, -1, keepdims=True) - unit * jnp.mean(g * unit, -1, keepdims=True)
    )


def load_rows(pieces, offsets, target, sems, columns=None):
    copies = []
    for index, (piece, offset) in enumerate(zip(pieces, offsets, strict=True)):
        rows = piece.shape[0]
        if not isinstance(offset, int):
            offset = pl.multiple_of(offset, rows)
        source = piece if columns is None else piece.at[:, pl.ds(columns[0], columns[1])]
        copies.append(
            pltpu.make_async_copy(source, target.at[pl.ds(offset, rows), :], sems.at[index])
        )
    for copy in copies:
        copy.start()
    return copies


def expand_heads(x, heads):
    rows, width = x.shape
    head_of = iota((rows, width), 1) // HEAD_DIM
    return jnp.concatenate(
        [jnp.where(head_of == h, x, jnp.zeros_like(x)) for h in range(heads)], 0
    )


def collapse_heads(x, heads):
    rows, width = x.shape[0] // heads, x.shape[1]
    head_of = iota((rows, width), 1) // HEAD_DIM
    total = jnp.zeros((rows, width), F32)
    for h in range(heads):
        total = total + jnp.where(head_of == h, x[h * rows : (h + 1) * rows], 0.0)
    return total


def front_kernel(tok, pid, seg, nxt, table, gain, shift, h1, xl, hl, prow):
    tokens, slots = tok.shape[0], xl.shape[0]
    step = min(128, tokens)

    @pl.loop(0, tokens // step)
    def _(i):
        rows = pl.ds(pl.multiple_of(i * step, step), step)
        onehot = (pid[rows, :] == iota((step, table.shape[0]), 1)).astype(BF16)
        pos = nn(onehot, table[...])
        prow[rows, :] = pos.astype(BF16)
        unit, _ = norm_parts(tok[rows, :].astype(F32) + pos)
        h1[rows, :] = (unit * gain[...] + shift[...]).astype(BF16)

    segment = seg[...]
    last = (segment == iota((slots, tokens), 0)) & (segment != nxt[...])
    pick = last.astype(BF16)
    xl[...] = nn(pick, tok[...]) + nn(pick, prow[...])
    hl[...] = nn(pick, h1[...]).astype(BF16)


def kv_kernel(micro, pieces, rank, *refs):
    offs = refs[0]
    h1 = refs[1 : 1 + micro]
    ad, bias = refs[1 + micro : 3 + micro]
    weights = refs[3 + micro : 3 + micro + pieces]
    kv, ukv, wide, sems = refs[3 + micro + pieces :]
    width = h1[0].shape[1]
    tokens = h1[0].shape[0]
    copies = load_rows(
        weights, [offs[i] for i in range(pieces)], wide, sems, (width, 2 * width)
    )
    for b in range(micro):
        u = nt(h1[b][...], ad[0]).astype(BF16)
        ukv[b] = lanes(u, rank, 3 * rank)
    for copy in copies:
        copy.wait()
    block = 512
    for part in range(2):
        low, high = rank * (1 + part), rank * (2 + part)

        @pl.loop(0, width // block)
        def _(i, part=part, low=low, high=high):
            cols = pl.ds(pl.multiple_of(i * block, block), block)
            wcols = pl.ds(pl.multiple_of(part * width + i * block, block), block)
            for b in range(micro):
                total = nn(h1[b][...], wide[:, wcols])
                total = total + bias[:, wcols]
                total = total + SCALE * nn(lanes(ukv[b], low, high), ad[1, :, cols])
                kv[b, :, wcols] = total.astype(BF16)


def rows_kernel(micro, pieces, rank, *refs):
    offs, seg = refs[:2]
    hl = refs[2 : 2 + micro]
    xl = refs[2 + micro : 2 + 2 * micro]
    kv, ad, bias_q, bias_o, gain, shift = refs[2 + 2 * micro : 8 + 2 * micro]
    weights = refs[8 + 2 * micro : 8 + 2 * micro + pieces]
    o, x1, e1, q, p, u, wide, sems = refs[8 + 2 * micro + pieces :]
    slots, width = hl[0].shape
    heads = width // HEAD_DIM
    tokens = kv.shape[1]
    places = [offs[i] for i in range(pieces)]
    copies = load_rows(weights, places, wide.at[:, pl.ds(0, width)], sems.at[0], (0, width))
    copies += load_rows(
        weights, places, wide.at[:, pl.ds(width, width)], sems.at[1], (3 * width, width)
    )
    for copy in copies:
        copy.wait()
    h_last = jnp.concatenate([h[...] for h in hl], 0)
    x_last = jnp.concatenate([x[...] for x in xl], 0)
    down, up = ad[0], ad[1]
    u_q = lanes(nt(h_last, down).astype(BF16), 0, rank)
    q_all = (nn(h_last, wide[:, :width]) + bias_q[...] + SCALE * nn(u_q, up)).astype(BF16)
    q[...] = q_all
    parts = []
    for b in range(micro):
        wide_q = expand_heads(q_all[b * slots : (b + 1) * slots], heads)
        scores = HEAD_DIM ** (-0.5) * nt(wide_q, kv[b, :, :width])
        inside = seg[b] == iota((slots, tokens), 0)
        inside = jnp.concatenate([inside.astype(F32)] * heads, 0) > 0.5
        scores = jnp.where(inside, scores, -1000000000.0)
        top = jnp.max(scores, -1, keepdims=True)
        e = jnp.exp(scores - top)
        probs = e / jnp.sum(e, -1, keepdims=True)
        p[b] = probs
        parts.append(collapse_heads(nn(probs.astype(BF16), kv[b, :, width:]), heads))
    o_all = jnp.concatenate(parts, 0).astype(BF16)
    o[...] = o_all
    u_o = lanes(nt(o_all, down).astype(BF16), 3 * rank, 4 * rank)
    mid = x_last + nn(o_all, wide[:, width:]) + bias_o[...] + SCALE * nn(u_o, up)
    x1[...] = mid
    unit, _ = norm_parts(mid)
    h2 = (unit * gain[...] + shift[...]).astype(BF16)
    u_up = lanes(nt(h2, down).astype(BF16), 4 * rank, 5 * rank)
    e1[:, :width] = h2
    e1[:, width:] = jnp.zeros_like(e1[:, width:])
    e1[:, width : width + 5 * rank] = u_up
    u[...] = u_q + u_o + u_up


def up_kernel(pieces, rank, *refs):
    offs, own, sib, f_own, f_sib, bias = refs[:6]
    weights = refs[6 : 6 + pieces]
    f, a, wide, sems = refs[6 + pieces :]
    width = wide.shape[0]
    copies = load_rows(weights, [offs[i] for i in range(pieces)], wide, sems)
    for copy in copies:
        copy.wait()
    rows = own.shape[0]
    h2 = jnp.concatenate([own[:, :width], sib[:, :width]], 0)
    lane = 5 * rank
    extra = jnp.concatenate(
        [
            nn(own[:, width : width + lane], f_own[1]),
            nn(sib[:, width : width + lane], f_sib[1]),
        ],
        0,
    )
    total = nn(h2, wide[...]) + bias[...] + SCALE * extra
    f[...] = total
    a[...] = jax.nn.gelu(total, approximate=True).astype(BF16)
    del rows


def down_kernel(pieces, rank, *refs):
    offs, a, f_own, f_sib = refs[:4]
    weights = refs[4 : 4 + pieces]
    mine, send, wide, sems = refs[4 + pieces :]
    width = wide.shape[1]
    copies = load_rows(weights, [offs[i] for i in range(pieces)], wide, sems)
    for copy in copies:
        copy.wait()
    rows = a.shape[0] // 2
    lane = 5 * rank
    y = nn(a[...], wide[...])
    for out, low, factor in ((mine, 0, f_own), (send, rows, f_sib)):
        out[:, :width] = y[low : low + rows]
        out[:, width:] = jnp.zeros_like(out[:, width:])
        out[:, width : width + lane] = nt(a[low : low + rows, :], factor[0])


def score_kernel(rank, x1, mine, recv, ad, bias, gain, shift, head, x2, u_dn, score):
    width = x1.shape[1]
    lane = 5 * rank
    u = (mine[:, width : width + lane] + recv[:, width : width + lane]).astype(BF16)
    u_dn[...] = u
    end = x1[...] + mine[:, :width] + recv[:, :width] + bias[...] + SCALE * nn(u, ad[1])
    x2[...] = end
    unit, _ = norm_parts(end)
    token = jnp.sum((unit * gain[...] + shift[...]) * head[...], -1, keepdims=True)
    score[...] = jnp.broadcast_to(token, score.shape)


def loss_kernel(rank, members, *refs):
    scores = refs[:members]
    x2, u_dn, pick, live, count, ad, gain, shift, head = refs[members : members + 9]
    e2, g_end, g_dn, small = refs[members + 9 :]
    rows, width = x2.shape
    half = rows // 2

    def value(m):
        if m % 2 == 0:
            return scores[m][...]
        return jnp.concatenate([scores[m][half:, :], scores[m][:half, :]], 0)

    level = [value(m) for m in range(members)]
    while len(level) > 1:
        level = [level[i] + level[i + 1] for i in range(0, len(level), 2)]
    mean_reward = level[0][:, :1] / members
    diff = jnp.sum(pick[...] * mean_reward, 0, keepdims=True)
    terms = live[...] * jax.nn.softplus(-diff)
    grad_diff = -live[...] * jax.nn.sigmoid(-diff) / count[:, :1]
    grad_score = jnp.sum(pick[...] * grad_diff, -1, keepdims=True) / members
    unit, rstd = norm_parts(x2[...])
    final = unit * gain[...] + shift[...]
    small[...] = jnp.zeros_like(small)
    small[0:1, :] = jnp.sum(final * grad_score, 0, keepdims=True)
    small[1:2, :] = jnp.broadcast_to(jnp.sum(terms, -1, keepdims=True), (1, width))
    end = norm_back(grad_score * head[...], gain[...], unit, rstd)
    g_end[...] = end
    g_ff = end.astype(BF16)
    left = lanes((SCALE * nt(g_ff, ad[1])).astype(BF16), 4 * rank, 5 * rank)
    g_dn[...] = SCALE * tn(u_dn[...], g_ff)
    e2[:, :width] = g_ff
    e2[:, width:] = jnp.zeros_like(e2[:, width:])
    e2[:, width : width + 5 * rank] = left


def ffn_back_kernel(up_pieces, down_pieces, rank, *refs):
    offs_u, offs_d, own, sib, e1_own, e1_sib, f, a, f_own, f_sib = refs[:10]
    ups = refs[10 : 10 + up_pieces]
    downs = refs[10 + up_pieces : 10 + up_pieces + down_pieces]
    mine, send, gf_mine, gf_send, wide_u, wide_d, sems_u, sems_d = refs[
        10 + up_pieces + down_pieces :
    ]
    width = wide_u.shape[0]
    lane = 5 * rank
    copies_d = load_rows(downs, [offs_d[i] for i in range(down_pieces)], wide_d, sems_d)
    copies_u = load_rows(ups, [offs_u[i] for i in range(up_pieces)], wide_u, sems_u)
    rows = own.shape[0]
    x = f[...]
    c0, c1 = math.sqrt(2.0 / math.pi), 0.044715
    t = jnp.tanh(c0 * (x + c1 * x * x * x))
    slope = 0.5 * (1.0 + t) + 0.5 * x * (1.0 - t * t) * (c0 * (1.0 + 3.0 * c1 * x * x))
    left_own, left_sib = own[:, width : width + lane], sib[:, width : width + lane]
    u_own, u_sib = e1_own[:, width : width + lane], e1_sib[:, width : width + lane]
    g_ff = jnp.concatenate([own[:, :width], sib[:, :width]], 0)
    extra = jnp.concatenate([nn(left_own, f_own[0]), nn(left_sib, f_sib[0])], 0)
    for copy in copies_d:
        copy.wait()
    g_a = (nt(g_ff, wide_d[...]) + extra).astype(BF16)
    g_f = (g_a.astype(F32) * slope).astype(BF16)
    for copy in copies_u:
        copy.wait()
    g_h = nt(g_f, wide_u[...])
    for out, gout, low, factor, left, u in (
        (mine, gf_mine, 0, f_own, left_own, u_own),
        (send, gf_send, rows, f_sib, left_sib, u_sib),
    ):
        part = g_f[low : low + rows]
        out[:, :width] = g_h[low : low + rows]
        out[:, width:] = jnp.zeros_like(out[:, width:])
        out[:, width : width + lane] = SCALE * nt(part, factor[1])
        gout[0:rank, :] = tn(left, a[low : low + rows, :])[4 * rank :]
        gout[rank:, :] = SCALE * tn(u, part)[4 * rank :]


def factor_kernel(grad, err, start, mat, left):
    mat[...] = grad[...] + err[...]
    left[...] = nn(start[...], mat[...], EXACT)


def rows_back_kernel(micro, pieces, rank, *refs):
    offs, mine, recv, x1, g_end, e1, u, o, q, p, kv, ukv = refs[:12]
    hl = refs[12 : 12 + micro]
    h1 = refs[12 + micro : 12 + 2 * micro]
    ad, gain, g_dn, err, start, small = refs[12 + 2 * micro : 18 + 2 * micro]
    weights = refs[18 + 2 * micro : 18 + 2 * micro + pieces]
    mat, left, wide, sems = refs[18 + 2 * micro + pieces :]
    rows, width = x1.shape
    slots = rows // micro
    heads = width // HEAD_DIM
    lane = 5 * rank
    copies = load_rows(weights, [offs[i] for i in range(pieces)], wide, sems, (3 * width, width))
    down, up = ad[0], ad[1]
    h2 = e1[:, :width]
    u_rows = u[...]
    g_u = (mine[:, width : width + lane] + recv[:, width : width + lane]).astype(BF16)
    g_h2 = (mine[:, :width] + recv[:, :width] + nn(g_u, down)).astype(BF16)
    grad_in = tn(g_u, h2)
    unit, rstd = norm_parts(x1[...])
    g_mid = g_end[...] + norm_back(g_h2.astype(F32), gain[...], unit, rstd)
    g_att = g_mid.astype(BF16)
    grad_out = g_dn[...] + SCALE * tn(lanes(u_rows, 3 * rank, 4 * rank), g_att)
    g_ol = lanes((SCALE * nt(g_att, up)).astype(BF16), 3 * rank, 4 * rank)
    grad_in = grad_in + tn(g_ol, o[...])
    for copy in copies:
        copy.wait()
    g_o = (nt(g_att, wide[...]) + nn(g_ol, down)).astype(BF16)
    scale = HEAD_DIM ** (-0.5)
    for b in range(micro):
        pick = slice(b * slots, (b + 1) * slots)
        wide_g = expand_heads(g_o[pick], heads)
        wide_q = expand_heads(q[pick, :], heads)
        probs = p[b]
        g_p = nt(wide_g, kv[b, :, width:])
        g_s = (probs * (g_p - jnp.sum(probs * g_p, -1, keepdims=True))).astype(BF16)
        g_q = (scale * collapse_heads(nn(g_s, kv[b, :, :width]), heads)).astype(BF16)
        g_k = (scale * tn(g_s, wide_q)).astype(BF16)
        g_v = tn(probs.astype(BF16), wide_g).astype(BF16)
        u_q = lanes(u_rows[pick], 0, rank)
        u_k, u_v = lanes(ukv[b], rank, 2 * rank), lanes(ukv[b], 2 * rank, 3 * rank)
        grad_out = grad_out + SCALE * (tn(u_q, g_q) + tn(u_k, g_k) + tn(u_v, g_v))
        g_uq = lanes((SCALE * nt(g_q, up)).astype(BF16), 0, rank)
        g_ukv = lanes((SCALE * nt(g_k, up)).astype(BF16), rank, 2 * rank) + lanes(
            (SCALE * nt(g_v, up)).astype(BF16), 2 * rank, 3 * rank
        )
        grad_in = grad_in + tn(g_uq, hl[b][...]) + tn(g_ukv, h1[b][...])
    mat[0] = grad_in + err[0]
    mat[1] = grad_out + err[1]
    first = start.shape[1]
    left[0:first, :] = nn(start[0], mat[0], EXACT)
    left[first : 2 * first, :] = nn(start[1], mat[1], EXACT)
    left[2 * first :, :] = small[...]


def orthonormal_rows(ref):
    count = ref.shape[0]
    at = iota(ref.shape, 0)
    for k in range(count):
        row = ref[k : k + 1, :]
        row = row * lax.rsqrt(jnp.sum(row * row, -1, keepdims=True) + 1e-06)
        ref[k : k + 1, :] = row
        if k + 1 < count:
            block = ref[...]
            dots = jnp.sum(block * row, -1, keepdims=True)
            ref[...] = jnp.where(at > k, block - dots * row, block)


def ortho_kernel(rank, left_d, left_f, mat_d, mat_f, ph_d, ph_f, new_q):
    count = ph_f.shape[0]
    ph_f[...] = left_f[...]
    orthonormal_rows(ph_f)
    new_q[...] = jnp.zeros_like(new_q)
    for j in range(2):
        ph_d[j] = left_d[j * count : (j + 1) * count, :]
        orthonormal_rows(ph_d.at[j])
        new_q[j * count : (j + 1) * count, : 5 * rank] = nt(ph_d[j], mat_d[j], EXACT)
    new_q[2 * count : 3 * count, : 2 * rank] = nt(ph_f[...], mat_f[...], EXACT)


def comp_kernel(rank, replicas, new_q, ph_d, ph_f, mat_d, mat_f, head, err_d, err_f, squares):
    count = ph_f.shape[0]
    total = jnp.sum(head[...] * head[...], keepdims=True)
    for j in range(2):
        comp = tn(new_q[j * count : (j + 1) * count, : 5 * rank], ph_d[j], EXACT)
        total = total + jnp.sum(comp * comp, keepdims=True)
        err_d[j] = mat_d[j] - comp * (1.0 / replicas)
    comp = tn(new_q[2 * count : 3 * count, : 2 * rank], ph_f[...], EXACT)
    total = total + jnp.sum(comp * comp, keepdims=True)
    err_f[...] = mat_f[...] - comp * (1.0 / replicas)
    squares[...] = jnp.broadcast_to(total, squares.shape)


def update_kernel(rank, total, new_q, ph_d, ph_f, ghead, wd, wf, wh, md, mf, mh,
                  nd, nf, nh, nmd, nmf, nmh, norm):
    count = ph_f.shape[0]
    grad_norm = jnp.sqrt(total[0:1, 0:1])
    norm[...] = jnp.broadcast_to(grad_norm, norm.shape)
    clip = jnp.minimum(1.0, CLIP / (grad_norm + 1e-06))
    for j in range(2):
        comp = tn(new_q[j * count : (j + 1) * count, : 5 * rank], ph_d[j], EXACT)
        fresh = MOMENTUM * md[j] + clip * comp
        nmd[j] = fresh
        nd[j] = wd[j] - RATE * fresh
    comp = tn(new_q[2 * count : 3 * count, : 2 * rank], ph_f[...], EXACT)
    fresh = MOMENTUM * mf[...] + clip * comp
    nmf[...] = fresh
    nf[...] = wf[...] - RATE * fresh
    fresh = MOMENTUM * mh[...] + clip * ghead[...]
    nmh[...] = fresh
    nh[...] = wh[...] - RATE * fresh


def call(kernel, outs, args, scratch=(), vmem=40, flops=0, name=None):
    spaces = {"v": pltpu.VMEM, "s": pltpu.SMEM, "a": pl.ANY}
    size = sum(math.prod(o.shape) * o.dtype.itemsize for o in outs)
    size += sum(math.prod(a.shape) * a.dtype.itemsize for a, _ in args)
    return pl.pallas_call(
        kernel,
        out_shape=tuple(outs),
        in_specs=[pl.BlockSpec(memory_space=spaces[k]) for _, k in args],
        out_specs=tuple(pl.BlockSpec(memory_space=pltpu.VMEM) for _ in outs),
        scratch_shapes=list(scratch),
        compiler_params=pltpu.CompilerParams(vmem_limit_bytes=vmem << 20),
        cost_estimate=pl.CostEstimate(flops=int(flops), bytes_accessed=int(size), transcendentals=0),
        name=name,
    )(*[a for a, _ in args])


def shaped(shape, dtype):
    return jax.ShapeDtypeStruct(tuple(shape), dtype)


def ring_order(count):
    side = math.isqrt(count // 2)
    if side < 2 or 2 * side * side != count:
        return list(range(count))
    depth = 2 * side
    cells = []
    for z in range(depth):
        ys = range(1, side) if z % 2 == 0 else range(side - 1, 0, -1)
        cells += [(z, y) for y in ys]
    cells += [(z, 0) for z in range(depth - 1, -1, -1)]
    return [z * side + y for z, y in cells]


def pairs_of(n, m, move):
    return [(r * m + s, t[0] * m + t[1]) for r in range(n) for s in range(m) for t in [move(r, s)]]


def on_device(n, m, *args):
    (
        token_ids, positions, segment_ids, pair_index, embed_table, pos_table,
        base_qkv, base_out, base_up, base_down, base_gains, base_bias,
        adapt_d, adapt_f, head, mom_d, mom_f, mom_head, err_d, err_f, qstart_d, qstart_f,
    ) = args
    micro, tokens = token_ids.shape
    width = embed_table.shape[1]
    pairs = pair_index.shape[1]
    slots = 2 * pairs
    rows = micro * slots
    hidden = base_up.shape[1]
    rank = adapt_f.shape[2] // 2
    heads = width // HEAD_DIM
    rd, rf = base_up.shape[0], base_down.shape[0]
    half = rf // 2
    own_hidden = hidden // 2
    rep, shard = lax.axis_index("rep"), lax.axis_index("shard")
    core = shard % 2

    order = ring_order(n)
    place = {r: i for i, r in enumerate(order)}
    around = pairs_of(
        n, m, lambda r, s: (order[(place[r] + (1 if s % 2 == 0 else -1)) % n], s)
    )
    sibling = pairs_of(n, m, lambda r, s: (r, s ^ 1))
    source = np.array(
        [
            [[order[(place[r] + (-k if c == 0 else k)) % n] for k in range(n)] for c in range(2)]
            for r in range(n)
        ],
        np.int32,
    )
    mine_at = lax.dynamic_slice(jnp.asarray(source), (rep, core, 0), (1, 1, n)).reshape(n)
    other_at = lax.dynamic_slice(jnp.asarray(source), (rep, 1 - core, 0), (1, 1, n)).reshape(n)

    def swap(x):
        return lax.ppermute(x, AXES, sibling)

    def ring(x):
        out = []
        for _ in range(n - 1):
            x = lax.ppermute(x, AXES, around)
            out.append(x)
        return out

    def pick(x, index, axis):
        return lax.dynamic_index_in_dim(x, index, axis, keepdims=False)

    first = jnp.concatenate([base_qkv, base_out], 1)
    first_half = pick(first.reshape(2, rd // 2, 4 * width), core, 0)
    up_half = pick(base_up.reshape(rd, n, 2, half), core, 2).reshape(rd, own_hidden)
    down_half = pick(base_down.reshape(2, half, width), core, 0)
    got = ring(first_half)
    got_sib = [swap(x) for x in got]
    ups = [up_half] + ring(up_half)
    downs = [down_half] + ring(down_half)
    firsts = [first] + got + got_sib
    first_at = jnp.concatenate(
        [mine_at[:1] * rd, mine_at[1:] * rd + core * (rd // 2), other_at[1:] * rd + (1 - core) * (rd // 2)]
    )
    up_at = mine_at * rd
    down_at = mine_at * half
    count_first, count_up, count_down = len(firsts), len(ups), len(downs)

    def local(x):
        return jnp.where(core == 0, x, x[::-1])

    segment = local(segment_ids)
    following = jnp.concatenate([segment[:, 1:], jnp.full((micro, 1), -1, segment.dtype)], 1)
    segment, following = segment[:, None, :], following[:, None, :]
    pos_col = local(positions)[:, :, None]
    pair_local = local(pair_index)
    live = (pair_local[..., 0] >= 0).astype(F32)
    slot = jnp.arange(slots)
    chosen = (pair_local[..., 0][:, None, :] == slot[None, :, None]).astype(F32)
    rejected = (pair_local[..., 1][:, None, :] == slot[None, :, None]).astype(F32)
    pick_t = (chosen - rejected)[:, :, None, :] * jnp.eye(micro, dtype=F32)[:, None, :, None]
    pick_t = pick_t.reshape(rows, micro * pairs)
    live_row = live.reshape(1, micro * pairs)

    def lookup(ids):
        held = embed_table.shape[0]
        near = ids - shard * held
        inside = (near >= 0) & (near < held)
        found = jnp.take(embed_table, jnp.clip(near, 0, held - 1), axis=0)
        return jnp.where(inside[:, None], found, jnp.zeros_like(found))

    ids = local(token_ids)
    for_sib = lookup(ids[1])
    tok = lookup(ids[0]) + swap(for_sib)
    bit = 2
    while bit < m:
        tok = tok + lax.ppermute(tok, AXES, pairs_of(n, m, lambda r, s, bit=bit: (r, s ^ bit)))
        bit *= 2
    toks = [tok, swap(tok)]

    d_t = adapt_d[0].transpose(1, 2, 0)
    f_t = adapt_f[0].T
    piece = jnp.concatenate(
        [
            d_t.reshape(10 * rank, rd),
            f_t.reshape(2 * rank * (rf // rd), rd),
            head,
            jnp.broadcast_to(jnp.sum(live), (1, rd)),
        ],
        0,
    ).astype(BF16)
    piece = jnp.pad(piece, ((0, PIECE_ROWS - piece.shape[0]), (0, 0)))[None]
    bit = 1
    while bit < n:
        got_piece = lax.ppermute(piece, AXES, pairs_of(n, m, lambda r, s, bit=bit: (r ^ bit, s)))
        high = (rep // bit) % 2 == 1
        piece = jnp.concatenate(
            [jnp.where(high, got_piece, piece), jnp.where(high, piece, got_piece)], 0
        )
        bit *= 2
    wide_d = piece[:, : 10 * rank].transpose(1, 0, 2).reshape(2, 5 * rank, width)
    f_rows = 2 * rank * (rf // rd)
    wide_f = piece[:, 10 * rank : 10 * rank + f_rows].reshape(n, 2 * rank, 2, half // rd, rd)
    wide_f = wide_f.transpose(2, 1, 0, 3, 4).reshape(2, 2 * rank, own_hidden)
    wide_head = piece[:, 10 * rank + f_rows].reshape(1, width).astype(F32)
    count = jnp.sum(piece[:, 10 * rank + f_rows + 1, 0].astype(F32))
    count_row = jnp.broadcast_to(count, (1, 128))

    def factors(x):
        zero = jnp.zeros((4 * rank, own_hidden), BF16)
        return jnp.stack(
            [jnp.concatenate([zero, x[:rank]], 0), jnp.concatenate([zero, x[rank:]], 0)]
        )

    f_own = factors(pick(wide_f, core, 0))
    f_sib = factors(swap(pick(wide_f, 1 - core, 0)))

    gain = [base_gains[i : i + 1] for i in range(3)]
    shift = [base_bias[i * width : (i + 1) * width][None] for i in range(3)]
    bias_q = base_bias[3 * width : 4 * width][None]
    bias_kv = base_bias[4 * width : 6 * width][None]
    bias_o = base_bias[6 * width : 7 * width][None]
    bias_1 = pick(base_bias[7 * width : 7 * width + hidden].reshape(n, 2, half), core, 1).reshape(1, own_hidden)
    bias_2 = base_bias[7 * width + hidden :][None]

    h1, xl, hl = [], [], []
    for b in range(micro):
        a, x, h = call(
            front_kernel,
            [shaped((tokens, width), BF16), shaped((slots, width), F32), shaped((slots, width), BF16)],
            [(toks[b], "v"), (pos_col[b], "v"), (segment[b], "v"), (following[b], "v"),
             (pos_table[:tokens], "v"), (gain[0], "v"), (shift[0], "v")],
            [pltpu.VMEM((tokens, width), BF16)],
            flops=2 * tokens * tokens * width, name="front",
        )
        h1.append(a)
        xl.append(x)
        hl.append(h)

    kv, ukv = call(
        functools.partial(kv_kernel, micro, count_first, rank),
        [shaped((micro, tokens, 2 * width), BF16), shaped((micro, tokens, 5 * rank), BF16)],
        [(first_at, "s")] + [(x, "v") for x in h1] + [(wide_d, "v"), (bias_kv, "v")]
        + [(x, "a") for x in firsts],
        [pltpu.VMEM((width, 2 * width), BF16), pltpu.SemaphoreType.DMA((count_first,))],
        flops=4 * micro * tokens * width * width, name="kv",
    )

    o, x1, e1, q, p, u = call(
        functools.partial(rows_kernel, micro, count_first, rank),
        [shaped((rows, width), BF16), shaped((rows, width), F32), shaped((rows, width + 128), BF16),
         shaped((rows, width), BF16), shaped((micro, heads * slots, tokens), F32), shaped((rows, 5 * rank), BF16)],
        [(first_at, "s"), (segment, "v")] + [(x, "v") for x in hl] + [(x, "v") for x in xl]
        + [(kv, "v"), (wide_d, "v"), (bias_q, "v"), (bias_o, "v"), (gain[1], "v"), (shift[1], "v")]
        + [(x, "a") for x in firsts],
        [pltpu.VMEM((width, 2 * width), BF16), pltpu.SemaphoreType.DMA((2, count_first))],
        flops=8 * rows * tokens * width * 8, name="rows",
    )

    e1_sib = swap(e1)
    f, a = call(
        functools.partial(up_kernel, count_up, rank),
        [shaped((2 * rows, own_hidden), F32), shaped((2 * rows, own_hidden), BF16)],
        [(up_at, "s"), (e1, "v"), (e1_sib, "v"), (f_own, "v"), (f_sib, "v"), (bias_1, "v")]
        + [(x, "a") for x in ups],
        [pltpu.VMEM((width, own_hidden), BF16), pltpu.SemaphoreType.DMA((count_up,))],
        flops=4 * rows * width * own_hidden * 4, name="up",
    )
    y_mine, y_send = call(
        functools.partial(down_kernel, count_down, rank),
        [shaped((rows, width + 128), F32)] * 2,
        [(down_at, "s"), (a, "v"), (f_own, "v"), (f_sib, "v")] + [(x, "a") for x in downs],
        [pltpu.VMEM((own_hidden, width), BF16), pltpu.SemaphoreType.DMA((count_down,))],
        flops=4 * rows * width * own_hidden * 4, name="down",
    )
    x2, u_dn, score = call(
        functools.partial(score_kernel, rank),
        [shaped((rows, width), F32), shaped((rows, 5 * rank), BF16), shaped((rows, 128), F32)],
        [(v, "v") for v in (x1, y_mine, swap(y_send), wide_d, bias_2, gain[2], shift[2], wide_head)],
        name="score",
    )
    scores = [score]
    for d in range(1, m):
        scores.append(lax.ppermute(score, AXES, pairs_of(n, m, lambda r, s, d=d: (r, s ^ d))))

    e2, g_end, g_dn, small = call(
        functools.partial(loss_kernel, rank, m),
        [shaped((rows, width + 128), BF16), shaped((rows, width), F32), shaped((5 * rank, width), F32),
         shaped((8, width), F32)],
        [(v, "v") for v in (*scores, x2, u_dn, pick_t, live_row, count_row, wide_d, gain[2], shift[2], wide_head)],
        name="loss",
    )
    y_mine, y_send, gf_mine, gf_send = call(
        functools.partial(ffn_back_kernel, count_up, count_down, rank),
        [shaped((rows, width + 128), F32)] * 2 + [shaped((2 * rank, own_hidden), F32)] * 2,
        [(up_at, "s"), (down_at, "s")]
        + [(v, "v") for v in (e2, swap(e2), e1, e1_sib, f, a, f_own, f_sib)]
        + [(x, "a") for x in ups] + [(x, "a") for x in downs],
        [pltpu.VMEM((width, own_hidden), BF16), pltpu.VMEM((own_hidden, width), BF16),
         pltpu.SemaphoreType.DMA((count_up,)), pltpu.SemaphoreType.DMA((count_down,))],
        flops=8 * rows * width * own_hidden * 4, name="ffn_back",
    )

    gf_other = swap(gf_send)
    pieces_f = [x.reshape(2 * rank, n, 1, half) for x in (gf_mine, gf_other)]
    grad_f = jnp.where(
        core == 0,
        jnp.concatenate(pieces_f, 2),
        jnp.concatenate(pieces_f[::-1], 2),
    ).reshape(2 * rank, hidden)
    mat_f, left_f = call(
        factor_kernel,
        [shaped((2 * rank, hidden), F32), shaped((rank, hidden), F32)],
        [(grad_f, "v"), (err_f[0, 0].T, "v"), (qstart_f[0].T, "v")],
        name="factor_f",
    )
    mat_d, left_d = call(
        functools.partial(rows_back_kernel, micro, count_first, rank),
        [shaped((2, 5 * rank, width), F32), shaped((2 * rank + 8, width), F32)],
        [(first_at, "s")]
        + [(v, "v") for v in (y_mine, swap(y_send), x1, g_end, e1, u, o, q, p, kv, ukv, *hl, *h1,
                              wide_d, gain[1], g_dn, err_d[0, 0].transpose(1, 2, 0),
                              qstart_d[0].transpose(0, 2, 1), small)]
        + [(x, "a") for x in firsts],
        [pltpu.VMEM((width, width), BF16), pltpu.SemaphoreType.DMA((count_first,))],
        flops=20 * rows * tokens * width * 8, name="rows_back",
    )

    def rep_sum(x):
        bit = 1
        while bit < n:
            x = x + lax.ppermute(x, AXES, pairs_of(n, m, lambda r, s, bit=bit: (r ^ bit, s)))
            bit *= 2
        return x

    def shard_sum(x):
        bit = 1
        while bit < m:
            x = x + lax.ppermute(x, AXES, pairs_of(n, m, lambda r, s, bit=bit: (r, s ^ bit)))
            bit *= 2
        return x

    left_f = rep_sum(left_f)
    left_d = rep_sum(left_d)
    comp_head = left_d[2 * rank : 2 * rank + 1]
    loss_rep = left_d[2 * rank + 1, 0]
    ph_d, ph_f, new_q = call(
        functools.partial(ortho_kernel, rank),
        [shaped((2, rank, width), F32), shaped((rank, hidden), F32), shaped((3 * rank, 128), F32)],
        [(v, "v") for v in (left_d, left_f, mat_d, mat_f)],
        name="ortho",
    )
    new_q = rep_sum(new_q)
    new_err_d, new_err_f, squares = call(
        functools.partial(comp_kernel, rank, n),
        [shaped((2, 5 * rank, width), F32), shaped((2 * rank, hidden), F32), shaped((1, 128), F32)],
        [(v, "v") for v in (new_q, ph_d, ph_f, mat_d, mat_f, comp_head)],
        name="comp",
    )
    total = jnp.concatenate([squares, jnp.broadcast_to(loss_rep / m, (1, 128))], 0)
    total = shard_sum(total)
    own_ph_d = lax.dynamic_slice_in_dim(ph_d, rep * rd, rd, 2)
    own_ph_f = lax.dynamic_slice_in_dim(ph_f, rep * rf, rf, 1)
    own_head = lax.dynamic_slice_in_dim(comp_head, rep * rd, rd, 1)
    nd, nf, nh, nmd, nmf, nmh, norm = call(
        functools.partial(update_kernel, rank),
        [shaped((2, 5 * rank, rd), F32), shaped((2 * rank, rf), F32), shaped((1, rd), F32)] * 2
        + [shaped((1, 128), F32)],
        [(v, "v") for v in (total, new_q, own_ph_d, own_ph_f, own_head, d_t, f_t, head,
                            mom_d[0].transpose(1, 2, 0), mom_f[0].T, mom_head)],
        name="update",
    )
    q_d = new_q[: 2 * rank, : 5 * rank].reshape(2, rank, 5 * rank).transpose(0, 2, 1)[None]
    q_f = new_q[2 * rank :, : 2 * rank].T[None]
    return (
        total[1, 0],
        count,
        norm[0, 0],
        nd.transpose(2, 0, 1)[None],
        nf.T[None],
        nh,
        nmd.transpose(2, 0, 1)[None],
        nmf.T[None],
        nmh,
        new_err_d.transpose(2, 0, 1)[None, None],
        new_err_f.T[None, None],
        q_d,
        q_f,
    )


def solution(mesh):
    n, m = mesh.shape["rep"], mesh.shape["shard"]
    return jax.shard_map(
        functools.partial(on_device, n, m),
        mesh=mesh,
        in_specs=(
            P("rep", None),
            P("rep", None),
            P("rep", None),
            P("rep", None, None),
            P("shard", None),
            P(),
            P("rep", None),
            P("rep", None),
            P("rep", None),
            P("rep", None),
            P(),
            P(),
            P("shard", "rep", None, None),
            P("shard", "rep", None),
            P("shard", "rep"),
            P("shard", "rep", None, None),
            P("shard", "rep", None),
            P("shard", "rep"),
            P("shard", "rep", None, None, None),
            P("shard", "rep", None, None),
            P("shard", None, None, None),
            P("shard", None, None),
        ),
        out_specs=(
            P(),
            P(),
            P(),
            P("shard", "rep", None, None),
            P("shard", "rep", None),
            P("shard", "rep"),
            P("shard", "rep", None, None),
            P("shard", "rep", None),
            P("shard", "rep"),
            P("shard", "rep", None, None, None),
            P("shard", "rep", None, None),
            P("shard", None, None, None),
            P("shard", None, None),
        ),
        check_vma=False,
    )
```

```python
import functools
import math

import jax
import jax.numpy as jnp
import numpy as np
from jax import lax
from jax.experimental import pallas as pl
from jax.experimental.pallas import tpu as pltpu
from jax.sharding import PartitionSpec as P

HEAD_DIM = 64
F32 = jnp.float32
BF16 = jnp.bfloat16
EXACT = lax.Precision.HIGHEST
CLIP = 0.01
MOMENTUM = 0.9
RATE = 1000.0
SCALE = 2.0
AXES = ("rep", "shard")


def nn(a, b, precision=None):
    return lax.dot_general(
        a, b, (((1,), (0,)), ((), ())), precision=precision, preferred_element_type=F32
    )


def nt(a, b, precision=None):
    return lax.dot_general(
        a, b, (((1,), (1,)), ((), ())), precision=precision, preferred_element_type=F32
    )


def tn(a, b, precision=None):
    return lax.dot_general(
        a, b, (((0,), (0,)), ((), ())), precision=precision, preferred_element_type=F32
    )


def iota(shape, dim):
    return lax.broadcasted_iota(jnp.int32, shape, dim)


def lanes(x, low, high):
    at = iota(x.shape, x.ndim - 1)
    return jnp.where((at >= low) & (at < high), x, jnp.zeros_like(x))


def norm_parts(x):
    centered = x - jnp.mean(x, -1, keepdims=True)
    rstd = lax.rsqrt(jnp.mean(centered * centered, -1, keepdims=True) + 1e-05)
    return centered * rstd, rstd


def norm_back(grad, gain, unit, rstd):
    g = grad * gain
    return rstd * (
        g - jnp.mean(g, -1, keepdims=True) - unit * jnp.mean(g * unit, -1, keepdims=True)
    )


def load(pieces, spots, target, sems):
    copies = []
    for index, (piece, (row, column)) in enumerate(zip(pieces, spots, strict=True)):
        rows, columns = piece.shape
        if not isinstance(row, int):
            row = pl.multiple_of(row, rows)
        if not isinstance(column, int):
            column = pl.multiple_of(column, columns)
        place = target.at[pl.ds(row, rows), pl.ds(column, columns)]
        copies.append(pltpu.make_async_copy(piece, place, sems.at[index]))
    for copy in copies:
        copy.start()

    def wait():
        for copy in copies:
            copy.wait()

    return wait


def expand_heads(x, heads):
    rows, width = x.shape
    head_of = iota((rows, width), 1) // HEAD_DIM
    return jnp.concatenate(
        [jnp.where(head_of == h, x, jnp.zeros_like(x)) for h in range(heads)], 0
    )


def collapse_heads(x, heads):
    rows, width = x.shape[0] // heads, x.shape[1]
    head_of = iota((rows, width), 1) // HEAD_DIM
    total = jnp.zeros((rows, width), F32)
    for h in range(heads):
        total = total + jnp.where(head_of == h, x[h * rows : (h + 1) * rows], 0.0)
    return total


def column(row):
    return jnp.transpose(jnp.broadcast_to(row, (8, row.shape[1])))[:, :1]


def split_kernel(ready, d_t, f_t, head, live, qkv, out, up, down, left, right, up_part, down_part, sems):
    shard = lax.axis_index("shard")
    core = shard % 2
    rows, width = out.shape
    below = left.shape[0] - rows
    half = down_part.shape[0]
    blocks = up_part.shape[1] // half
    part = width // 2
    copies = []

    def move(piece, to):
        copies.append(pltpu.make_async_copy(piece, to, sems.at[len(copies)]))
        copies[-1].start()

    for j in range(4):
        at = pl.multiple_of(core * part, part)
        piece = out.at[:, pl.ds(at, part)] if j == 3 else qkv.at[:, pl.ds(at + j * width, part)]
        move(piece, (left, right)[j // 2].at[pl.ds(0, rows), pl.ds(j % 2 * part, part)])
    move(down.at[pl.ds(pl.multiple_of(core * half, half), half), :], down_part)
    for b in range(blocks):
        at = pl.multiple_of((2 * b + core) * half, half)
        move(up.at[:, pl.ds(at, half)], up_part.at[:, pl.ds(b * half, half)])
    ready()
    left[rows:, :] = jnp.zeros((below, width), BF16)
    right[rows:, :] = jnp.zeros((below, width), BF16)
    flat = jnp.concatenate([d_t[0], d_t[1]], 0).astype(BF16)
    count = flat.shape[0] // below
    for j in range(count):
        left[rows:, j * rows : (j + 1) * rows] = flat[j * below : (j + 1) * below]
    alive = jnp.sum((live[...] >= 0).astype(F32), keepdims=True)
    two = jnp.where(iota((below, rows), 0) == 0, head[...], alive)
    left[rows:, count * rows : (count + 1) * rows] = two.astype(BF16)
    right[rows:, : f_t.shape[1]] = f_t[...].astype(BF16)
    for copy in copies:
        copy.wait()


def assemble_kernel(ready, source, *refs):
    pieces, (mat, sems) = refs[:-2], refs[-2:]
    rep, core = lax.axis_index("rep"), lax.axis_index("shard") % 2
    n = len(pieces) // 2
    rows, width = mat.shape[0] // n, mat.shape[1] // 2
    tops = [piece.at[pl.ds(0, rows), :] for piece in pieces]
    spots = [(source[rep, core, k % n] * rows, k // n * width) for k in range(2 * n)]
    load(tops, spots, mat, sems)()


def unpack_kernel(rank, rows, ready, source, *refs):
    pieces = refs[:-8]
    wide_d, own, other, head, count, flat, both, sems = refs[-8:]
    rep, core = lax.axis_index("rep"), lax.axis_index("shard") % 2
    n = len(pieces) // 2
    below, hidden = both.shape
    blocks = 10 * rank // below
    copies = []
    for k in range(n):
        r = source[rep, core, k]
        lanes_d = pl.ds(pl.multiple_of(r * rows, rows), rows)
        lanes_f = pl.ds(pl.multiple_of(r * (hidden // n), hidden // n), hidden // n)
        low = pl.ds(rows, below)
        for j in range(blocks + 1):
            place = flat.at[pl.ds(j * below, below), lanes_d]
            copies.append((pieces[k].at[low, pl.ds(j * rows, rows)], place))
        copies.append((pieces[n + k].at[low, pl.ds(0, hidden // n)], both.at[:, lanes_f]))
    copies = [pltpu.make_async_copy(a, b, sems.at[i]) for i, (a, b) in enumerate(copies)]
    for copy in copies:
        copy.start()
    for copy in copies:
        copy.wait()
    ready()
    wide_d[0] = flat[0 : 5 * rank, :]
    wide_d[1] = flat[5 * rank : 10 * rank, :]
    head[...] = flat[10 * rank : 10 * rank + 1, :].astype(F32)
    live = flat[10 * rank + 1 : 10 * rank + 2, :].astype(F32)
    count[...] = jnp.broadcast_to(jnp.sum(live, keepdims=True) / rows, count.shape)
    half = hidden // n // 2
    value = both[...]
    halves = [
        jnp.concatenate([value[:, (2 * r + c) * half : (2 * r + c + 1) * half] for r in range(n)], 1)
        for c in range(2)
    ]
    mine = (core == 0).astype(F32)
    zero, one = halves[0].astype(F32), halves[1].astype(F32)
    own[...] = (zero * mine + one * (1.0 - mine)).astype(BF16)
    other[...] = (zero * (1.0 - mine) + one * mine).astype(BF16)


def factors(ref, rank):
    value = ref[...]
    zero = jnp.zeros((4 * rank, value.shape[1]), value.dtype)
    return jnp.concatenate([zero, value[:rank]], 0), jnp.concatenate([zero, value[rank:]], 0)


def front_kernel(offset, ready, parts, pos_v, seg_v, table, gains, bias, h1, xl, hl, prow, tok):
    tokens, width = h1.shape
    slots = xl.shape[0]
    seq = (lax.axis_index("shard") + offset) % 2
    step = min(128, tokens)
    ready()
    position = pos_v[pl.ds(seq, 1), :]
    total = parts[0][...]
    for part in parts[1:]:
        total = total + part[...]
    tok[...] = total
    for i in range(tokens // step):
        rows = pl.ds(i * step, step)
        place = position[:, i * step : (i + 1) * step]
        onehot = (iota((tokens, step), 0) == place).astype(BF16)
        pos = tn(onehot, table[...])
        prow[rows, :] = pos.astype(BF16)
        unit, _ = norm_parts(tok[rows, :].astype(F32) + pos)
        h1[rows, :] = (unit * gains[0:1, :] + bias[0:1, :]).astype(BF16)
    segment = seg_v[pl.ds(seq, 1), :]
    after = pltpu.roll(jnp.broadcast_to(segment, (8, tokens)), tokens - 1, 1)[0:1]
    final = (segment != after) | (iota((1, tokens), 1) == tokens - 1)
    pick = ((segment == iota((slots, tokens), 0)) & final).astype(BF16)
    xl[...] = nn(pick, tok[...]) + nn(pick, prow[...])
    hl[...] = nn(pick, h1[...]).astype(BF16)


def kv_half(rank, h1, mat, at, u, ad, bias, kv):
    part = mat.shape[1] // 4
    width = 2 * part
    cols = pl.ds(at, part)
    for j in range(2):
        to = pl.ds(pl.multiple_of(at + j * width, part), part)
        for b in range(len(h1)):
            total = nn(h1[b][...], mat[:, (1 + j) * part : (2 + j) * part]) + bias[4 + j : 5 + j, cols]
            total = total + SCALE * nn(lanes(u[b], rank * (1 + j), rank * (2 + j)), ad[1, :, cols])
            kv[b, :, to] = total.astype(BF16)


def rows_kernel(micro, rank, ready, flush, *refs):
    seg_v, refs = refs[0], refs[1:]
    h1, hl, xl = refs[:micro], refs[micro : 2 * micro], refs[2 * micro : 3 * micro]
    ad, gains, bias, mat_own, mat_sib, kv, ukv_t, o, x1, q, p_t, u, w_out, e1, ukv = refs[3 * micro :]
    core = lax.axis_index("shard") % 2
    slots, width = hl[0].shape
    heads = width // HEAD_DIM
    tokens = h1[0].shape[0]
    part = width // 2
    mats = [(mat_own, pl.multiple_of(core * part, part)), (mat_sib, pl.multiple_of((1 - core) * part, part))]
    ready(ad, *h1)
    down, up = ad[0], ad[1]
    for b in range(micro):
        ukv[b] = lanes(nt(h1[b][...], down).astype(BF16), rank, 3 * rank)
        ukv_t[b] = nt(down, h1[b][...]).astype(BF16)
    ready(mat_own, bias)
    kv_half(rank, h1, *mats[0], ukv, ad, bias, kv)
    ready()
    kv_half(rank, h1, *mats[1], ukv, ad, bias, kv)
    flush(0)
    flush(1)
    for mat, at in mats:
        w_out[:, pl.ds(at, part)] = mat[:, 3 * part :]
    flush(7)
    h_last = jnp.concatenate([h[...] for h in hl], 0)
    x_last = jnp.concatenate([x[...] for x in xl], 0)
    u_q = lanes(nt(h_last, down).astype(BF16), 0, rank)
    for mat, at in mats:
        cols = pl.ds(at, part)
        total = nn(h_last, mat[:, :part]) + bias[3:4, cols] + SCALE * nn(u_q, ad[1, :, cols])
        q[:, cols] = total.astype(BF16)
    q_all = q[...]
    parts = []
    for b in range(micro):
        wide_q = expand_heads(q_all[b * slots : (b + 1) * slots], heads)
        scores = HEAD_DIM ** (-0.5) * nt(kv[b, :, :width], wide_q)
        segment = column(seg_v[pl.ds((core + b) % 2, 1), :])
        inside = segment == iota((tokens, heads * slots), 1) % slots
        scores = jnp.where(inside, scores, -1000000000.0)
        e = jnp.exp(scores - jnp.max(scores, 0, keepdims=True))
        probs = e / jnp.sum(e, 0, keepdims=True)
        p_t[b] = probs
        parts.append(collapse_heads(tn(probs.astype(BF16), kv[b, :, width:]), heads))
    flush(5)
    o_all = jnp.concatenate(parts, 0).astype(BF16)
    o[...] = o_all
    u_o = lanes(nt(o_all, down).astype(BF16), 3 * rank, 4 * rank)
    mid = x_last + nn(o_all, w_out[...]) + bias[6:7, :] + SCALE * nn(u_o, up)
    x1[...] = mid
    unit, _ = norm_parts(mid)
    h2 = (unit * gains[1:2, :] + bias[1:2, :]).astype(BF16)
    u_up = lanes(nt(h2, down).astype(BF16), 4 * rank, 5 * rank)
    e1[:, :width] = h2
    e1[:, width:] = jnp.zeros_like(e1[:, width:])
    e1[:, width : width + 5 * rank] = u_up
    u[...] = u_q + u_o + u_up


def up_kernel(rank, ready, source, own, sib, f_own, f_sib, bias, *refs):
    weights = refs[:-4]
    f, a, wide, sems = refs[-4:]
    width = wide.shape[0]
    rep, core = lax.axis_index("rep"), lax.axis_index("shard") % 2
    height = weights[0].shape[0]
    spots = [(source[rep, core, k] * height, 0) for k in range(len(weights))]
    tops = weights
    loaded = load(tops, spots, wide, sems)
    ready()
    h2 = jnp.concatenate([own[:, :width], sib[:, :width]], 0)
    lane = 5 * rank
    extra = jnp.concatenate(
        [
            nn(own[:, width : width + lane], factors(f_own, rank)[1]),
            nn(sib[:, width : width + lane], factors(f_sib, rank)[1]),
        ],
        0,
    )
    loaded()
    total = nn(h2, wide[...]) + bias[...] + SCALE * extra
    f[...] = total
    a[...] = jax.nn.gelu(total, approximate=True).astype(BF16)


def down_kernel(rank, ready, source, a, f_own, f_sib, *refs):
    weights = refs[:-4]
    mine, send, wide, sems = refs[-4:]
    width = wide.shape[1]
    rep, core = lax.axis_index("rep"), lax.axis_index("shard") % 2
    height = weights[0].shape[0]
    spots = [(source[rep, core, k] * height, 0) for k in range(len(weights))]
    ends = weights
    loaded = load(ends, spots, wide, sems)
    ready()
    rows = a.shape[0] // 2
    lane = 5 * rank
    for out, low, factor in ((mine, 0, f_own), (send, rows, f_sib)):
        out[:, width:] = jnp.zeros_like(out[:, width:])
        out[:, width : width + lane] = nt(a[low : low + rows, :], factors(factor, rank)[0])
    loaded()
    y = nn(a[...], wide[...])
    mine[:, :width] = y[:rows]
    send[:, :width] = y[rows:]


def score_kernel(rank, ready, x1, mine, recv, ad, gains, bias, head, x2, u_dn, score):
    ready()
    width = x1.shape[1]
    lane = 5 * rank
    u = (mine[:, width : width + lane] + recv[:, width : width + lane]).astype(BF16)
    u_dn[...] = u
    end = x1[...] + mine[:, :width] + recv[:, :width] + bias[11:12, :] + SCALE * nn(u, ad[1])
    x2[...] = end
    unit, _ = norm_parts(end)
    token = jnp.sum((unit * gains[2:3, :] + bias[2:3, :]) * head[...], -1, keepdims=True)
    score[...] = jnp.broadcast_to(token, score.shape)


def loss_kernel(rank, members, ready, *refs):
    scores = refs[:members]
    x2, u_dn, pairs, count, ad, gains, bias, head = refs[members : members + 8]
    e2, g_end, g_dn, small = refs[members + 8 :]
    ready()
    rows, width = x2.shape
    half = rows // 2

    def value(m):
        if m % 2 == 0:
            return scores[m][...]
        return jnp.concatenate([scores[m][half:, :], scores[m][:half, :]], 0)

    level = [value(m) for m in range(members)]
    while len(level) > 1:
        level = [level[i] + level[i + 1] for i in range(0, len(level), 2)]
    mean_reward = level[0][:, :1] / members
    at = iota((rows, pairs.shape[1]), 0)
    pick = (at == pairs[0:1, :]).astype(F32) - (at == pairs[1:2, :]).astype(F32)
    live = (pairs[0:1, :] >= 0).astype(F32)
    diff = jnp.sum(pick * mean_reward, 0, keepdims=True)
    terms = live * jax.nn.softplus(-diff)
    grad_diff = -live * jax.nn.sigmoid(-diff) / count[:, :1]
    grad_score = jnp.sum(pick * grad_diff, -1, keepdims=True) / members
    unit, rstd = norm_parts(x2[...])
    final = unit * gains[2:3, :] + bias[2:3, :]
    small[...] = jnp.zeros_like(small)
    small[0:1, :] = jnp.sum(final * grad_score, 0, keepdims=True)
    small[1:2, :] = jnp.broadcast_to(jnp.sum(terms, -1, keepdims=True), (1, width))
    end = norm_back(grad_score * head[...], gains[2:3, :], unit, rstd)
    g_end[...] = end
    g_ff = end.astype(BF16)
    left = lanes((SCALE * nt(g_ff, ad[1])).astype(BF16), 4 * rank, 5 * rank)
    g_dn[...] = SCALE * tn(u_dn[...], g_ff)
    e2[:, :width] = g_ff
    e2[:, width:] = jnp.zeros_like(e2[:, width:])
    e2[:, width : width + 5 * rank] = left


def ffn_back_kernel(rank, ready, own, sib, e1_own, e1_sib, f, a, f_own, f_sib, wide_u, wide_d,
                    mine, send, gf_mine, gf_send):
    width = wide_u.shape[0]
    lane = 5 * rank
    ready()
    rows = own.shape[0]
    x = f[...]
    c0, c1 = math.sqrt(2.0 / math.pi), 0.044715
    t = jnp.tanh(c0 * (x + c1 * x * x * x))
    slope = 0.5 * (1.0 + t) + 0.5 * x * (1.0 - t * t) * (c0 * (1.0 + 3.0 * c1 * x * x))
    left_own, left_sib = own[:, width : width + lane], sib[:, width : width + lane]
    u_own, u_sib = e1_own[:, width : width + lane], e1_sib[:, width : width + lane]
    g_ff = jnp.concatenate([own[:, :width], sib[:, :width]], 0)
    pair_own, pair_sib = factors(f_own, rank), factors(f_sib, rank)
    extra = jnp.concatenate([nn(left_own, pair_own[0]), nn(left_sib, pair_sib[0])], 0)
    g_a = (nt(g_ff, wide_d[...]) + extra).astype(BF16)
    g_f = (g_a.astype(F32) * slope).astype(BF16)
    g_h = nt(g_f, wide_u[...])
    parts = (
        (mine, gf_mine, 0, pair_own, left_own, u_own),
        (send, gf_send, rows, pair_sib, left_sib, u_sib),
    )
    for out, _, low, factor, _, _ in parts:
        out[:, :width] = g_h[low : low + rows]
        out[:, width:] = jnp.zeros_like(out[:, width:])
        out[:, width : width + lane] = SCALE * nt(g_f[low : low + rows], factor[1])
    for _, gout, low, _, left, u in parts:
        gout[0:rank, :] = tn(left, a[low : low + rows, :])[4 * rank :]
        gout[rank:, :] = SCALE * tn(u, g_f[low : low + rows])[4 * rank :]


def factor_kernel(rank, half, ready, mine, other, err, start, mat, left):
    ready()
    core = lax.axis_index("shard") % 2
    first = (core == 0).astype(F32)
    even = mine[...] * first + other[...] * (1.0 - first)
    odd = mine[...] * (1.0 - first) + other[...] * first
    parts = []
    for r in range(mine.shape[1] // half):
        cut = slice(r * half, (r + 1) * half)
        parts += [even[:, cut], odd[:, cut]]
    mat[...] = jnp.concatenate(parts, 1) + err[...]
    left[...] = nn(start[...], mat[...], EXACT)


def rows_back_kernel(micro, rank, ready, *refs):
    mine, recv, g_end, g_dn, small, x1, e1, u, o, q, p_t, kv, ukv_t = refs[:13]
    hl = refs[13 : 13 + micro]
    h1 = refs[13 + micro : 13 + 2 * micro]
    ad, gains, err, start, w_out, mat, left = refs[13 + 2 * micro :]
    ready(ad, gains)
    rows, width = x1.shape
    slots = rows // micro
    heads = width // HEAD_DIM
    lane = 5 * rank
    down, up = ad[0], ad[1]
    h2 = e1[:, :width]
    u_rows = u[...]
    g_u = (mine[:, width : width + lane] + recv[:, width : width + lane]).astype(BF16)
    g_h2 = (mine[:, :width] + recv[:, :width] + nn(g_u, down)).astype(BF16)
    grad_in = tn(g_u, h2)
    unit, rstd = norm_parts(x1[...])
    g_mid = g_end[...] + norm_back(g_h2.astype(F32), gains[1:2, :], unit, rstd)
    g_att = g_mid.astype(BF16)
    grad_out = g_dn[...] + SCALE * tn(lanes(u_rows, 3 * rank, 4 * rank), g_att)
    g_ol = lanes((SCALE * nt(g_att, up)).astype(BF16), 3 * rank, 4 * rank)
    grad_in = grad_in + tn(g_ol, o[...])
    g_o = (nt(g_att, w_out[...]) + nn(g_ol, down)).astype(BF16)
    ready()
    scale = HEAD_DIM ** (-0.5)

    def row_part(x, low, high):
        at = iota(x.shape, 0)
        return jnp.where((at >= low) & (at < high), x, jnp.zeros_like(x))

    for b in range(micro):
        pick = slice(b * slots, (b + 1) * slots)
        wide_g = expand_heads(g_o[pick], heads)
        wide_q = expand_heads(q[pick, :], heads)
        probs = p_t[b]
        g_p = nt(kv[b, :, width:], wide_g)
        g_s = (probs * (g_p - jnp.sum(probs * g_p, 0, keepdims=True))).astype(BF16)
        g_q = (scale * collapse_heads(tn(g_s, kv[b, :, :width]), heads)).astype(BF16)
        g_k = (scale * nn(g_s, wide_q)).astype(BF16)
        g_v = nn(probs.astype(BF16), wide_g).astype(BF16)
        u_q = lanes(u_rows[pick], 0, rank)
        u_k = row_part(ukv_t[b], rank, 2 * rank)
        u_v = row_part(ukv_t[b], 2 * rank, 3 * rank)
        grad_out = grad_out + SCALE * (tn(u_q, g_q) + nn(u_k, g_k) + nn(u_v, g_v))
        g_uq = lanes((SCALE * nt(g_q, up)).astype(BF16), 0, rank)
        g_ukv = row_part((SCALE * nt(up, g_k)).astype(BF16), rank, 2 * rank) + row_part(
            (SCALE * nt(up, g_v)).astype(BF16), 2 * rank, 3 * rank
        )
        grad_in = grad_in + tn(g_uq, hl[b][...]) + nn(g_ukv, h1[b][...])
    mat[0] = grad_in + err[0]
    mat[1] = grad_out + err[1]
    first = start.shape[1]
    left[0:first, :] = nn(start[0], mat[0], EXACT)
    left[first : 2 * first, :] = nn(start[1], mat[1], EXACT)
    left[2 * first :, :] = small[...]


def orthonormal_rows(refs):
    count = refs[0].shape[0]
    for k in range(count):
        for ref in refs:
            row = ref[k : k + 1, :]
            row = row * lax.rsqrt(jnp.sum(row * row, -1, keepdims=True) + 1e-06)
            if k + 1 < count:
                block = ref[...]
                at = iota(block.shape, 0)
                dots = jnp.sum(block * row, -1, keepdims=True)
                block = jnp.where(at > k, block - dots * row, block)
                ref[...] = jnp.where(at == k, row, block)
            else:
                ref[k : k + 1, :] = row


def ortho_kernel(rank, ready, d_a, d_b, f_a, f_b, mat_d, mat_f, ph_d, ph_f, head, note):
    count = rank
    for j in range(2):
        part = slice(j * count, (j + 1) * count)
        ph_d[j] = d_a[part, :] + d_b[part, :]
    ph_f[...] = f_a[...] + f_b[...]
    rest = d_a[2 * count :, :] + d_b[2 * count :, :]
    refs = (ph_d.at[0], ph_d.at[1], ph_f)
    orthonormal_rows(refs)
    ready()
    grad = rest[0:1, :]
    head[...] = grad
    parts = []
    for ref, mat in zip(refs, (mat_d.at[0], mat_d.at[1], mat_f), strict=True):
        parts.append(nt(ref[...], mat[...], EXACT))
    for ref in refs:
        parts.append(nt(ref[...], ref[...], EXACT))
    parts.append(jnp.broadcast_to(jnp.sum(grad * grad, keepdims=True), (count, 1)))
    parts.append(jnp.broadcast_to(rest[1:2, :1], (count, 1)))
    used = sum(x.shape[1] for x in parts)
    parts.append(jnp.zeros((count, 128 - used), F32))
    own = jnp.concatenate(parts, 1)

    @pl.loop(0, note.shape[0])
    def _(i):
        note[i] = own


def final_kernel(rank, n, m, ready, notes, ph_d, ph_f, ph_do, ph_fo, ghead, mat_d, mat_f,
                 wd, wf, wh, md, mf, mh,
                 nd, nf, nh, nmd, nmf, nmh, err_d, err_f, q_d, q_f, mean_loss, norm):
    ready()
    shard = lax.axis_index("shard")
    count = rank
    sizes = (5 * rank, 5 * rank, 2 * rank)
    total = jnp.zeros((1, 1), F32)
    loss = jnp.zeros((1, 1), F32)
    own = jnp.zeros((count, 128), F32)
    for s in range(m):
        block = notes[s]
        for r in range(1, n):
            block = block + notes[r * m + s]
        own = jnp.where(shard == s, block, own)
        note = notes[s]
        at, gram = 0, sum(sizes)
        for size in sizes:
            right = block[:, at : at + size]
            inner = note[:, gram : gram + count]
            total = total + jnp.sum(right * nn(inner, right, EXACT), keepdims=True)
            at += size
            gram += count
        total = total + note[0:1, gram : gram + 1]
        loss = loss + note[0:1, gram + 1 : gram + 2]
    grad_norm = jnp.sqrt(total)
    clip = jnp.minimum(1.0, CLIP / (grad_norm + 1e-06))
    mean_loss[...] = loss / m
    norm[...] = grad_norm
    at = 0
    for j in range(2):
        right = own[:, at : at + sizes[j]]
        q_d[j] = right
        at += sizes[j]
        err_d[j] = mat_d[j] - tn(right, ph_d[j], EXACT) * (1.0 / n)
        fresh = MOMENTUM * md[j] + clip * tn(right, ph_do[j], EXACT)
        nmd[j] = fresh
        nd[j] = wd[j] - RATE * fresh
    right = own[:, at : at + sizes[2]]
    q_f[...] = right
    err_f[...] = mat_f[...] - tn(right, ph_f[...], EXACT) * (1.0 / n)
    fresh = MOMENTUM * mf[...] + clip * tn(right, ph_fo[...], EXACT)
    nmf[...] = fresh
    nf[...] = wf[...] - RATE * fresh
    fresh = MOMENTUM * mh[...] + clip * ghead[...]
    nmh[...] = fresh
    nh[...] = wh[...] - RATE * fresh


class Raw:
    def __init__(self, array):
        self.array = array


class Scalars(Raw):
    pass


class Far(Raw):
    pass


class Fresh(Raw):
    pass


class Part:
    def __init__(self, array, rows):
        self.array, self.rows = array, rows


class Kept:
    def __init__(self, shape, dtype):
        self.shape, self.dtype = tuple(shape), dtype


class Placed(Kept):
    pass


def call(body, outs, args, scratch=(), vmem=60, name=None, groups=None, aliases=None, flushes=False):
    arrays, specs, staged = [], [], []
    for arg in args:
        arrays.append(arg.array if isinstance(arg, Raw | Part) else arg)
        space = pl.ANY
        if isinstance(arg, Scalars):
            space = pltpu.SMEM
        elif isinstance(arg, Fresh):
            space = pltpu.VMEM
        elif isinstance(arg, Far):
            space = pltpu.HBM
        specs.append(pl.BlockSpec(memory_space=space))
        if isinstance(arg, Part):
            staged.append(pltpu.VMEM((arg.rows, *arg.array.shape[1:]), arg.array.dtype))
        elif not isinstance(arg, Raw):
            staged.append(pltpu.VMEM(arg.shape, arg.dtype))
    results = [pltpu.VMEM(o.shape, o.dtype) for o in outs if not isinstance(o, Kept)]

    def kernel(*refs):
        ins, refs = refs[: len(args)], refs[len(args) :]
        targets, refs = refs[: len(outs)], refs[len(outs) :]
        held, refs = refs[: len(staged)], refs[len(staged) :]
        buffers, refs = refs[: len(results)], refs[len(results) :]
        extra, sems = refs[:-1], refs[-1]
        copies, given, i = {}, [], 0
        for arg, ref in zip(args, ins, strict=True):
            if isinstance(arg, Raw):
                given.append(ref)
                continue
            origin = ref.at[pl.ds(0, arg.rows)] if isinstance(arg, Part) else ref
            copies[id(held[i])] = pltpu.make_async_copy(origin, held[i], sems.at[i])
            given.append(held[i])
            i += 1
        for copy in copies.values():
            copy.start()

        def ready(*some):
            for key in [id(r) for r in some] or list(copies):
                copies.pop(key).wait()

        local, back, i = [], {}, 0
        for j, out in enumerate(outs):
            if isinstance(out, Kept):
                local.append(targets[j])
                continue
            local.append(buffers[i])
            back[j] = pltpu.make_async_copy(buffers[i], targets[j], sems.at[len(staged) + i])
            i += 1
        def flush(j):
            back[j].start()
            begun.append(j)

        begun = []
        if groups:
            given = [given[:groups], *given[groups:]]
        body(ready, *((flush,) if flushes else ()), *given, *local, *extra)
        for j, copy in back.items():
            if j not in begun:
                copy.start()
        for copy in back.values():
            copy.wait()

    def place(out):
        if type(out) is Kept:
            return pltpu.VMEM
        return pl.ANY if isinstance(out, Kept) else pltpu.HBM

    return pl.pallas_call(
        kernel,
        out_shape=tuple(jax.ShapeDtypeStruct(o.shape, o.dtype) for o in outs),
        in_specs=specs,
        out_specs=tuple(pl.BlockSpec(memory_space=place(o)) for o in outs),
        scratch_shapes=[
            *staged, *results, *scratch, pltpu.SemaphoreType.DMA((max(1, len(staged) + len(results)),)),
        ],
        compiler_params=pltpu.CompilerParams(vmem_limit_bytes=vmem << 20),
        cost_estimate=pl.CostEstimate(flops=0, bytes_accessed=0, transcendentals=0),
        input_output_aliases=aliases or {},
        name=name,
    )(*arrays)


def shaped(shape, dtype):
    return jax.ShapeDtypeStruct(tuple(shape), dtype)


def ring_order(count):
    side = math.isqrt(count // 2)
    if side < 2 or 2 * side * side != count:
        return list(range(count))
    depth = 2 * side
    cells = []
    for z in range(depth):
        ys = range(1, side) if z % 2 == 0 else range(side - 1, 0, -1)
        cells += [(z, y) for y in ys]
    cells += [(z, 0) for z in range(depth - 1, -1, -1)]
    return [z * side + y for z, y in cells]


def pairs_of(n, m, move):
    return [(r * m + s, t[0] * m + t[1]) for r in range(n) for s in range(m) for t in [move(r, s)]]


def on_device(n, m, *args):
    (
        token_ids, positions, segment_ids, pair_index, embed_table, pos_table,
        base_qkv, base_out, base_up, base_down, base_gains, base_bias,
        adapt_d, adapt_f, head, mom_d, mom_f, mom_head, err_d, err_f, qstart_d, qstart_f,
    ) = args
    micro, tokens = token_ids.shape
    held, width = embed_table.shape
    pairs = pair_index.shape[1]
    slots = 2 * pairs
    rows = micro * slots
    hidden = base_up.shape[1]
    rank = adapt_f.shape[2] // 2
    heads = width // HEAD_DIM
    rd, rf = base_up.shape[0], base_down.shape[0]
    half = rf // 2
    own_hidden = hidden // 2
    rep, shard = lax.axis_index("rep"), lax.axis_index("shard")
    core = shard % 2

    order = ring_order(n)
    place = {r: i for i, r in enumerate(order)}
    around = pairs_of(
        n, m, lambda r, s: (order[(place[r] + (1 if s % 2 == 0 else -1)) % n], s)
    )
    turns = [
        [[order[(place[r] + (-k if c == 0 else k)) % n] for k in range(n)] for c in range(2)]
        for r in range(n)
    ]
    source = Scalars(jnp.asarray(np.array(turns, np.int32)))

    def send(x, perm):
        return lax.ppermute(x, AXES, perm)

    def across(x, mask):
        return send(x, pairs_of(n, m, lambda r, s: (r, s ^ mask)))

    def ring(x):
        out = []
        for _ in range(n - 1):
            x = send(x, around)
            out.append(x)
        return out

    def pick(x, index, axis):
        return lax.dynamic_index_in_dim(x, index, axis, keepdims=False)

    d_t = adapt_d[0].transpose(1, 2, 0)
    f_t = adapt_f[0].T
    below = 2 * rank
    live = pair_index[..., 0].reshape(1, micro * pairs)
    whole_blocks = rd % 128 == 0 and half % 128 == 0
    if whole_blocks:
        left, right, up_part, down_part = call(
            split_kernel,
            [shaped((rd + below, width), BF16), shaped((rd + below, width), BF16),
             shaped((rd, own_hidden), BF16), shaped((half, width), BF16)],
            [d_t, f_t, head, live, Raw(base_qkv), Raw(base_out), Raw(base_up), Raw(base_down)],
            [pltpu.SemaphoreType.DMA((n + 5,))],
            vmem=56, name="split",
        )
    else:
        two = jnp.concatenate([head, jnp.broadcast_to(jnp.sum((live >= 0).astype(F32)), (below - 1, rd))], 0)
        flat = [x for x in d_t.reshape(10 * rank // below, below, rd)]
        first = jnp.concatenate([base_qkv, base_out], 1).reshape(rd, 4, 2, width // 2)
        first = pick(first, core, 2).reshape(rd, 2, width)
        sides = []
        for side, extra in enumerate((jnp.concatenate([*flat, two], 1), f_t)):
            extra = jnp.pad(extra.astype(BF16), ((0, 0), (0, width - extra.shape[1])))
            sides.append(jnp.concatenate([first[:, side], extra], 0))
        left, right = sides
        up_part = pick(base_up.reshape(rd, n, 2, half), core, 2).reshape(rd, own_hidden)
        down_part = pick(base_down.reshape(2, half, width), core, 0)

    def after(x, *others):
        return pl.pallas_call(
            lambda *refs: None,
            out_shape=jax.ShapeDtypeStruct(x.shape, x.dtype),
            in_specs=[pl.BlockSpec(memory_space=pl.ANY)] * (1 + len(others)),
            out_specs=pl.BlockSpec(memory_space=pl.ANY),
            input_output_aliases={0: 0},
            cost_estimate=pl.CostEstimate(flops=0, bytes_accessed=0, transcendentals=0),
            name="after",
        )(x, *others)

    def lookup(*start):
        ids = jnp.stack([pick(token_ids, (core + b) % micro, 0) for b in range(micro)])
        ids = after(ids, *start)
        near = ids - shard * held
        inside = (near >= 0) & (near < held)
        found = jnp.take(embed_table, jnp.clip(near, 0, held - 1), axis=0)
        found = jnp.where(inside[..., None], found, jnp.zeros_like(found))
        return found[0], found[1]

    def shared(own, given, *others):
        own = own + across(after(given, *others), 1)
        mask = 2
        while mask < m // 2:
            own = own + across(own, mask)
            mask *= 2
        return own, across(own, mask) if m > 2 else own

    bias = base_bias.reshape(-1, width)
    bias_1 = pick(base_bias[7 * width : 7 * width + hidden].reshape(n, 2, half), core, 1)
    bias_1 = bias_1.reshape(1, own_hidden)
    local = (jnp.arange(micro) + core) % micro * slots
    pair_rows = jnp.where(pair_index >= 0, pair_index + local[:, None, None], -1)
    pair_rows = pair_rows.reshape(micro * pairs, 2).T

    pos_rows = pos_table[:tokens]

    lefts, rights, ups, downs = [left], [right], [up_part], [down_part]
    for k in range(1, n):
        gate = []
        if k == 9:
            gate = [ups[1], downs[1]]
        if k == 4:
            gate = [tok_own]
        if k == 7:
            gate = [tok_far]
        if gate:
            lefts[-1], rights[-1] = after(lefts[-1], *gate), after(rights[-1], *gate)
        lefts.append(send(lefts[-1], around))
        rights.append(send(rights[-1], around))
        if k == 1:
            ups[-1], downs[-1] = after(ups[-1], lefts[1]), after(downs[-1], lefts[1])
            ups.append(send(ups[-1], around))
            downs.append(send(downs[-1], around))
            own, given = lookup(lefts[1], rights[1], bias, bias_1, pos_rows, pair_rows)
        if k == 2:
            tok_own, tok_far = shared(own, given, lefts[2], rights[2], ups[1], downs[1])

    def behind(low, high, *gate):
        for k in range(low, min(high, n)):
            if gate:
                ups[-1], downs[-1] = after(ups[-1], *gate), after(downs[-1], *gate)
            gate = ()
            ups.append(send(ups[-1], around))
            downs.append(send(downs[-1], around))

    behind(2, 4, lefts[5])
    parts = [tok_own, tok_far] if m > 2 else [tok_own]
    both = tok_own + tok_far if m > 2 else tok_own
    toks = [parts, [across(both, 1)]]

    lefts[-1] = after(lefts[-1], ups[2], downs[2])
    step_a = [*lefts, *rights]
    if whole_blocks:
        (mat_own,) = call(
            assemble_kernel,
            [shaped((width, 2 * width), BF16)],
            [source, *[Far(x) for x in step_a]],
            [pltpu.SemaphoreType.DMA((2 * n,))],
            vmem=58, name="assemble",
        )
        wide_d, f_own, f_other, wide_head, count_row = call(
            functools.partial(unpack_kernel, rank, rd),
            [shaped((2, 5 * rank, width), BF16), shaped((2 * rank, own_hidden), BF16),
             Kept((2 * rank, own_hidden), BF16), shaped((1, width), F32), shaped((1, 128), F32)],
            [source, *[Far(x) for x in step_a]],
            [pltpu.VMEM((10 * rank + below, width), BF16), pltpu.VMEM((below, hidden), BF16),
             pltpu.SemaphoreType.DMA((n * (10 * rank // below + 2),))],
            vmem=52, name="unpack",
        )
    else:
        turned = jnp.asarray(np.argsort(np.array(turns, np.int32), -1).astype(np.int32))
        place_at = lax.dynamic_slice(turned, (rep, core, 0), (1, 1, n)).reshape(n)
        steps_l, steps_r = [
            jnp.stack([pick(jnp.stack(x), place_at[r], 0) for r in range(n)]) for x in (lefts, rights)
        ]
        mat_own = jnp.concatenate([steps_l[:, :rd], steps_r[:, :rd]], 2).reshape(width, 2 * width)
        count_d = 10 * rank // below
        wide_d = steps_l[:, rd:, : count_d * rd].reshape(n, below, count_d, rd)
        wide_d = wide_d.transpose(2, 1, 0, 3).reshape(2, 5 * rank, width)
        wide_f = steps_r[:, rd:, :rf].reshape(n, 2 * rank, 2, half)
        wide_f = wide_f.transpose(2, 1, 0, 3).reshape(2, 2 * rank, own_hidden)
        f_own, f_other = pick(wide_f, core, 0), pick(wide_f, 1 - core, 0)
        last = steps_l[:, rd:, count_d * rd : (count_d + 1) * rd].astype(F32)
        wide_head = last[:, 0].reshape(1, width)
        count_row = jnp.broadcast_to(jnp.sum(last[:, 1, 0]), (1, 128))
    count = count_row[0, 0]
    behind(4, 5, mat_own)
    f_sib = across(f_other, 1)
    mat_sib = across(mat_own, 1)

    h1, xl, hl = [], [], []
    for b in range(micro):
        a, x, h = call(
            functools.partial(front_kernel, b),
            [Kept((tokens, width), BF16), Kept((slots, width), F32), Kept((slots, width), BF16)],
            [*toks[b], positions, segment_ids, pos_rows, base_gains, bias],
            [pltpu.VMEM((tokens, width), BF16), pltpu.VMEM((tokens, width), BF16)],
            groups=len(toks[b]), vmem=14, name="front",
        )
        h1.append(a)
        xl.append(x)
        hl.append(h)

    behind(5, 7, *hl, wide_d)
    kv, ukv_t, o, x1, q, p_t, u, w_out, e1 = call(
        functools.partial(rows_kernel, micro, rank),
        [shaped((micro, tokens, 2 * width), BF16), shaped((micro, 5 * rank, tokens), BF16),
         shaped((rows, width), BF16), shaped((rows, width), F32), shaped((rows, width), BF16),
         shaped((micro, tokens, heads * slots), F32), shaped((rows, 5 * rank), BF16),
         shaped((width, width), BF16), shaped((rows, width + 128), BF16)],
        [segment_ids, *h1, *hl, *xl, wide_d, base_gains, bias, mat_own, mat_sib],
        [pltpu.VMEM((micro, tokens, 5 * rank), BF16)],
        vmem=60, flushes=True, name="rows",
    )
    behind(7, n, o)
    ups, downs = [[Far(y) for y in x] for x in (ups, downs)]
    e1_sib = across(e1, 1)
    f, a, w_up = call(
        functools.partial(up_kernel, rank),
        [Kept((2 * rows, own_hidden), F32), Kept((2 * rows, own_hidden), BF16),
         Kept((width, own_hidden), BF16)],
        [source, Fresh(e1), Fresh(e1_sib), f_own, f_sib, bias_1, *ups],
        [pltpu.SemaphoreType.DMA((n,))],
        vmem=10, name="up",
    )
    y_mine, y_send, w_down = call(
        functools.partial(down_kernel, rank),
        [Kept((rows, width + 128), F32)] * 2 + [Kept((own_hidden, width), BF16)],
        [source, Fresh(a), f_own, f_sib, *downs],
        [pltpu.SemaphoreType.DMA((n,))],
        vmem=10, name="down",
    )
    x2, u_dn, score = call(
        functools.partial(score_kernel, rank),
        [Kept((rows, width), F32), Kept((rows, 5 * rank), BF16), Kept((rows, 128), F32)],
        [Fresh(x1), Fresh(y_mine), Fresh(across(y_send, 1)), wide_d, base_gains, bias, wide_head],
        vmem=10, name="score",
    )
    scores = [score] + [across(score, k) for k in range(1, m)]
    e2, g_end, g_dn, small = call(
        functools.partial(loss_kernel, rank, m),
        [Kept((rows, width + 128), BF16), Kept((rows, width), F32), Kept((5 * rank, width), F32),
         Kept((8, width), F32)],
        [*[Fresh(x) for x in scores], Fresh(x2), Fresh(u_dn), pair_rows, count_row, wide_d, base_gains, bias, wide_head],
        vmem=10, name="loss",
    )
    y_mine, y_send, gf_mine, gf_send = call(
        functools.partial(ffn_back_kernel, rank),
        [Kept((rows, width + 128), F32)] * 2 + [Kept((2 * rank, own_hidden), F32)] * 2,
        [Fresh(e2), Fresh(across(e2, 1)), Fresh(e1), Fresh(e1_sib), Fresh(f), Fresh(a), f_own, f_sib,
         Fresh(w_up), Fresh(w_down)],
        vmem=14, name="ffn_back",
    )
    mat_f, left_f = call(
        functools.partial(factor_kernel, rank, half),
        [Kept((2 * rank, hidden), F32), Kept((rank, hidden), F32)],
        [Fresh(gf_mine), Fresh(across(gf_send, 1)), err_f[0, 0].T, qstart_f[0].T],
        vmem=10, name="factor_f",
    )
    mat_d, left_d = call(
        functools.partial(rows_back_kernel, micro, rank),
        [Kept((2, 5 * rank, width), F32), Kept((2 * rank + 8, width), F32)],
        [Fresh(y_mine), Fresh(across(y_send, 1)), Fresh(g_end), Fresh(g_dn), Fresh(small),
         *[Fresh(x) for x in (x1, e1, u, o, q, p_t, kv, ukv_t, *hl, *h1)],
         wide_d, base_gains, err_d[0, 0].transpose(1, 2, 0), qstart_d[0].transpose(0, 2, 1), Fresh(w_out)],
        vmem=26, name="rows_back",
    )

    def rep_parts(x):
        bit, part = 1, jnp.zeros_like(x)
        while bit < n:
            part = send(x, pairs_of(n, m, lambda r, s, bit=bit: (r ^ bit, s)))
            bit *= 2
            if bit < n:
                x = x + part
        return Fresh(x), Fresh(part)

    ph_d, ph_f, total_head, note = call(
        functools.partial(ortho_kernel, rank),
        [Kept((2, rank, width), F32), Kept((rank, hidden), F32), Kept((1, width), F32),
         Kept((n * m, rank, 128), F32)],
        [*rep_parts(left_d), *rep_parts(left_f), Fresh(mat_d), Fresh(mat_f)],
        vmem=10, name="ortho",
    )
    notes = lax.all_to_all(note, AXES, 0, 0)
    own_ph_d = lax.dynamic_slice_in_dim(ph_d, rep * rd, rd, 2)
    own_ph_f = lax.dynamic_slice_in_dim(ph_f, rep * rf, rf, 1)
    own_head = lax.dynamic_slice_in_dim(total_head, rep * rd, rd, 1)
    nd, nf, nh, nmd, nmf, nmh, new_err_d, new_err_f, q_d, q_f, loss_sum, norm = call(
        functools.partial(final_kernel, rank, n, m),
        [shaped((2, 5 * rank, rd), F32), shaped((2 * rank, rf), F32), shaped((1, rd), F32)] * 2
        + [shaped((2, 5 * rank, width), F32), shaped((2 * rank, hidden), F32),
           shaped((2, rank, 5 * rank), F32), shaped((rank, 2 * rank), F32), shaped((1, 1), F32), shaped((1, 1), F32)],
        [Fresh(notes), Fresh(ph_d), Fresh(ph_f), Fresh(own_ph_d), Fresh(own_ph_f), Fresh(own_head),
         Fresh(mat_d), Fresh(mat_f), d_t, f_t, head, mom_d[0].transpose(1, 2, 0), mom_f[0].T, mom_head],
        vmem=16, name="final",
    )
    return (
        loss_sum[0, 0],
        count,
        norm[0, 0],
        nd.transpose(2, 0, 1)[None],
        nf.T[None],
        nh,
        nmd.transpose(2, 0, 1)[None],
        nmf.T[None],
        nmh,
        new_err_d.transpose(2, 0, 1)[None, None],
        new_err_f.T[None, None],
        q_d.transpose(0, 2, 1)[None],
        q_f.T[None],
    )


def solution(mesh):
    n, m = mesh.shape["rep"], mesh.shape["shard"]
    return jax.shard_map(
        functools.partial(on_device, n, m),
        mesh=mesh,
        in_specs=(
            P("rep", None),
            P("rep", None),
            P("rep", None),
            P("rep", None, None),
            P("shard", None),
            P(),
            P("rep", None),
            P("rep", None),
            P("rep", None),
            P("rep", None),
            P(),
            P(),
            P("shard", "rep", None, None),
            P("shard", "rep", None),
            P("shard", "rep"),
            P("shard", "rep", None, None),
            P("shard", "rep", None),
            P("shard", "rep"),
            P("shard", "rep", None, None, None),
            P("shard", "rep", None, None),
            P("shard", None, None, None),
            P("shard", None, None),
        ),
        out_specs=(
            P(),
            P(),
            P(),
            P("shard", "rep", None, None),
            P("shard", "rep", None),
            P("shard", "rep"),
            P("shard", "rep", None, None),
            P("shard", "rep", None),
            P("shard", "rep"),
            P("shard", "rep", None, None, None),
            P("shard", "rep", None, None),
            P("shard", None, None, None),
            P("shard", None, None),
        ),
        check_vma=False,
    )
```

```python
import functools
import math

import jax
import jax.numpy as jnp
import numpy as np
from jax import lax
from jax.experimental import pallas as pl
from jax.experimental.pallas import tpu as pltpu
from jax.sharding import PartitionSpec as P

HEAD_DIM = 64
F32 = jnp.float32
BF16 = jnp.bfloat16
EXACT = lax.Precision.HIGHEST
CLIP = 0.01
MOMENTUM = 0.9
RATE = 1000.0
SCALE = 2.0
AXES = ("rep", "shard")


def nn(a, b, precision=None):
    return lax.dot_general(
        a, b, (((1,), (0,)), ((), ())), precision=precision, preferred_element_type=F32
    )


def nt(a, b, precision=None):
    return lax.dot_general(
        a, b, (((1,), (1,)), ((), ())), precision=precision, preferred_element_type=F32
    )


def tn(a, b, precision=None):
    return lax.dot_general(
        a, b, (((0,), (0,)), ((), ())), precision=precision, preferred_element_type=F32
    )


def iota(shape, dim):
    return lax.broadcasted_iota(jnp.int32, shape, dim)


def lanes(x, low, high):
    at = iota(x.shape, x.ndim - 1)
    return jnp.where((at >= low) & (at < high), x, jnp.zeros_like(x))


def norm_parts(x):
    centered = x - jnp.mean(x, -1, keepdims=True)
    rstd = lax.rsqrt(jnp.mean(centered * centered, -1, keepdims=True) + 1e-05)
    return centered * rstd, rstd


def norm_back(grad, gain, unit, rstd):
    g = grad * gain
    return rstd * (
        g - jnp.mean(g, -1, keepdims=True) - unit * jnp.mean(g * unit, -1, keepdims=True)
    )


def load(pieces, spots, target, sems):
    copies = []
    for index, (piece, (row, column)) in enumerate(zip(pieces, spots, strict=True)):
        rows, columns = piece.shape
        if not isinstance(row, int):
            row = pl.multiple_of(row, rows)
        if not isinstance(column, int):
            column = pl.multiple_of(column, columns)
        place = target.at[pl.ds(row, rows), pl.ds(column, columns)]
        copies.append(pltpu.make_async_copy(piece, place, sems.at[index]))
    for copy in copies:
        copy.start()

    def wait():
        for copy in copies:
            copy.wait()

    return wait


def expand_heads(x, heads):
    rows, width = x.shape
    head_of = iota((rows, width), 1) // HEAD_DIM
    return jnp.concatenate(
        [jnp.where(head_of == h, x, jnp.zeros_like(x)) for h in range(heads)], 0
    )


def collapse_heads(x, heads):
    rows, width = x.shape[0] // heads, x.shape[1]
    head_of = iota((rows, width), 1) // HEAD_DIM
    total = jnp.zeros((rows, width), F32)
    for h in range(heads):
        total = total + jnp.where(head_of == h, x[h * rows : (h + 1) * rows], 0.0)
    return total


def column(row):
    return jnp.transpose(jnp.broadcast_to(row, (8, row.shape[1])))[:, :1]


def split_kernel(ready, d_t, f_t, head, live, qkv, out, up, down, left, right, up_part, down_part, sems):
    shard = lax.axis_index("shard")
    core = shard % 2
    rows, width = out.shape
    below = left.shape[0] - rows
    half = down_part.shape[0]
    blocks = up_part.shape[1] // half
    part = width // 2
    copies = []

    def move(piece, to):
        copies.append(pltpu.make_async_copy(piece, to, sems.at[len(copies)]))
        copies[-1].start()

    for j in range(4):
        at = pl.multiple_of(core * part, part)
        piece = out.at[:, pl.ds(at, part)] if j == 3 else qkv.at[:, pl.ds(at + j * width, part)]
        move(piece, (left, right)[j // 2].at[pl.ds(0, rows), pl.ds(j % 2 * part, part)])
    move(down.at[pl.ds(pl.multiple_of(core * half, half), half), :], down_part)
    for b in range(blocks):
        at = pl.multiple_of((2 * b + core) * half, half)
        move(up.at[:, pl.ds(at, half)], up_part.at[:, pl.ds(b * half, half)])
    ready()
    left[rows:, :] = jnp.zeros((below, width), BF16)
    right[rows:, :] = jnp.zeros((below, width), BF16)
    flat = jnp.concatenate([d_t[0], d_t[1]], 0).astype(BF16)
    count = flat.shape[0] // below
    for j in range(count):
        left[rows:, j * rows : (j + 1) * rows] = flat[j * below : (j + 1) * below]
    alive = jnp.sum((live[...] >= 0).astype(F32), keepdims=True)
    two = jnp.where(iota((below, rows), 0) == 0, head[...], alive)
    left[rows:, count * rows : (count + 1) * rows] = two.astype(BF16)
    right[rows:, : f_t.shape[1]] = f_t[...].astype(BF16)
    for copy in copies:
        copy.wait()


def assemble_kernel(column, ready, source, *refs):
    pieces, (mat, sems) = refs[:-2], refs[-2:]
    rep, core = lax.axis_index("rep"), lax.axis_index("shard") % 2
    rows, part = mat.shape[0] // len(pieces), mat.shape[1]
    tops = [piece.at[pl.ds(0, rows), pl.ds(column * part, part)] for piece in pieces]
    load(tops, [(source[rep, core, k] * rows, 0) for k in range(len(pieces))], mat, sems)()


def unpack_kernel(rank, rows, ready, source, *refs):
    pieces = refs[:-8]
    wide_d, own, other, head, count, flat, both, sems = refs[-8:]
    rep, core = lax.axis_index("rep"), lax.axis_index("shard") % 2
    n = len(pieces) // 2
    below, hidden = both.shape
    blocks = 10 * rank // below
    copies = []
    for k in range(n):
        r = source[rep, core, k]
        lanes_d = pl.ds(pl.multiple_of(r * rows, rows), rows)
        lanes_f = pl.ds(pl.multiple_of(r * (hidden // n), hidden // n), hidden // n)
        low = pl.ds(rows, below)
        for j in range(blocks + 1):
            place = flat.at[pl.ds(j * below, below), lanes_d]
            copies.append((pieces[k].at[low, pl.ds(j * rows, rows)], place))
        copies.append((pieces[n + k].at[low, pl.ds(0, hidden // n)], both.at[:, lanes_f]))
    copies = [pltpu.make_async_copy(a, b, sems.at[i]) for i, (a, b) in enumerate(copies)]
    for copy in copies:
        copy.start()
    for copy in copies:
        copy.wait()
    ready()
    wide_d[0] = flat[0 : 5 * rank, :]
    wide_d[1] = flat[5 * rank : 10 * rank, :]
    head[...] = flat[10 * rank : 10 * rank + 1, :].astype(F32)
    live = flat[10 * rank + 1 : 10 * rank + 2, :].astype(F32)
    count[...] = jnp.broadcast_to(jnp.sum(live, keepdims=True) / rows, count.shape)
    half = hidden // n // 2
    value = both[...]
    halves = [
        jnp.concatenate([value[:, (2 * r + c) * half : (2 * r + c + 1) * half] for r in range(n)], 1)
        for c in range(2)
    ]
    mine = (core == 0).astype(F32)
    zero, one = halves[0].astype(F32), halves[1].astype(F32)
    own[...] = (zero * mine + one * (1.0 - mine)).astype(BF16)
    other[...] = (zero * (1.0 - mine) + one * mine).astype(BF16)


def factors(ref, rank):
    value = ref[...]
    zero = jnp.zeros((4 * rank, value.shape[1]), value.dtype)
    return jnp.concatenate([zero, value[:rank]], 0), jnp.concatenate([zero, value[rank:]], 0)


def front_kernel(offset, ready, parts, pos_v, seg_v, table, gains, bias, h1, xl, hl, prow, tok):
    tokens, width = h1.shape
    slots = xl.shape[0]
    seq = (lax.axis_index("shard") + offset) % 2
    step = min(128, tokens)
    ready()
    position = pos_v[pl.ds(seq, 1), :]
    total = parts[0][...]
    for part in parts[1:]:
        total = total + part[...]
    tok[...] = total
    for i in range(tokens // step):
        rows = pl.ds(i * step, step)
        place = position[:, i * step : (i + 1) * step]
        onehot = (iota((tokens, step), 0) == place).astype(BF16)
        pos = tn(onehot, table[...])
        prow[rows, :] = pos.astype(BF16)
        unit, _ = norm_parts(tok[rows, :].astype(F32) + pos)
        h1[rows, :] = (unit * gains[0:1, :] + bias[0:1, :]).astype(BF16)
    segment = seg_v[pl.ds(seq, 1), :]
    after = pltpu.roll(jnp.broadcast_to(segment, (8, tokens)), tokens - 1, 1)[0:1]
    final = (segment != after) | (iota((1, tokens), 1) == tokens - 1)
    pick = ((segment == iota((slots, tokens), 0)) & final).astype(BF16)
    xl[...] = nn(pick, tok[...]) + nn(pick, prow[...])
    hl[...] = nn(pick, h1[...]).astype(BF16)


def kv_half(rank, h1, mat, at, u, ad, bias, kv):
    part = mat[0].shape[1]
    width = 2 * part
    cols = pl.ds(at, part)
    for j in range(2):
        to = pl.ds(pl.multiple_of(at + j * width, part), part)
        for b in range(len(h1)):
            total = nn(h1[b][...], mat[1 + j][...]) + bias[4 + j : 5 + j, cols]
            total = total + SCALE * nn(lanes(u[b], rank * (1 + j), rank * (2 + j)), ad[1, :, cols])
            kv[b, :, to] = total.astype(BF16)


def rows_kernel(micro, rank, ready, flush, *refs):
    seg_v, refs = refs[0], refs[1:]
    h1, hl, xl = refs[:micro], refs[micro : 2 * micro], refs[2 * micro : 3 * micro]
    ad, gains, bias = refs[3 * micro : 3 * micro + 3]
    mats = refs[3 * micro + 3 : 3 * micro + 11]
    kv, ukv_t, o, x1, q, p_t, u, w_out, e1, ukv = refs[3 * micro + 11 :]
    core = lax.axis_index("shard") % 2
    slots, width = hl[0].shape
    heads = width // HEAD_DIM
    tokens = h1[0].shape[0]
    part = width // 2
    places = [pl.multiple_of(core * part, part), pl.multiple_of((1 - core) * part, part)]
    mats = [(mats[:4], places[0]), (mats[4:], places[1])]
    ready(ad, *h1)
    down, up = ad[0], ad[1]
    for b in range(micro):
        ukv[b] = lanes(nt(h1[b][...], down).astype(BF16), rank, 3 * rank)
        ukv_t[b] = nt(down, h1[b][...]).astype(BF16)
    ready(*mats[0][0][1:3], bias)
    kv_half(rank, h1, *mats[0], ukv, ad, bias, kv)
    ready()
    kv_half(rank, h1, *mats[1], ukv, ad, bias, kv)
    flush(0)
    flush(1)
    for mat, at in mats:
        w_out[:, pl.ds(at, part)] = mat[3][...]
    flush(7)
    h_last = jnp.concatenate([h[...] for h in hl], 0)
    x_last = jnp.concatenate([x[...] for x in xl], 0)
    u_q = lanes(nt(h_last, down).astype(BF16), 0, rank)
    for mat, at in mats:
        cols = pl.ds(at, part)
        total = nn(h_last, mat[0][...]) + bias[3:4, cols] + SCALE * nn(u_q, ad[1, :, cols])
        q[:, cols] = total.astype(BF16)
    q_all = q[...]
    parts = []
    for b in range(micro):
        wide_q = expand_heads(q_all[b * slots : (b + 1) * slots], heads)
        scores = HEAD_DIM ** (-0.5) * nt(kv[b, :, :width], wide_q)
        segment = column(seg_v[pl.ds((core + b) % 2, 1), :])
        inside = segment == iota((tokens, heads * slots), 1) % slots
        scores = jnp.where(inside, scores, -1000000000.0)
        e = jnp.exp(scores - jnp.max(scores, 0, keepdims=True))
        probs = e / jnp.sum(e, 0, keepdims=True)
        p_t[b] = probs
        parts.append(collapse_heads(tn(probs.astype(BF16), kv[b, :, width:]), heads))
    flush(5)
    o_all = jnp.concatenate(parts, 0).astype(BF16)
    o[...] = o_all
    u_o = lanes(nt(o_all, down).astype(BF16), 3 * rank, 4 * rank)
    mid = x_last + nn(o_all, w_out[...]) + bias[6:7, :] + SCALE * nn(u_o, up)
    x1[...] = mid
    unit, _ = norm_parts(mid)
    h2 = (unit * gains[1:2, :] + bias[1:2, :]).astype(BF16)
    u_up = lanes(nt(h2, down).astype(BF16), 4 * rank, 5 * rank)
    e1[:, :width] = h2
    e1[:, width:] = jnp.zeros_like(e1[:, width:])
    e1[:, width : width + 5 * rank] = u_up
    u[...] = u_q + u_o + u_up


def preload_kernel(n, ready, source, _, *refs):
    w_up, w_down, sems = refs[-3:]
    rep, core = lax.axis_index("rep"), lax.axis_index("shard") % 2
    loads = []
    for index, wide in enumerate((w_up, w_down)):
        pieces = refs[index * n : (index + 1) * n]
        height = pieces[0].shape[0]
        spots = [(source[rep, core, k] * height, 0) for k in range(n)]
        loads.append(load(pieces, spots, wide, sems.at[index]))
    for wait in loads:
        wait()


def ffn_kernel(rank, last, ready, source, own, sib, f_own, f_sib, bias, *refs):
    up_last, down_last, _, _, f, a, w_up, w_down, mine, send, sems = refs
    width = w_up.shape[0]
    rep, core = lax.axis_index("rep"), lax.axis_index("shard") % 2
    loads = []
    for index, (piece, wide) in enumerate(((up_last, w_up), (down_last, w_down))):
        spots = [(source[rep, core, last] * piece.shape[0], 0)]
        loads.append(load([piece], spots, wide, sems.at[index]))
    ready()
    lane = 5 * rank
    rows = own.shape[0]
    h2 = jnp.concatenate([own[:, :width], sib[:, :width]], 0)
    pair_own, pair_sib = factors(f_own, rank), factors(f_sib, rank)
    extra = jnp.concatenate(
        [
            nn(own[:, width : width + lane], pair_own[1]),
            nn(sib[:, width : width + lane], pair_sib[1]),
        ],
        0,
    )
    loads[0]()
    total = nn(h2, w_up[...]) + bias[...] + SCALE * extra
    f[...] = total
    low = jax.nn.gelu(total, approximate=True).astype(BF16)
    a[...] = low
    for out, at, pair in ((mine, 0, pair_own), (send, rows, pair_sib)):
        out[:, width:] = jnp.zeros_like(out[:, width:])
        out[:, width : width + lane] = nt(low[at : at + rows], pair[0])
    loads[1]()
    y = nn(low, w_down[...])
    mine[:, :width] = y[:rows]
    send[:, :width] = y[rows:]


def score_kernel(rank, ready, x1, mine, recv, ad, gains, bias, head, x2, u_dn, score):
    ready()
    width = x1.shape[1]
    lane = 5 * rank
    u = (mine[:, width : width + lane] + recv[:, width : width + lane]).astype(BF16)
    u_dn[...] = u
    end = x1[...] + mine[:, :width] + recv[:, :width] + bias[11:12, :] + SCALE * nn(u, ad[1])
    x2[...] = end
    unit, _ = norm_parts(end)
    token = jnp.sum((unit * gains[2:3, :] + bias[2:3, :]) * head[...], -1, keepdims=True)
    score[...] = jnp.broadcast_to(token, score.shape)


def loss_kernel(rank, members, ready, *refs):
    scores = refs[:members]
    x2, u_dn, pairs, count, ad, gains, bias, head = refs[members : members + 8]
    e2, g_end, g_dn, small = refs[members + 8 :]
    ready()
    rows, width = x2.shape
    half = rows // 2

    def value(m):
        if m % 2 == 0:
            return scores[m][...]
        return jnp.concatenate([scores[m][half:, :], scores[m][:half, :]], 0)

    level = [value(m) for m in range(members)]
    while len(level) > 1:
        level = [level[i] + level[i + 1] for i in range(0, len(level), 2)]
    mean_reward = level[0][:, :1] / members
    at = iota((rows, pairs.shape[1]), 0)
    pick = (at == pairs[0:1, :]).astype(F32) - (at == pairs[1:2, :]).astype(F32)
    live = (pairs[0:1, :] >= 0).astype(F32)
    diff = jnp.sum(pick * mean_reward, 0, keepdims=True)
    terms = live * jax.nn.softplus(-diff)
    grad_diff = -live * jax.nn.sigmoid(-diff) / count[:, :1]
    grad_score = jnp.sum(pick * grad_diff, -1, keepdims=True) / members
    unit, rstd = norm_parts(x2[...])
    final = unit * gains[2:3, :] + bias[2:3, :]
    small[...] = jnp.zeros_like(small)
    small[0:1, :] = jnp.sum(final * grad_score, 0, keepdims=True)
    small[1:2, :] = jnp.broadcast_to(jnp.sum(terms, -1, keepdims=True), (1, width))
    end = norm_back(grad_score * head[...], gains[2:3, :], unit, rstd)
    g_end[...] = end
    g_ff = end.astype(BF16)
    left = lanes((SCALE * nt(g_ff, ad[1])).astype(BF16), 4 * rank, 5 * rank)
    g_dn[...] = SCALE * tn(u_dn[...], g_ff)
    e2[:, :width] = g_ff
    e2[:, width:] = jnp.zeros_like(e2[:, width:])
    e2[:, width : width + 5 * rank] = left


def slope_kernel(ready, f, _, out):
    x = f[...]
    c0, c1 = math.sqrt(2.0 / math.pi), 0.044715
    t = jnp.tanh(c0 * (x + c1 * x * x * x))
    out[...] = 0.5 * (1.0 + t) + 0.5 * x * (1.0 - t * t) * (c0 * (1.0 + 3.0 * c1 * x * x))


def ffn_back_kernel(rank, ready, own, sib, slope, f_own, f_sib, wide_u, wide_d,
                    mine, send, g_out):
    width = wide_u.shape[0]
    lane = 5 * rank
    ready()
    rows = own.shape[0]
    left_own, left_sib = own[:, width : width + lane], sib[:, width : width + lane]
    g_ff = jnp.concatenate([own[:, :width], sib[:, :width]], 0)
    pair_own, pair_sib = factors(f_own, rank), factors(f_sib, rank)
    extra = jnp.concatenate([nn(left_own, pair_own[0]), nn(left_sib, pair_sib[0])], 0)
    g_a = (nt(g_ff, wide_d[...]) + extra).astype(BF16)
    g_f = (g_a.astype(F32) * slope[...]).astype(BF16)
    g_h = nt(g_f, wide_u[...])
    for out, low, factor in ((mine, 0, pair_own), (send, rows, pair_sib)):
        out[:, :width] = g_h[low : low + rows]
        out[:, width:] = jnp.zeros_like(out[:, width:])
        out[:, width : width + lane] = SCALE * nt(g_f[low : low + rows], factor[1])
    g_out[...] = g_f


def hidden_kernel(rank, ready, own, sib, e1_own, e1_sib, a, g_f, mine, send):
    rows = own.shape[0]
    cut = slice(own.shape[1] - 128, own.shape[1] - 128 + 5 * rank)
    for out, low, left, u in ((mine, 0, own, e1_own), (send, rows, sib, e1_sib)):
        out[0:rank, :] = tn(left[:, cut], a[low : low + rows, :])[4 * rank :]
        out[rank:, :] = SCALE * tn(u[:, cut], g_f[low : low + rows, :])[4 * rank :]


def factor_kernel(rank, half, ready, mine, other, err, start, mat, left):
    ready()
    core = lax.axis_index("shard") % 2
    first = (core == 0).astype(F32)
    even = mine[...] * first + other[...] * (1.0 - first)
    odd = mine[...] * (1.0 - first) + other[...] * first
    parts = []
    for r in range(mine.shape[1] // half):
        cut = slice(r * half, (r + 1) * half)
        parts += [even[:, cut], odd[:, cut]]
    mat[...] = jnp.concatenate(parts, 1) + err[...]
    left[...] = nn(start[...], mat[...], EXACT)


def rows_back_kernel(micro, rank, ready, *refs):
    mine, recv, g_end, g_dn, small, x1, e1, u, o, q, p_t, kv, ukv_t = refs[:13]
    hl = refs[13 : 13 + micro]
    h1 = refs[13 + micro : 13 + 2 * micro]
    ad, gains, err, start, w_out, mat, left = refs[13 + 2 * micro :]
    ready(ad, gains)
    rows, width = x1.shape
    slots = rows // micro
    heads = width // HEAD_DIM
    lane = 5 * rank
    down, up = ad[0], ad[1]
    h2 = e1[:, :width]
    u_rows = u[...]
    g_u = (mine[:, width : width + lane] + recv[:, width : width + lane]).astype(BF16)
    g_h2 = (mine[:, :width] + recv[:, :width] + nn(g_u, down)).astype(BF16)
    grad_in = tn(g_u, h2)
    unit, rstd = norm_parts(x1[...])
    g_mid = g_end[...] + norm_back(g_h2.astype(F32), gains[1:2, :], unit, rstd)
    g_att = g_mid.astype(BF16)
    grad_out = g_dn[...] + SCALE * tn(lanes(u_rows, 3 * rank, 4 * rank), g_att)
    g_ol = lanes((SCALE * nt(g_att, up)).astype(BF16), 3 * rank, 4 * rank)
    grad_in = grad_in + tn(g_ol, o[...])
    g_o = (nt(g_att, w_out[...]) + nn(g_ol, down)).astype(BF16)
    ready()
    scale = HEAD_DIM ** (-0.5)

    both = (lane, 2 * heads * slots)
    group, side = iota(both, 0) // rank, iota(both, 1) // (heads * slots)
    keep = jnp.where(group == 1 + side, jnp.where(side == 0, scale, 1.0), 0.0)

    for b in range(micro):
        pick = slice(b * slots, (b + 1) * slots)
        wide_g = expand_heads(g_o[pick], heads)
        wide_q = expand_heads(q[pick, :], heads)
        probs = p_t[b]
        g_p = nt(kv[b, :, width:], wide_g)
        g_s = (probs * (g_p - jnp.sum(probs * g_p, 0, keepdims=True))).astype(BF16)
        g_q = (scale * collapse_heads(tn(g_s, kv[b, :, :width]), heads)).astype(BF16)
        u_q = lanes(u_rows[pick], 0, rank)
        tall = jnp.concatenate([g_s, probs.astype(BF16)], 1)
        flat = jnp.concatenate([wide_q, wide_g], 0)
        inner = (nn(ukv_t[b], tall) * keep).astype(BF16)
        grad_out = grad_out + SCALE * (tn(u_q, g_q) + nn(inner, flat))
        g_uq = lanes((SCALE * nt(g_q, up)).astype(BF16), 0, rank)
        inner = (nt(up, flat) * keep).astype(BF16)
        g_ukv = (SCALE * nt(inner, tall)).astype(BF16)
        grad_in = grad_in + tn(g_uq, hl[b][...]) + nn(g_ukv, h1[b][...])
    mat[0] = grad_in + err[0]
    mat[1] = grad_out + err[1]
    first = start.shape[1]
    left[0:first, :] = nn(start[0], mat[0], EXACT)
    left[first : 2 * first, :] = nn(start[1], mat[1], EXACT)
    left[2 * first :, :] = small[...]


def orthonormal_rows(refs):
    count = refs[0].shape[0]
    for k in range(count):
        for ref in refs:
            block = ref[...]
            row = block[k : k + 1, :]
            dots = jnp.sum(block * row, -1, keepdims=True)
            scale = lax.rsqrt(dots[k : k + 1] + 1e-06)
            row = row * scale
            at = iota(block.shape, 0)
            later = jnp.where(at > k, block - (dots * scale) * row, block)
            ref[...] = jnp.where(at == k, row, later)


def ortho_kernel(rank, ready, d_a, d_b, f_a, f_b, mat_d, mat_f, ph_d, ph_f, head, note):
    count = rank
    for j in range(2):
        part = slice(j * count, (j + 1) * count)
        ph_d[j] = d_a[part, :] + d_b[part, :]
    ph_f[...] = f_a[...] + f_b[...]
    rest = d_a[2 * count :, :] + d_b[2 * count :, :]
    refs = (ph_d.at[0], ph_d.at[1], ph_f)
    orthonormal_rows(refs)
    ready()
    grad = rest[0:1, :]
    head[...] = grad
    parts = []
    for ref, mat in zip(refs, (mat_d.at[0], mat_d.at[1], mat_f), strict=True):
        parts.append(nt(ref[...], mat[...], EXACT))
    for ref in refs:
        parts.append(nt(ref[...], ref[...], EXACT))
    parts.append(jnp.broadcast_to(jnp.sum(grad * grad, keepdims=True), (count, 1)))
    parts.append(jnp.broadcast_to(rest[1:2, :1], (count, 1)))
    used = sum(x.shape[1] for x in parts)
    parts.append(jnp.zeros((count, 128 - used), F32))
    own = jnp.concatenate(parts, 1)

    @pl.loop(0, note.shape[0])
    def _(i):
        note[i] = own


def final_kernel(rank, n, m, ready, notes, ph_d, ph_f, ph_do, ph_fo, ghead, mat_d, mat_f,
                 wd, wf, wh, md, mf, mh,
                 nd, nf, nh, nmd, nmf, nmh, err_d, err_f, q_d, q_f, mean_loss, norm):
    ready()
    shard = lax.axis_index("shard")
    count = rank
    sizes = (5 * rank, 5 * rank, 2 * rank)
    total = jnp.zeros((1, 1), F32)
    loss = jnp.zeros((1, 1), F32)
    own = jnp.zeros((count, 128), F32)
    for s in range(m):
        block = notes[s]
        for r in range(1, n):
            block = block + notes[r * m + s]
        own = jnp.where(shard == s, block, own)
        note = notes[s]
        at, gram = 0, sum(sizes)
        for size in sizes:
            right = block[:, at : at + size]
            inner = note[:, gram : gram + count]
            total = total + jnp.sum(right * nn(inner, right, EXACT), keepdims=True)
            at += size
            gram += count
        total = total + note[0:1, gram : gram + 1]
        loss = loss + note[0:1, gram + 1 : gram + 2]
    grad_norm = jnp.sqrt(total)
    clip = jnp.minimum(1.0, CLIP / (grad_norm + 1e-06))
    mean_loss[...] = loss / m
    norm[...] = grad_norm
    at = 0
    for j in range(2):
        right = own[:, at : at + sizes[j]]
        q_d[j] = right
        at += sizes[j]
        err_d[j] = mat_d[j] - tn(right, ph_d[j], EXACT) * (1.0 / n)
        fresh = MOMENTUM * md[j] + clip * tn(right, ph_do[j], EXACT)
        nmd[j] = fresh
        nd[j] = wd[j] - RATE * fresh
    right = own[:, at : at + sizes[2]]
    q_f[...] = right
    err_f[...] = mat_f[...] - tn(right, ph_f[...], EXACT) * (1.0 / n)
    fresh = MOMENTUM * mf[...] + clip * tn(right, ph_fo[...], EXACT)
    nmf[...] = fresh
    nf[...] = wf[...] - RATE * fresh
    fresh = MOMENTUM * mh[...] + clip * ghead[...]
    nmh[...] = fresh
    nh[...] = wh[...] - RATE * fresh


class Raw:
    def __init__(self, array):
        self.array = array


class Scalars(Raw):
    pass


class Far(Raw):
    pass


class Fresh(Raw):
    pass


class Part:
    def __init__(self, array, rows):
        self.array, self.rows = array, rows


class Kept:
    def __init__(self, shape, dtype):
        self.shape, self.dtype = tuple(shape), dtype


class Placed(Kept):
    pass


def call(body, outs, args, scratch=(), vmem=60, name=None, groups=None, aliases=None, flushes=False):
    arrays, specs, staged = [], [], []
    for arg in args:
        arrays.append(arg.array if isinstance(arg, Raw | Part) else arg)
        space = pl.ANY
        if isinstance(arg, Scalars):
            space = pltpu.SMEM
        elif isinstance(arg, Fresh):
            space = pltpu.VMEM
        elif isinstance(arg, Far):
            space = pltpu.HBM
        specs.append(pl.BlockSpec(memory_space=space))
        if isinstance(arg, Part):
            staged.append(pltpu.VMEM((arg.rows, *arg.array.shape[1:]), arg.array.dtype))
        elif not isinstance(arg, Raw):
            staged.append(pltpu.VMEM(arg.shape, arg.dtype))
    results = [pltpu.VMEM(o.shape, o.dtype) for o in outs if not isinstance(o, Kept)]

    def kernel(*refs):
        ins, refs = refs[: len(args)], refs[len(args) :]
        targets, refs = refs[: len(outs)], refs[len(outs) :]
        held, refs = refs[: len(staged)], refs[len(staged) :]
        buffers, refs = refs[: len(results)], refs[len(results) :]
        extra, sems = refs[:-1], refs[-1]
        copies, given, i = {}, [], 0
        for arg, ref in zip(args, ins, strict=True):
            if isinstance(arg, Raw):
                given.append(ref)
                continue
            origin = ref.at[pl.ds(0, arg.rows)] if isinstance(arg, Part) else ref
            copies[id(held[i])] = pltpu.make_async_copy(origin, held[i], sems.at[i])
            given.append(held[i])
            i += 1
        for copy in copies.values():
            copy.start()

        def ready(*some):
            for key in [id(r) for r in some] or list(copies):
                copies.pop(key).wait()

        local, back, i = [], {}, 0
        for j, out in enumerate(outs):
            if isinstance(out, Kept):
                local.append(targets[j])
                continue
            local.append(buffers[i])
            back[j] = pltpu.make_async_copy(buffers[i], targets[j], sems.at[len(staged) + i])
            i += 1
        def flush(j):
            back[j].start()
            begun.append(j)

        begun = []
        if groups:
            given = [given[:groups], *given[groups:]]
        body(ready, *((flush,) if flushes else ()), *given, *local, *extra)
        for j, copy in back.items():
            if j not in begun:
                copy.start()
        for copy in back.values():
            copy.wait()

    def place(out):
        if type(out) is Kept:
            return pltpu.VMEM
        return pl.ANY if isinstance(out, Kept) else pltpu.HBM

    return pl.pallas_call(
        kernel,
        out_shape=tuple(jax.ShapeDtypeStruct(o.shape, o.dtype) for o in outs),
        in_specs=specs,
        out_specs=tuple(pl.BlockSpec(memory_space=place(o)) for o in outs),
        scratch_shapes=[
            *staged, *results, *scratch, pltpu.SemaphoreType.DMA((max(1, len(staged) + len(results)),)),
        ],
        compiler_params=pltpu.CompilerParams(vmem_limit_bytes=vmem << 20),
        cost_estimate=pl.CostEstimate(flops=0, bytes_accessed=0, transcendentals=0),
        input_output_aliases=aliases or {},
        name=name,
    )(*arrays)


def shaped(shape, dtype):
    return jax.ShapeDtypeStruct(tuple(shape), dtype)


def ring_order(count):
    side = math.isqrt(count // 2)
    if side < 2 or 2 * side * side != count:
        return list(range(count))
    depth = 2 * side
    cells = []
    for z in range(depth):
        ys = range(1, side) if z % 2 == 0 else range(side - 1, 0, -1)
        cells += [(z, y) for y in ys]
    cells += [(z, 0) for z in range(depth - 1, -1, -1)]
    return [z * side + y for z, y in cells]


def pairs_of(n, m, move):
    return [(r * m + s, t[0] * m + t[1]) for r in range(n) for s in range(m) for t in [move(r, s)]]


def on_device(n, m, *args):
    (
        token_ids, positions, segment_ids, pair_index, embed_table, pos_table,
        base_qkv, base_out, base_up, base_down, base_gains, base_bias,
        adapt_d, adapt_f, head, mom_d, mom_f, mom_head, err_d, err_f, qstart_d, qstart_f,
    ) = args
    micro, tokens = token_ids.shape
    held, width = embed_table.shape
    pairs = pair_index.shape[1]
    slots = 2 * pairs
    rows = micro * slots
    hidden = base_up.shape[1]
    rank = adapt_f.shape[2] // 2
    heads = width // HEAD_DIM
    rd, rf = base_up.shape[0], base_down.shape[0]
    half = rf // 2
    own_hidden = hidden // 2
    rep, shard = lax.axis_index("rep"), lax.axis_index("shard")
    core = shard % 2

    order = ring_order(n)
    place = {r: i for i, r in enumerate(order)}
    around = pairs_of(
        n, m, lambda r, s: (order[(place[r] + (1 if s % 2 == 0 else -1)) % n], s)
    )
    turns = [
        [[order[(place[r] + (-k if c == 0 else k)) % n] for k in range(n)] for c in range(2)]
        for r in range(n)
    ]
    source = Scalars(jnp.asarray(np.array(turns, np.int32)))

    def send(x, perm):
        return lax.ppermute(x, AXES, perm)

    def across(x, mask):
        return send(x, pairs_of(n, m, lambda r, s: (r, s ^ mask)))

    def ring(x):
        out = []
        for _ in range(n - 1):
            x = send(x, around)
            out.append(x)
        return out

    def pick(x, index, axis):
        return lax.dynamic_index_in_dim(x, index, axis, keepdims=False)

    d_t = adapt_d[0].transpose(1, 2, 0)
    f_t = adapt_f[0].T
    below = 2 * rank
    live = pair_index[..., 0].reshape(1, micro * pairs)
    whole_blocks = rd % 128 == 0 and half % 128 == 0
    if whole_blocks:
        left, right, up_part, down_part = call(
            split_kernel,
            [shaped((rd + below, width), BF16), shaped((rd + below, width), BF16),
             shaped((rd, own_hidden), BF16), shaped((half, width), BF16)],
            [d_t, f_t, head, live, Raw(base_qkv), Raw(base_out), Raw(base_up), Raw(base_down)],
            [pltpu.SemaphoreType.DMA((n + 5,))],
            vmem=56, name="split",
        )
    else:
        two = jnp.concatenate([head, jnp.broadcast_to(jnp.sum((live >= 0).astype(F32)), (below - 1, rd))], 0)
        flat = [x for x in d_t.reshape(10 * rank // below, below, rd)]
        first = jnp.concatenate([base_qkv, base_out], 1).reshape(rd, 4, 2, width // 2)
        first = pick(first, core, 2).reshape(rd, 2, width)
        sides = []
        for side, extra in enumerate((jnp.concatenate([*flat, two], 1), f_t)):
            extra = jnp.pad(extra.astype(BF16), ((0, 0), (0, width - extra.shape[1])))
            sides.append(jnp.concatenate([first[:, side], extra], 0))
        left, right = sides
        up_part = pick(base_up.reshape(rd, n, 2, half), core, 2).reshape(rd, own_hidden)
        down_part = pick(base_down.reshape(2, half, width), core, 0)

    def after(x, *others):
        return pl.pallas_call(
            lambda *refs: None,
            out_shape=jax.ShapeDtypeStruct(x.shape, x.dtype),
            in_specs=[pl.BlockSpec(memory_space=pl.ANY)] * (1 + len(others)),
            out_specs=pl.BlockSpec(memory_space=pl.ANY),
            input_output_aliases={0: 0},
            cost_estimate=pl.CostEstimate(flops=0, bytes_accessed=0, transcendentals=0),
            name="after",
        )(x, *others)

    def lookup(*start):
        ids = jnp.stack([pick(token_ids, (core + b) % micro, 0) for b in range(micro)])
        near = ids - shard * held
        inside = (near >= 0) & (near < held)
        found = jnp.take(embed_table, after(jnp.clip(near, 0, held - 1), *start), axis=0)
        found = jnp.where(inside[..., None], found, jnp.zeros_like(found))
        return found[0], found[1]

    def shared(own, given, *others):
        own = own + across(after(given, *others), 1)
        mask = 2
        while mask < m // 2:
            own = own + across(own, mask)
            mask *= 2
        return own, across(own, mask) if m > 2 else own

    bias = base_bias.reshape(-1, width)
    bias_1 = pick(base_bias[7 * width : 7 * width + hidden].reshape(n, 2, half), core, 1)
    bias_1 = bias_1.reshape(1, own_hidden)
    local = (jnp.arange(micro) + core) % micro * slots
    pair_rows = jnp.where(pair_index >= 0, pair_index + local[:, None, None], -1)
    pair_rows = pair_rows.reshape(micro * pairs, 2).T

    pos_rows = pos_table[:tokens]

    lefts, rights, ups, downs = [left], [right], [up_part], [down_part]

    def behind(low, high, *gate):
        for k in range(low, min(high, n)):
            if gate:
                ups[-1], downs[-1] = after(ups[-1], *gate), after(downs[-1], *gate)
            gate = ()
            ups.append(send(ups[-1], around))
            downs.append(send(downs[-1], around))

    for k in range(1, n):
        gate = []
        if k == 9:
            gate = [ups[1], downs[1]]
        if k == 4:
            gate = [tok_own]
        if k == 7:
            gate = [tok_far]
        if gate:
            lefts[-1], rights[-1] = after(lefts[-1], *gate), after(rights[-1], *gate)
        lefts.append(send(lefts[-1], around))
        rights.append(send(rights[-1], around))
        if k == 1:
            ups[-1], downs[-1] = ups[-1], downs[-1]
            ups.append(send(ups[-1], around))
            downs.append(send(downs[-1], around))
            own, given = lookup(lefts[1], rights[1], bias, bias_1, pos_rows, pair_rows)
        if k == 2:
            tok_own, tok_far = shared(own, given, lefts[2], rights[2], ups[1], downs[1])

    behind(2, 4, lefts[5])
    parts = [tok_own, tok_far] if m > 2 else [tok_own]
    both = tok_own + tok_far if m > 2 else tok_own
    toks = [parts, [across(both, 1)]]

    step_a = [*lefts, *rights]
    if whole_blocks:
        mats = []
        for k in range(4):
            mats += call(
                functools.partial(assemble_kernel, k % 2),
                [shaped((width, width // 2), BF16)],
                [source, *[Far(x) for x in (lefts, rights)[k // 2]]],
                [pltpu.SemaphoreType.DMA((n,))],
                vmem=8, name="assemble",
            )
        wide_d, f_own, f_other, wide_head, count_row = call(
            functools.partial(unpack_kernel, rank, rd),
            [shaped((2, 5 * rank, width), BF16), shaped((2 * rank, own_hidden), BF16),
             Kept((2 * rank, own_hidden), BF16), shaped((1, width), F32), shaped((1, 128), F32)],
            [source, *[Far(x) for x in step_a]],
            [pltpu.VMEM((10 * rank + below, width), BF16), pltpu.VMEM((below, hidden), BF16),
             pltpu.SemaphoreType.DMA((n * (10 * rank // below + 2),))],
            vmem=52, name="unpack",
        )
    else:
        turned = jnp.asarray(np.argsort(np.array(turns, np.int32), -1).astype(np.int32))
        place_at = lax.dynamic_slice(turned, (rep, core, 0), (1, 1, n)).reshape(n)
        steps_l, steps_r = [
            jnp.stack([pick(jnp.stack(x), place_at[r], 0) for r in range(n)]) for x in (lefts, rights)
        ]
        mats = [x[:, :rd].reshape(width, 2, width // 2) for x in (steps_l, steps_r)]
        mats = [x[:, j] for x in mats for j in range(2)]
        count_d = 10 * rank // below
        wide_d = steps_l[:, rd:, : count_d * rd].reshape(n, below, count_d, rd)
        wide_d = wide_d.transpose(2, 1, 0, 3).reshape(2, 5 * rank, width)
        wide_f = steps_r[:, rd:, :rf].reshape(n, 2 * rank, 2, half)
        wide_f = wide_f.transpose(2, 1, 0, 3).reshape(2, 2 * rank, own_hidden)
        f_own, f_other = pick(wide_f, core, 0), pick(wide_f, 1 - core, 0)
        last = steps_l[:, rd:, count_d * rd : (count_d + 1) * rd].astype(F32)
        wide_head = last[:, 0].reshape(1, width)
        count_row = jnp.broadcast_to(jnp.sum(last[:, 1, 0]), (1, 128))
    count = count_row[0, 0]
    behind(4, 5, *mats)
    f_sib = across(f_other, 1)
    mats += [across(x, 1) for x in mats]

    h1, xl, hl = [], [], []
    for b in range(micro):
        a, x, h = call(
            functools.partial(front_kernel, b),
            [Kept((tokens, width), BF16), Kept((slots, width), F32), Kept((slots, width), BF16)],
            [*toks[b], positions, segment_ids, pos_rows, base_gains, bias],
            [pltpu.VMEM((tokens, width), BF16), pltpu.VMEM((tokens, width), BF16)],
            groups=len(toks[b]), vmem=14, name="front",
        )
        h1.append(a)
        xl.append(x)
        hl.append(h)

    behind(5, 7, *hl, wide_d)
    kv, ukv_t, o, x1, q, p_t, u, w_out, e1 = call(
        functools.partial(rows_kernel, micro, rank),
        [shaped((micro, tokens, 2 * width), BF16), shaped((micro, 5 * rank, tokens), BF16),
         shaped((rows, width), BF16), shaped((rows, width), F32), shaped((rows, width), BF16),
         shaped((micro, tokens, heads * slots), F32), shaped((rows, 5 * rank), BF16),
         shaped((width, width), BF16), shaped((rows, width + 128), BF16)],
        [segment_ids, *h1, *hl, *xl, wide_d, base_gains, bias, *mats],
        [pltpu.VMEM((micro, tokens, 5 * rank), BF16)],
        vmem=60, flushes=True, name="rows",
    )
    behind(7, n, o)
    ups, downs = [[Far(y) for y in x] for x in (ups, downs)]
    e1_sib = across(e1, 1)
    w_up, w_down = call(
        functools.partial(preload_kernel, n - 1),
        [Kept((width, own_hidden), BF16), Kept((own_hidden, width), BF16)],
        [source, Raw(o), *ups[:-1], *downs[:-1]],
        [pltpu.SemaphoreType.DMA((2, n - 1))],
        vmem=4, name="preload",
    )
    f, a, w_up, w_down, y_mine, y_send = call(
        functools.partial(ffn_kernel, rank, n - 1),
        [Kept((2 * rows, own_hidden), F32), Kept((2 * rows, own_hidden), BF16),
         Kept((width, own_hidden), BF16), Kept((own_hidden, width), BF16)]
        + [Kept((rows, width + 128), F32)] * 2,
        [source, Fresh(e1), Fresh(e1_sib), f_own, f_sib, bias_1, ups[-1], downs[-1], Fresh(w_up), Fresh(w_down)],
        [pltpu.SemaphoreType.DMA((2, 1))],
        aliases={8: 2, 9: 3}, vmem=10, name="ffn",
    )
    x2, u_dn, score = call(
        functools.partial(score_kernel, rank),
        [Kept((rows, width), F32), Kept((rows, 5 * rank), BF16), Kept((rows, 128), F32)],
        [Fresh(x1), Fresh(y_mine), Fresh(across(y_send, 1)), wide_d, base_gains, bias, wide_head],
        vmem=10, name="score",
    )
    scores = [score] + [across(score, k) for k in range(1, m)]
    (slope,) = call(
        slope_kernel,
        [Kept((2 * rows, own_hidden), F32)],
        [Fresh(f), Fresh(score)],
        vmem=6, name="slope",
    )
    e2, g_end, g_dn, small = call(
        functools.partial(loss_kernel, rank, m),
        [Kept((rows, width + 128), BF16), Kept((rows, width), F32), Kept((5 * rank, width), F32),
         Kept((8, width), F32)],
        [*[Fresh(x) for x in scores], Fresh(x2), Fresh(u_dn), pair_rows, count_row, wide_d, base_gains, bias, wide_head],
        vmem=10, name="loss",
    )
    e2_sib = across(e2, 1)
    y_mine, y_send, g_f = call(
        functools.partial(ffn_back_kernel, rank),
        [Kept((rows, width + 128), F32)] * 2 + [Kept((2 * rows, own_hidden), BF16)],
        [Fresh(e2), Fresh(e2_sib), Fresh(slope), f_own, f_sib,
         Fresh(w_up), Fresh(w_down)],
        vmem=14, name="ffn_back",
    )
    y_other = across(y_send, 1)
    gf_mine, gf_send = call(
        functools.partial(hidden_kernel, rank),
        [Kept((2 * rank, own_hidden), F32)] * 2,
        [Fresh(x) for x in (e2, e2_sib, e1, e1_sib, a, g_f)],
        vmem=6, name="hidden",
    )
    mat_f, left_f = call(
        functools.partial(factor_kernel, rank, half),
        [Kept((2 * rank, hidden), F32), Kept((rank, hidden), F32)],
        [Fresh(gf_mine), Fresh(across(gf_send, 1)), err_f[0, 0].T, qstart_f[0].T],
        vmem=10, name="factor_f",
    )
    mat_d, left_d = call(
        functools.partial(rows_back_kernel, micro, rank),
        [Kept((2, 5 * rank, width), F32), Kept((2 * rank + 8, width), F32)],
        [Fresh(y_mine), Fresh(y_other), Fresh(g_end), Fresh(g_dn), Fresh(small),
         *[Fresh(x) for x in (x1, e1, u, o, q, p_t, kv, ukv_t, *hl, *h1)],
         wide_d, base_gains, err_d[0, 0].transpose(1, 2, 0), qstart_d[0].transpose(0, 2, 1), Fresh(w_out)],
        vmem=26, name="rows_back",
    )

    def rep_parts(x):
        bit, part = 1, jnp.zeros_like(x)
        while bit < n:
            part = send(x, pairs_of(n, m, lambda r, s, bit=bit: (r ^ bit, s)))
            bit *= 2
            if bit < n:
                x = x + part
        return Fresh(x), Fresh(part)

    ph_d, ph_f, total_head, note = call(
        functools.partial(ortho_kernel, rank),
        [Kept((2, rank, width), F32), Kept((rank, hidden), F32), Kept((1, width), F32),
         Kept((n * m, rank, 128), F32)],
        [*rep_parts(left_d), *rep_parts(left_f), Fresh(mat_d), Fresh(mat_f)],
        vmem=10, name="ortho",
    )
    notes = lax.all_to_all(note, AXES, 0, 0)
    own_ph_d = lax.dynamic_slice_in_dim(ph_d, rep * rd, rd, 2)
    own_ph_f = lax.dynamic_slice_in_dim(ph_f, rep * rf, rf, 1)
    own_head = lax.dynamic_slice_in_dim(total_head, rep * rd, rd, 1)
    nd, nf, nh, nmd, nmf, nmh, new_err_d, new_err_f, q_d, q_f, loss_sum, norm = call(
        functools.partial(final_kernel, rank, n, m),
        [shaped((2, 5 * rank, rd), F32), shaped((2 * rank, rf), F32), shaped((1, rd), F32)] * 2
        + [shaped((2, 5 * rank, width), F32), shaped((2 * rank, hidden), F32),
           shaped((2, rank, 5 * rank), F32), shaped((rank, 2 * rank), F32), shaped((1, 1), F32), shaped((1, 1), F32)],
        [Fresh(notes), Fresh(ph_d), Fresh(ph_f), Fresh(own_ph_d), Fresh(own_ph_f), Fresh(own_head),
         Fresh(mat_d), Fresh(mat_f), d_t, f_t, head, mom_d[0].transpose(1, 2, 0), mom_f[0].T, mom_head],
        vmem=16, name="final",
    )
    return (
        loss_sum[0, 0],
        count,
        norm[0, 0],
        nd.transpose(2, 0, 1)[None],
        nf.T[None],
        nh,
        nmd.transpose(2, 0, 1)[None],
        nmf.T[None],
        nmh,
        new_err_d.transpose(2, 0, 1)[None, None],
        new_err_f.T[None, None],
        q_d.transpose(0, 2, 1)[None],
        q_f.T[None],
    )


def solution(mesh):
    n, m = mesh.shape["rep"], mesh.shape["shard"]
    return jax.shard_map(
        functools.partial(on_device, n, m),
        mesh=mesh,
        in_specs=(
            P("rep", None),
            P("rep", None),
            P("rep", None),
            P("rep", None, None),
            P("shard", None),
            P(),
            P("rep", None),
            P("rep", None),
            P("rep", None),
            P("rep", None),
            P(),
            P(),
            P("shard", "rep", None, None),
            P("shard", "rep", None),
            P("shard", "rep"),
            P("shard", "rep", None, None),
            P("shard", "rep", None),
            P("shard", "rep"),
            P("shard", "rep", None, None, None),
            P("shard", "rep", None, None),
            P("shard", None, None, None),
            P("shard", None, None),
        ),
        out_specs=(
            P(),
            P(),
            P(),
            P("shard", "rep", None, None),
            P("shard", "rep", None),
            P("shard", "rep"),
            P("shard", "rep", None, None),
            P("shard", "rep", None),
            P("shard", "rep"),
            P("shard", "rep", None, None, None),
            P("shard", "rep", None, None),
            P("shard", None, None, None),
            P("shard", None, None),
        ),
        check_vma=False,
    )
```

```python
import functools
import math

import jax
import jax.numpy as jnp
import numpy as np
from jax import lax
from jax.experimental import pallas as pl
from jax.experimental.pallas import tpu as pltpu
from jax.sharding import PartitionSpec as P

HEAD_DIM = 64
F32 = jnp.float32
BF16 = jnp.bfloat16
EXACT = lax.Precision.HIGHEST
CLIP = 0.01
MOMENTUM = 0.9
RATE = 1000.0
SCALE = 2.0
AXES = ("rep", "shard")


def nn(a, b, precision=None):
    return lax.dot_general(
        a, b, (((1,), (0,)), ((), ())), precision=precision, preferred_element_type=F32
    )


def nt(a, b, precision=None):
    return lax.dot_general(
        a, b, (((1,), (1,)), ((), ())), precision=precision, preferred_element_type=F32
    )


def tn(a, b, precision=None):
    return lax.dot_general(
        a, b, (((0,), (0,)), ((), ())), precision=precision, preferred_element_type=F32
    )


def iota(shape, dim):
    return lax.broadcasted_iota(jnp.int32, shape, dim)


def lanes(x, low, high):
    at = iota(x.shape, x.ndim - 1)
    return jnp.where((at >= low) & (at < high), x, jnp.zeros_like(x))


def norm_parts(x):
    centered = x - jnp.mean(x, -1, keepdims=True)
    rstd = lax.rsqrt(jnp.mean(centered * centered, -1, keepdims=True) + 1e-05)
    return centered * rstd, rstd


def norm_back(grad, gain, unit, rstd):
    g = grad * gain
    return rstd * (
        g - jnp.mean(g, -1, keepdims=True) - unit * jnp.mean(g * unit, -1, keepdims=True)
    )


def load(pieces, spots, target, sems):
    copies = []
    for index, (piece, (row, column)) in enumerate(zip(pieces, spots, strict=True)):
        rows, columns = piece.shape
        if not isinstance(row, int):
            row = pl.multiple_of(row, rows)
        if not isinstance(column, int):
            column = pl.multiple_of(column, columns)
        place = target.at[pl.ds(row, rows), pl.ds(column, columns)]
        copies.append(pltpu.make_async_copy(piece, place, sems.at[index]))
    for copy in copies:
        copy.start()

    def wait():
        for copy in copies:
            copy.wait()

    return wait


def expand_heads(x, heads):
    rows, width = x.shape
    head_of = iota((rows, width), 1) // HEAD_DIM
    return jnp.concatenate(
        [jnp.where(head_of == h, x, jnp.zeros_like(x)) for h in range(heads)], 0
    )


def collapse_heads(x, heads):
    rows, width = x.shape[0] // heads, x.shape[1]
    head_of = iota((rows, width), 1) // HEAD_DIM
    total = jnp.zeros((rows, width), F32)
    for h in range(heads):
        total = total + jnp.where(head_of == h, x[h * rows : (h + 1) * rows], 0.0)
    return total


def column(row):
    return jnp.transpose(jnp.broadcast_to(row, (8, row.shape[1])))[:, :1]


def split_kernel(ready, d_t, f_t, head, live, qkv, out, up, down, left, right, up_part, down_part, sems):
    shard = lax.axis_index("shard")
    core = shard % 2
    rows, width = out.shape
    below = left.shape[0] - rows
    half = down_part.shape[0]
    blocks = up_part.shape[1] // half
    part = width // 2
    copies = []

    def move(piece, to):
        copies.append(pltpu.make_async_copy(piece, to, sems.at[len(copies)]))
        copies[-1].start()

    for j in range(4):
        at = pl.multiple_of(core * part, part)
        piece = out.at[:, pl.ds(at, part)] if j == 3 else qkv.at[:, pl.ds(at + j * width, part)]
        move(piece, (left, right)[j // 2].at[pl.ds(0, rows), pl.ds(j % 2 * part, part)])
    move(down.at[pl.ds(pl.multiple_of(core * half, half), half), :], down_part)
    for b in range(blocks):
        at = pl.multiple_of((2 * b + core) * half, half)
        move(up.at[:, pl.ds(at, half)], up_part.at[:, pl.ds(b * half, half)])
    ready()
    left[rows:, :] = jnp.zeros((below, width), BF16)
    right[rows:, :] = jnp.zeros((below, width), BF16)
    flat = jnp.concatenate([d_t[0], d_t[1]], 0).astype(BF16)
    count = flat.shape[0] // below
    for j in range(count):
        left[rows:, j * rows : (j + 1) * rows] = flat[j * below : (j + 1) * below]
    alive = jnp.sum((live[...] >= 0).astype(F32), keepdims=True)
    two = jnp.where(iota((below, rows), 0) == 0, head[...], alive)
    left[rows:, count * rows : (count + 1) * rows] = two.astype(BF16)
    right[rows:, : f_t.shape[1]] = f_t[...].astype(BF16)
    for copy in copies:
        copy.wait()


def assemble_kernel(column, ready, source, *refs):
    pieces, (mat, sems) = refs[:-2], refs[-2:]
    rep, core = lax.axis_index("rep"), lax.axis_index("shard") % 2
    rows, part = mat.shape[0] // len(pieces), mat.shape[1]
    tops = [piece.at[pl.ds(0, rows), pl.ds(column * part, part)] for piece in pieces]
    load(tops, [(source[rep, core, k] * rows, 0) for k in range(len(pieces))], mat, sems)()


def unpack_kernel(rank, rows, ready, source, *refs):
    pieces = refs[:-8]
    wide_d, own, other, head, count, flat, both, sems = refs[-8:]
    rep, core = lax.axis_index("rep"), lax.axis_index("shard") % 2
    n = len(pieces) // 2
    below, hidden = both.shape
    blocks = 10 * rank // below
    copies = []
    for k in range(n):
        r = source[rep, core, k]
        lanes_d = pl.ds(pl.multiple_of(r * rows, rows), rows)
        lanes_f = pl.ds(pl.multiple_of(r * (hidden // n), hidden // n), hidden // n)
        low = pl.ds(rows, below)
        for j in range(blocks + 1):
            place = flat.at[pl.ds(j * below, below), lanes_d]
            copies.append((pieces[k].at[low, pl.ds(j * rows, rows)], place))
        copies.append((pieces[n + k].at[low, pl.ds(0, hidden // n)], both.at[:, lanes_f]))
    copies = [pltpu.make_async_copy(a, b, sems.at[i]) for i, (a, b) in enumerate(copies)]
    for copy in copies:
        copy.start()
    for copy in copies:
        copy.wait()
    ready()
    wide_d[0] = flat[0 : 5 * rank, :]
    wide_d[1] = flat[5 * rank : 10 * rank, :]
    head[...] = flat[10 * rank : 10 * rank + 1, :].astype(F32)
    live = flat[10 * rank + 1 : 10 * rank + 2, :].astype(F32)
    count[...] = jnp.broadcast_to(jnp.sum(live, keepdims=True) / rows, count.shape)
    half = hidden // n // 2
    value = both[...]
    halves = [
        jnp.concatenate([value[:, (2 * r + c) * half : (2 * r + c + 1) * half] for r in range(n)], 1)
        for c in range(2)
    ]
    mine = (core == 0).astype(F32)
    zero, one = halves[0].astype(F32), halves[1].astype(F32)
    own[...] = (zero * mine + one * (1.0 - mine)).astype(BF16)
    other[...] = (zero * (1.0 - mine) + one * mine).astype(BF16)


def factors(ref, rank):
    value = ref[...]
    zero = jnp.zeros((4 * rank, value.shape[1]), value.dtype)
    return jnp.concatenate([zero, value[:rank]], 0), jnp.concatenate([zero, value[rank:]], 0)


def front_kernel(offset, ready, parts, pos_v, seg_v, table, gains, bias, h1, xl, hl, prow, tok):
    tokens, width = h1.shape
    slots = xl.shape[0]
    seq = (lax.axis_index("shard") + offset) % 2
    step = min(128, tokens)
    ready()
    position = pos_v[pl.ds(seq, 1), :]
    total = parts[0][...]
    for part in parts[1:]:
        total = total + part[...]
    tok[...] = total
    for i in range(tokens // step):
        rows = pl.ds(i * step, step)
        place = position[:, i * step : (i + 1) * step]
        onehot = (iota((tokens, step), 0) == place).astype(BF16)
        pos = tn(onehot, table[...])
        prow[rows, :] = pos.astype(BF16)
        unit, _ = norm_parts(tok[rows, :].astype(F32) + pos)
        h1[rows, :] = (unit * gains[0:1, :] + bias[0:1, :]).astype(BF16)
    segment = seg_v[pl.ds(seq, 1), :]
    after = pltpu.roll(jnp.broadcast_to(segment, (8, tokens)), tokens - 1, 1)[0:1]
    final = (segment != after) | (iota((1, tokens), 1) == tokens - 1)
    pick = ((segment == iota((slots, tokens), 0)) & final).astype(BF16)
    xl[...] = nn(pick, tok[...]) + nn(pick, prow[...])
    hl[...] = nn(pick, h1[...]).astype(BF16)


def kv_half(rank, h1, mat, at, u, ad, bias, kv):
    part = mat[0].shape[1]
    width = 2 * part
    cols = pl.ds(at, part)
    for j in range(2):
        to = pl.ds(pl.multiple_of(at + j * width, part), part)
        for b in range(len(h1)):
            total = nn(h1[b][...], mat[1 + j][...]) + bias[4 + j : 5 + j, cols]
            total = total + SCALE * nn(lanes(u[b], rank * (1 + j), rank * (2 + j)), ad[1, :, cols])
            kv[b, :, to] = total.astype(BF16)


def rows_kernel(micro, rank, ready, flush, *refs):
    seg_v, refs = refs[0], refs[1:]
    h1, hl, xl = refs[:micro], refs[micro : 2 * micro], refs[2 * micro : 3 * micro]
    ad, gains, bias = refs[3 * micro : 3 * micro + 3]
    mats = refs[3 * micro + 3 : 3 * micro + 11]
    kv, ukv_t, o, x1, q, p_t, u, w_out, e1, ukv = refs[3 * micro + 11 :]
    core = lax.axis_index("shard") % 2
    slots, width = hl[0].shape
    heads = width // HEAD_DIM
    tokens = h1[0].shape[0]
    part = width // 2
    places = [pl.multiple_of(core * part, part), pl.multiple_of((1 - core) * part, part)]
    mats = [(mats[:4], places[0]), (mats[4:], places[1])]
    ready(ad, *h1)
    down, up = ad[0], ad[1]
    for b in range(micro):
        ukv[b] = lanes(nt(h1[b][...], down).astype(BF16), rank, 3 * rank)
        ukv_t[b] = nt(down, h1[b][...]).astype(BF16)
    ready(*mats[0][0][1:3], bias)
    kv_half(rank, h1, *mats[0], ukv, ad, bias, kv)
    ready()
    kv_half(rank, h1, *mats[1], ukv, ad, bias, kv)
    flush(0)
    flush(1)
    for mat, at in mats:
        w_out[:, pl.ds(at, part)] = mat[3][...]
    flush(7)
    h_last = jnp.concatenate([h[...] for h in hl], 0)
    x_last = jnp.concatenate([x[...] for x in xl], 0)
    u_q = lanes(nt(h_last, down).astype(BF16), 0, rank)
    for mat, at in mats:
        cols = pl.ds(at, part)
        total = nn(h_last, mat[0][...]) + bias[3:4, cols] + SCALE * nn(u_q, ad[1, :, cols])
        q[:, cols] = total.astype(BF16)
    q_all = q[...]
    parts = []
    for b in range(micro):
        wide_q = expand_heads(q_all[b * slots : (b + 1) * slots], heads)
        scores = HEAD_DIM ** (-0.5) * nt(kv[b, :, :width], wide_q)
        segment = column(seg_v[pl.ds((core + b) % 2, 1), :])
        inside = segment == iota((tokens, heads * slots), 1) % slots
        scores = jnp.where(inside, scores, -1000000000.0)
        e = jnp.exp(scores - jnp.max(scores, 0, keepdims=True))
        probs = e / jnp.sum(e, 0, keepdims=True)
        p_t[b] = probs
        parts.append(collapse_heads(tn(probs.astype(BF16), kv[b, :, width:]), heads))
    flush(5)
    o_all = jnp.concatenate(parts, 0).astype(BF16)
    o[...] = o_all
    u_o = lanes(nt(o_all, down).astype(BF16), 3 * rank, 4 * rank)
    mid = x_last + nn(o_all, w_out[...]) + bias[6:7, :] + SCALE * nn(u_o, up)
    x1[...] = mid
    unit, _ = norm_parts(mid)
    h2 = (unit * gains[1:2, :] + bias[1:2, :]).astype(BF16)
    u_up = lanes(nt(h2, down).astype(BF16), 4 * rank, 5 * rank)
    e1[:, :width] = h2
    e1[:, width:] = jnp.zeros_like(e1[:, width:])
    e1[:, width : width + 5 * rank] = u_up
    u[...] = u_q + u_o + u_up


def preload_kernel(n, ready, source, _, *refs):
    w_up, w_down, sems = refs[-3:]
    rep, core = lax.axis_index("rep"), lax.axis_index("shard") % 2
    loads = []
    for index, wide in enumerate((w_up, w_down)):
        pieces = refs[index * n : (index + 1) * n]
        height = pieces[0].shape[0]
        spots = [(source[rep, core, k] * height, 0) for k in range(n)]
        loads.append(load(pieces, spots, wide, sems.at[index]))
    for wait in loads:
        wait()


def ffn_kernel(rank, last, ready, source, own, sib, f_own, f_sib, bias, *refs):
    up_last, down_last, _, _, f, a, w_up, w_down, mine, send, sems = refs
    width = w_up.shape[0]
    rep, core = lax.axis_index("rep"), lax.axis_index("shard") % 2
    loads = []
    for index, (piece, wide) in enumerate(((up_last, w_up), (down_last, w_down))):
        spots = [(source[rep, core, last] * piece.shape[0], 0)]
        loads.append(load([piece], spots, wide, sems.at[index]))
    ready()
    lane = 5 * rank
    rows = own.shape[0]
    h2 = jnp.concatenate([own[:, :width], sib[:, :width]], 0)
    pair_own, pair_sib = factors(f_own, rank), factors(f_sib, rank)
    extra = jnp.concatenate(
        [
            nn(own[:, width : width + lane], pair_own[1]),
            nn(sib[:, width : width + lane], pair_sib[1]),
        ],
        0,
    )
    loads[0]()
    total = nn(h2, w_up[...]) + bias[...] + SCALE * extra
    f[...] = total
    low = jax.nn.gelu(total, approximate=True).astype(BF16)
    a[...] = low
    for out, at, pair in ((mine, 0, pair_own), (send, rows, pair_sib)):
        out[:, width:] = jnp.zeros_like(out[:, width:])
        out[:, width : width + lane] = nt(low[at : at + rows], pair[0])
    loads[1]()
    y = nn(low, w_down[...])
    mine[:, :width] = y[:rows]
    send[:, :width] = y[rows:]


def score_kernel(rank, ready, x1, mine, recv, ad, gains, bias, head, x2, u_dn, score):
    ready()
    width = x1.shape[1]
    lane = 5 * rank
    u = (mine[:, width : width + lane] + recv[:, width : width + lane]).astype(BF16)
    u_dn[...] = u
    end = x1[...] + mine[:, :width] + recv[:, :width] + bias[11:12, :] + SCALE * nn(u, ad[1])
    x2[...] = end
    unit, _ = norm_parts(end)
    token = jnp.sum((unit * gains[2:3, :] + bias[2:3, :]) * head[...], -1, keepdims=True)
    score[...] = jnp.broadcast_to(token, score.shape)


def loss_kernel(rank, members, ready, *refs):
    scores = refs[:members]
    x2, u_dn, pairs, count, ad, gains, bias, head = refs[members : members + 8]
    e2, g_end, g_dn, small = refs[members + 8 :]
    ready()
    rows, width = x2.shape
    half = rows // 2

    def value(m):
        if m % 2 == 0:
            return scores[m][...]
        return jnp.concatenate([scores[m][half:, :], scores[m][:half, :]], 0)

    level = [value(m) for m in range(members)]
    while len(level) > 1:
        level = [level[i] + level[i + 1] for i in range(0, len(level), 2)]
    mean_reward = level[0][:, :1] / members
    at = iota((rows, pairs.shape[1]), 0)
    pick = (at == pairs[0:1, :]).astype(F32) - (at == pairs[1:2, :]).astype(F32)
    live = (pairs[0:1, :] >= 0).astype(F32)
    diff = jnp.sum(pick * mean_reward, 0, keepdims=True)
    terms = live * jax.nn.softplus(-diff)
    grad_diff = -live * jax.nn.sigmoid(-diff) / count[:, :1]
    grad_score = jnp.sum(pick * grad_diff, -1, keepdims=True) / members
    unit, rstd = norm_parts(x2[...])
    final = unit * gains[2:3, :] + bias[2:3, :]
    small[...] = jnp.zeros_like(small)
    small[0:1, :] = jnp.sum(final * grad_score, 0, keepdims=True)
    small[1:2, :] = jnp.broadcast_to(jnp.sum(terms, -1, keepdims=True), (1, width))
    end = norm_back(grad_score * head[...], gains[2:3, :], unit, rstd)
    g_end[...] = end
    g_ff = end.astype(BF16)
    left = lanes((SCALE * nt(g_ff, ad[1])).astype(BF16), 4 * rank, 5 * rank)
    g_dn[...] = SCALE * tn(u_dn[...], g_ff)
    e2[:, :width] = g_ff
    e2[:, width:] = jnp.zeros_like(e2[:, width:])
    e2[:, width : width + 5 * rank] = left


def slope_kernel(ready, f, _, out):
    x = f[...]
    c0, c1 = math.sqrt(2.0 / math.pi), 0.044715
    t = jnp.tanh(c0 * (x + c1 * x * x * x))
    out[...] = 0.5 * (1.0 + t) + 0.5 * x * (1.0 - t * t) * (c0 * (1.0 + 3.0 * c1 * x * x))


def ffn_back_kernel(rank, ready, own, sib, slope, f_own, f_sib, wide_u, wide_d,
                    mine, send, g_out):
    width = wide_u.shape[0]
    lane = 5 * rank
    ready()
    rows = own.shape[0]
    left_own, left_sib = own[:, width : width + lane], sib[:, width : width + lane]
    g_ff = jnp.concatenate([own[:, :width], sib[:, :width]], 0)
    pair_own, pair_sib = factors(f_own, rank), factors(f_sib, rank)
    extra = jnp.concatenate([nn(left_own, pair_own[0]), nn(left_sib, pair_sib[0])], 0)
    g_a = (nt(g_ff, wide_d[...]) + extra).astype(BF16)
    g_f = (g_a.astype(F32) * slope[...]).astype(BF16)
    g_h = nt(g_f, wide_u[...])
    for out, low, factor in ((mine, 0, pair_own), (send, rows, pair_sib)):
        out[:, :width] = g_h[low : low + rows]
        out[:, width:] = jnp.zeros_like(out[:, width:])
        out[:, width : width + lane] = SCALE * nt(g_f[low : low + rows], factor[1])
    g_out[...] = g_f


def hidden_kernel(rank, ready, own, sib, e1_own, e1_sib, a, g_f, mine, send):
    rows = own.shape[0]
    cut = slice(own.shape[1] - 128, own.shape[1] - 128 + 5 * rank)
    for out, low, left, u in ((mine, 0, own, e1_own), (send, rows, sib, e1_sib)):
        out[0:rank, :] = tn(left[:, cut], a[low : low + rows, :])[4 * rank :]
        out[rank:, :] = SCALE * tn(u[:, cut], g_f[low : low + rows, :])[4 * rank :]


def factor_kernel(rank, half, ready, mine, other, err, start, mat, left):
    ready()
    core = lax.axis_index("shard") % 2
    first = (core == 0).astype(F32)
    even = mine[...] * first + other[...] * (1.0 - first)
    odd = mine[...] * (1.0 - first) + other[...] * first
    parts = []
    for r in range(mine.shape[1] // half):
        cut = slice(r * half, (r + 1) * half)
        parts += [even[:, cut], odd[:, cut]]
    mat[...] = jnp.concatenate(parts, 1) + err[...]
    left[...] = nn(start[...], mat[...], EXACT)


def rows_back_kernel(micro, rank, ready, *refs):
    mine, recv, g_end, g_dn, small, x1, e1, u, o, q, p_t, kv, ukv_t = refs[:13]
    hl = refs[13 : 13 + micro]
    h1 = refs[13 + micro : 13 + 2 * micro]
    ad, gains, err, start, w_out, mat, left = refs[13 + 2 * micro :]
    ready(ad, gains)
    rows, width = x1.shape
    slots = rows // micro
    heads = width // HEAD_DIM
    lane = 5 * rank
    down, up = ad[0], ad[1]
    h2 = e1[:, :width]
    u_rows = u[...]
    g_u = (mine[:, width : width + lane] + recv[:, width : width + lane]).astype(BF16)
    g_h2 = (mine[:, :width] + recv[:, :width] + nn(g_u, down)).astype(BF16)
    grad_in = tn(g_u, h2)
    unit, rstd = norm_parts(x1[...])
    g_mid = g_end[...] + norm_back(g_h2.astype(F32), gains[1:2, :], unit, rstd)
    g_att = g_mid.astype(BF16)
    grad_out = g_dn[...] + SCALE * tn(lanes(u_rows, 3 * rank, 4 * rank), g_att)
    g_ol = lanes((SCALE * nt(g_att, up)).astype(BF16), 3 * rank, 4 * rank)
    grad_in = grad_in + tn(g_ol, o[...])
    g_o = (nt(g_att, w_out[...]) + nn(g_ol, down)).astype(BF16)
    ready()
    scale = HEAD_DIM ** (-0.5)

    both = (lane, 2 * heads * slots)
    group, side = iota(both, 0) // rank, iota(both, 1) // (heads * slots)
    keep = jnp.where(group == 1 + side, jnp.where(side == 0, scale, 1.0), 0.0)

    for b in range(micro):
        pick = slice(b * slots, (b + 1) * slots)
        wide_g = expand_heads(g_o[pick], heads)
        wide_q = expand_heads(q[pick, :], heads)
        probs = p_t[b]
        g_p = nt(kv[b, :, width:], wide_g)
        g_s = (probs * (g_p - jnp.sum(probs * g_p, 0, keepdims=True))).astype(BF16)
        g_q = (scale * collapse_heads(tn(g_s, kv[b, :, :width]), heads)).astype(BF16)
        u_q = lanes(u_rows[pick], 0, rank)
        tall = jnp.concatenate([g_s, probs.astype(BF16)], 1)
        flat = jnp.concatenate([wide_q, wide_g], 0)
        inner = (nn(ukv_t[b], tall) * keep).astype(BF16)
        grad_out = grad_out + SCALE * (tn(u_q, g_q) + nn(inner, flat))
        g_uq = lanes((SCALE * nt(g_q, up)).astype(BF16), 0, rank)
        inner = (nt(up, flat) * keep).astype(BF16)
        g_ukv = (SCALE * nt(inner, tall)).astype(BF16)
        grad_in = grad_in + tn(g_uq, hl[b][...]) + nn(g_ukv, h1[b][...])
    mat[0] = grad_in + err[0]
    mat[1] = grad_out + err[1]
    first = start.shape[1]
    left[0:first, :] = nn(start[0], mat[0], EXACT)
    left[first : 2 * first, :] = nn(start[1], mat[1], EXACT)
    left[2 * first :, :] = small[...]


def orthonormal_rows(refs):
    count = refs[0].shape[0]
    for k in range(count):
        for ref in refs:
            block = ref[...]
            row = block[k : k + 1, :]
            dots = jnp.sum(block * row, -1, keepdims=True)
            scale = lax.rsqrt(dots[k : k + 1] + 1e-06)
            row = row * scale
            at = iota(block.shape, 0)
            later = jnp.where(at > k, block - (dots * scale) * row, block)
            ref[...] = jnp.where(at == k, row, later)


def ortho_kernel(rank, ready, d_a, d_b, f_a, f_b, mat_d, mat_f, ph_d, ph_f, head, note):
    count = rank
    for j in range(2):
        part = slice(j * count, (j + 1) * count)
        ph_d[j] = d_a[part, :] + d_b[part, :]
    ph_f[...] = f_a[...] + f_b[...]
    rest = d_a[2 * count :, :] + d_b[2 * count :, :]
    refs = (ph_d.at[0], ph_d.at[1], ph_f)
    orthonormal_rows(refs)
    ready()
    grad = rest[0:1, :]
    head[...] = grad
    parts = []
    for ref, mat in zip(refs, (mat_d.at[0], mat_d.at[1], mat_f), strict=True):
        parts.append(nt(ref[...], mat[...], EXACT))
    for ref in refs:
        parts.append(nt(ref[...], ref[...], EXACT))
    parts.append(jnp.broadcast_to(jnp.sum(grad * grad, keepdims=True), (count, 1)))
    parts.append(jnp.broadcast_to(rest[1:2, :1], (count, 1)))
    used = sum(x.shape[1] for x in parts)
    parts.append(jnp.zeros((count, 128 - used), F32))
    own = jnp.concatenate(parts, 1)

    @pl.loop(0, note.shape[0])
    def _(i):
        note[i] = own


def final_kernel(rank, n, m, ready, notes, ph_d, ph_f, ph_do, ph_fo, ghead, mat_d, mat_f,
                 wd, wf, wh, md, mf, mh,
                 nd, nf, nh, nmd, nmf, nmh, err_d, err_f, q_d, q_f, mean_loss, norm):
    ready()
    shard = lax.axis_index("shard")
    count = rank
    sizes = (5 * rank, 5 * rank, 2 * rank)
    total = jnp.zeros((1, 1), F32)
    loss = jnp.zeros((1, 1), F32)
    own = jnp.zeros((count, 128), F32)
    for s in range(m):
        block = notes[s]
        for r in range(1, n):
            block = block + notes[r * m + s]
        own = jnp.where(shard == s, block, own)
        note = notes[s]
        at, gram = 0, sum(sizes)
        for size in sizes:
            right = block[:, at : at + size]
            inner = note[:, gram : gram + count]
            total = total + jnp.sum(right * nn(inner, right, EXACT), keepdims=True)
            at += size
            gram += count
        total = total + note[0:1, gram : gram + 1]
        loss = loss + note[0:1, gram + 1 : gram + 2]
    grad_norm = jnp.sqrt(total)
    clip = jnp.minimum(1.0, CLIP / (grad_norm + 1e-06))
    mean_loss[...] = loss / m
    norm[...] = grad_norm
    at = 0
    for j in range(2):
        right = own[:, at : at + sizes[j]]
        q_d[j] = right
        at += sizes[j]
        err_d[j] = mat_d[j] - tn(right, ph_d[j], EXACT) * (1.0 / n)
        fresh = MOMENTUM * md[j] + clip * tn(right, ph_do[j], EXACT)
        nmd[j] = fresh
        nd[j] = wd[j] - RATE * fresh
    right = own[:, at : at + sizes[2]]
    q_f[...] = right
    err_f[...] = mat_f[...] - tn(right, ph_f[...], EXACT) * (1.0 / n)
    fresh = MOMENTUM * mf[...] + clip * tn(right, ph_fo[...], EXACT)
    nmf[...] = fresh
    nf[...] = wf[...] - RATE * fresh
    fresh = MOMENTUM * mh[...] + clip * ghead[...]
    nmh[...] = fresh
    nh[...] = wh[...] - RATE * fresh


class Raw:
    def __init__(self, array):
        self.array = array


class Scalars(Raw):
    pass


class Far(Raw):
    pass


class Fresh(Raw):
    pass


class Part:
    def __init__(self, array, rows):
        self.array, self.rows = array, rows


class Kept:
    def __init__(self, shape, dtype):
        self.shape, self.dtype = tuple(shape), dtype


class Placed(Kept):
    pass


def call(body, outs, args, scratch=(), vmem=60, name=None, groups=None, aliases=None, flushes=False):
    arrays, specs, staged = [], [], []
    for arg in args:
        arrays.append(arg.array if isinstance(arg, Raw | Part) else arg)
        space = pl.ANY
        if isinstance(arg, Scalars):
            space = pltpu.SMEM
        elif isinstance(arg, Fresh):
            space = pltpu.VMEM
        elif isinstance(arg, Far):
            space = pltpu.HBM
        specs.append(pl.BlockSpec(memory_space=space))
        if isinstance(arg, Part):
            staged.append(pltpu.VMEM((arg.rows, *arg.array.shape[1:]), arg.array.dtype))
        elif not isinstance(arg, Raw):
            staged.append(pltpu.VMEM(arg.shape, arg.dtype))
    results = [pltpu.VMEM(o.shape, o.dtype) for o in outs if not isinstance(o, Kept)]

    def kernel(*refs):
        ins, refs = refs[: len(args)], refs[len(args) :]
        targets, refs = refs[: len(outs)], refs[len(outs) :]
        held, refs = refs[: len(staged)], refs[len(staged) :]
        buffers, refs = refs[: len(results)], refs[len(results) :]
        extra, sems = refs[:-1], refs[-1]
        copies, given, i = {}, [], 0
        for arg, ref in zip(args, ins, strict=True):
            if isinstance(arg, Raw):
                given.append(ref)
                continue
            origin = ref.at[pl.ds(0, arg.rows)] if isinstance(arg, Part) else ref
            copies[id(held[i])] = pltpu.make_async_copy(origin, held[i], sems.at[i])
            given.append(held[i])
            i += 1
        for copy in copies.values():
            copy.start()

        def ready(*some):
            for key in [id(r) for r in some] or list(copies):
                copies.pop(key).wait()

        local, back, i = [], {}, 0
        for j, out in enumerate(outs):
            if isinstance(out, Kept):
                local.append(targets[j])
                continue
            local.append(buffers[i])
            back[j] = pltpu.make_async_copy(buffers[i], targets[j], sems.at[len(staged) + i])
            i += 1
        def flush(j):
            back[j].start()
            begun.append(j)

        begun = []
        if groups:
            given = [given[:groups], *given[groups:]]
        body(ready, *((flush,) if flushes else ()), *given, *local, *extra)
        for j, copy in back.items():
            if j not in begun:
                copy.start()
        for copy in back.values():
            copy.wait()

    def place(out):
        if type(out) is Kept:
            return pltpu.VMEM
        return pl.ANY if isinstance(out, Kept) else pltpu.HBM

    return pl.pallas_call(
        kernel,
        out_shape=tuple(jax.ShapeDtypeStruct(o.shape, o.dtype) for o in outs),
        in_specs=specs,
        out_specs=tuple(pl.BlockSpec(memory_space=place(o)) for o in outs),
        scratch_shapes=[
            *staged, *results, *scratch, pltpu.SemaphoreType.DMA((max(1, len(staged) + len(results)),)),
        ],
        compiler_params=pltpu.CompilerParams(vmem_limit_bytes=vmem << 20),
        cost_estimate=pl.CostEstimate(flops=0, bytes_accessed=0, transcendentals=0),
        input_output_aliases=aliases or {},
        name=name,
    )(*arrays)


def shaped(shape, dtype):
    return jax.ShapeDtypeStruct(tuple(shape), dtype)


def ring_order(count):
    side = math.isqrt(count // 2)
    if side < 2 or 2 * side * side != count:
        return list(range(count))
    depth = 2 * side
    cells = []
    for z in range(depth):
        ys = range(1, side) if z % 2 == 0 else range(side - 1, 0, -1)
        cells += [(z, y) for y in ys]
    cells += [(z, 0) for z in range(depth - 1, -1, -1)]
    return [z * side + y for z, y in cells]


def pairs_of(n, m, move):
    return [(r * m + s, t[0] * m + t[1]) for r in range(n) for s in range(m) for t in [move(r, s)]]


def on_device(n, m, *args):
    (
        token_ids, positions, segment_ids, pair_index, embed_table, pos_table,
        base_qkv, base_out, base_up, base_down, base_gains, base_bias,
        adapt_d, adapt_f, head, mom_d, mom_f, mom_head, err_d, err_f, qstart_d, qstart_f,
    ) = args
    micro, tokens = token_ids.shape
    held, width = embed_table.shape
    pairs = pair_index.shape[1]
    slots = 2 * pairs
    rows = micro * slots
    hidden = base_up.shape[1]
    rank = adapt_f.shape[2] // 2
    heads = width // HEAD_DIM
    rd, rf = base_up.shape[0], base_down.shape[0]
    half = rf // 2
    own_hidden = hidden // 2
    rep, shard = lax.axis_index("rep"), lax.axis_index("shard")
    core = shard % 2

    order = ring_order(n)
    place = {r: i for i, r in enumerate(order)}
    around = pairs_of(
        n, m, lambda r, s: (order[(place[r] + (1 if s % 2 == 0 else -1)) % n], s)
    )
    turns = [
        [[order[(place[r] + (-k if c == 0 else k)) % n] for k in range(n)] for c in range(2)]
        for r in range(n)
    ]
    source = Scalars(jnp.asarray(np.array(turns, np.int32)))

    def send(x, perm):
        return lax.ppermute(x, AXES, perm)

    def across(x, mask):
        return send(x, pairs_of(n, m, lambda r, s: (r, s ^ mask)))

    def ring(x):
        out = []
        for _ in range(n - 1):
            x = send(x, around)
            out.append(x)
        return out

    def pick(x, index, axis):
        return lax.dynamic_index_in_dim(x, index, axis, keepdims=False)

    d_t = adapt_d[0].transpose(1, 2, 0)
    f_t = adapt_f[0].T
    below = 2 * rank
    live = pair_index[..., 0].reshape(1, micro * pairs)
    whole_blocks = rd % 128 == 0 and half % 128 == 0
    if whole_blocks:
        left, right, up_part, down_part = call(
            split_kernel,
            [shaped((rd + below, width), BF16), shaped((rd + below, width), BF16),
             shaped((rd, own_hidden), BF16), shaped((half, width), BF16)],
            [d_t, f_t, head, live, Raw(base_qkv), Raw(base_out), Raw(base_up), Raw(base_down)],
            [pltpu.SemaphoreType.DMA((n + 5,))],
            vmem=56, name="split",
        )
    else:
        two = jnp.concatenate([head, jnp.broadcast_to(jnp.sum((live >= 0).astype(F32)), (below - 1, rd))], 0)
        flat = [x for x in d_t.reshape(10 * rank // below, below, rd)]
        first = jnp.concatenate([base_qkv, base_out], 1).reshape(rd, 4, 2, width // 2)
        first = pick(first, core, 2).reshape(rd, 2, width)
        sides = []
        for side, extra in enumerate((jnp.concatenate([*flat, two], 1), f_t)):
            extra = jnp.pad(extra.astype(BF16), ((0, 0), (0, width - extra.shape[1])))
            sides.append(jnp.concatenate([first[:, side], extra], 0))
        left, right = sides
        up_part = pick(base_up.reshape(rd, n, 2, half), core, 2).reshape(rd, own_hidden)
        down_part = pick(base_down.reshape(2, half, width), core, 0)

    def after(x, *others):
        return pl.pallas_call(
            lambda *refs: None,
            out_shape=jax.ShapeDtypeStruct(x.shape, x.dtype),
            in_specs=[pl.BlockSpec(memory_space=pl.ANY)] * (1 + len(others)),
            out_specs=pl.BlockSpec(memory_space=pl.ANY),
            input_output_aliases={0: 0},
            cost_estimate=pl.CostEstimate(flops=0, bytes_accessed=0, transcendentals=0),
            name="after",
        )(x, *others)

    def lookup(*start):
        ids = jnp.stack([pick(token_ids, (core + b) % micro, 0) for b in range(micro)])
        near = ids - shard * held
        inside = (near >= 0) & (near < held)
        found = jnp.take(embed_table, after(jnp.clip(near, 0, held - 1), *start), axis=0)
        found = jnp.where(inside[..., None], found, jnp.zeros_like(found))
        return found[0], found[1]

    def shared(own, given, *others):
        own = own + across(after(given, *others), 1)
        mask = 2
        while mask < m // 2:
            own = own + across(own, mask)
            mask *= 2
        return own, across(own, mask) if m > 2 else own

    bias = base_bias.reshape(-1, width)
    bias_1 = pick(base_bias[7 * width : 7 * width + hidden].reshape(n, 2, half), core, 1)
    bias_1 = bias_1.reshape(1, own_hidden)
    local = (jnp.arange(micro) + core) % micro * slots
    pair_rows = jnp.where(pair_index >= 0, pair_index + local[:, None, None], -1)
    pair_rows = pair_rows.reshape(micro * pairs, 2).T

    pos_rows = pos_table[:tokens]

    lefts, rights, ups, downs = [left], [right], [up_part], [down_part]

    def behind(low, high, *gate):
        for k in range(low, min(high, n)):
            if gate:
                ups[-1], downs[-1] = after(ups[-1], *gate), after(downs[-1], *gate)
            gate = ()
            ups.append(send(ups[-1], around))
            downs.append(send(downs[-1], around))

    for k in range(1, n):
        gate = []
        if k == 9:
            gate = [ups[1], downs[1]]
        if k == 4:
            gate = [tok_own, bias, bias_1, pos_rows, pair_rows]
        if k == 9:
            gate = [tok_far]
        if gate:
            lefts[-1], rights[-1] = after(lefts[-1], *gate), after(rights[-1], *gate)
        lefts.append(send(lefts[-1], around))
        rights.append(send(rights[-1], around))
        if k == 1:
            ups[-1], downs[-1] = ups[-1], downs[-1]
            ups.append(send(ups[-1], around))
            downs.append(send(downs[-1], around))
            own, given = lookup(left)
        if k == 1:
            tok_own, tok_far = shared(own, given, lefts[1], rights[1], ups[1], downs[1])

    parts = [tok_own, tok_far] if m > 2 else [tok_own]
    both = tok_own + tok_far if m > 2 else tok_own
    toks = [parts, [across(both, 1)]]

    step_a = [*lefts, *rights]
    if whole_blocks:
        mats = []
        for k in range(4):
            mats += call(
                functools.partial(assemble_kernel, k % 2),
                [shaped((width, width // 2), BF16)],
                [source, *[Far(x) for x in (lefts, rights)[k // 2]]],
                [pltpu.SemaphoreType.DMA((n,))],
                vmem=8, name="assemble",
            )
        wide_d, f_own, f_other, wide_head, count_row = call(
            functools.partial(unpack_kernel, rank, rd),
            [shaped((2, 5 * rank, width), BF16), shaped((2 * rank, own_hidden), BF16),
             Kept((2 * rank, own_hidden), BF16), shaped((1, width), F32), shaped((1, 128), F32)],
            [source, *[Far(x) for x in step_a]],
            [pltpu.VMEM((10 * rank + below, width), BF16), pltpu.VMEM((below, hidden), BF16),
             pltpu.SemaphoreType.DMA((n * (10 * rank // below + 2),))],
            vmem=52, name="unpack",
        )
    else:
        turned = jnp.asarray(np.argsort(np.array(turns, np.int32), -1).astype(np.int32))
        place_at = lax.dynamic_slice(turned, (rep, core, 0), (1, 1, n)).reshape(n)
        steps_l, steps_r = [
            jnp.stack([pick(jnp.stack(x), place_at[r], 0) for r in range(n)]) for x in (lefts, rights)
        ]
        mats = [x[:, :rd].reshape(width, 2, width // 2) for x in (steps_l, steps_r)]
        mats = [x[:, j] for x in mats for j in range(2)]
        count_d = 10 * rank // below
        wide_d = steps_l[:, rd:, : count_d * rd].reshape(n, below, count_d, rd)
        wide_d = wide_d.transpose(2, 1, 0, 3).reshape(2, 5 * rank, width)
        wide_f = steps_r[:, rd:, :rf].reshape(n, 2 * rank, 2, half)
        wide_f = wide_f.transpose(2, 1, 0, 3).reshape(2, 2 * rank, own_hidden)
        f_own, f_other = pick(wide_f, core, 0), pick(wide_f, 1 - core, 0)
        last = steps_l[:, rd:, count_d * rd : (count_d + 1) * rd].astype(F32)
        wide_head = last[:, 0].reshape(1, width)
        count_row = jnp.broadcast_to(jnp.sum(last[:, 1, 0]), (1, 128))
    count = count_row[0, 0]
    f_sib = across(f_other, 1)
    mats += [across(x, 1) for x in mats]

    h1, xl, hl = [], [], []
    for b in range(micro):
        a, x, h = call(
            functools.partial(front_kernel, b),
            [Kept((tokens, width), BF16), Kept((slots, width), F32), Kept((slots, width), BF16)],
            [*toks[b], positions, segment_ids, pos_rows, base_gains, bias],
            [pltpu.VMEM((tokens, width), BF16), pltpu.VMEM((tokens, width), BF16)],
            groups=len(toks[b]), vmem=14, name="front",
        )
        h1.append(a)
        xl.append(x)
        hl.append(h)

    behind(2, 3, lefts[5])
    behind(3, 4, *mats[:2])
    behind(4, 5, *mats[2:4], hl[0])
    behind(5, 6, hl[1], wide_d)
    behind(6, 7)
    kv, ukv_t, o, x1, q, p_t, u, w_out, e1 = call(
        functools.partial(rows_kernel, micro, rank),
        [shaped((micro, tokens, 2 * width), BF16), shaped((micro, 5 * rank, tokens), BF16),
         shaped((rows, width), BF16), shaped((rows, width), F32), shaped((rows, width), BF16),
         shaped((micro, tokens, heads * slots), F32), shaped((rows, 5 * rank), BF16),
         shaped((width, width), BF16), shaped((rows, width + 128), BF16)],
        [segment_ids, *h1, *hl, *xl, wide_d, base_gains, bias, *mats],
        [pltpu.VMEM((micro, tokens, 5 * rank), BF16)],
        vmem=60, flushes=True, name="rows",
    )
    behind(7, n, o)
    ups, downs = [[Far(y) for y in x] for x in (ups, downs)]
    e1_sib = across(e1, 1)
    w_up, w_down = call(
        functools.partial(preload_kernel, n - 1),
        [Kept((width, own_hidden), BF16), Kept((own_hidden, width), BF16)],
        [source, Raw(o), *ups[:-1], *downs[:-1]],
        [pltpu.SemaphoreType.DMA((2, n - 1))],
        vmem=4, name="preload",
    )
    f, a, w_up, w_down, y_mine, y_send = call(
        functools.partial(ffn_kernel, rank, n - 1),
        [Kept((2 * rows, own_hidden), F32), Kept((2 * rows, own_hidden), BF16),
         Kept((width, own_hidden), BF16), Kept((own_hidden, width), BF16)]
        + [Kept((rows, width + 128), F32)] * 2,
        [source, Fresh(e1), Fresh(e1_sib), f_own, f_sib, bias_1, ups[-1], downs[-1], Fresh(w_up), Fresh(w_down)],
        [pltpu.SemaphoreType.DMA((2, 1))],
        aliases={8: 2, 9: 3}, vmem=10, name="ffn",
    )
    x2, u_dn, score = call(
        functools.partial(score_kernel, rank),
        [Kept((rows, width), F32), Kept((rows, 5 * rank), BF16), Kept((rows, 128), F32)],
        [Fresh(x1), Fresh(y_mine), Fresh(across(y_send, 1)), wide_d, base_gains, bias, wide_head],
        vmem=10, name="score",
    )
    scores = [score] + [across(score, k) for k in range(1, m)]
    (slope,) = call(
        slope_kernel,
        [Kept((2 * rows, own_hidden), F32)],
        [Fresh(f), Fresh(score)],
        vmem=6, name="slope",
    )
    e2, g_end, g_dn, small = call(
        functools.partial(loss_kernel, rank, m),
        [Kept((rows, width + 128), BF16), Kept((rows, width), F32), Kept((5 * rank, width), F32),
         Kept((8, width), F32)],
        [*[Fresh(x) for x in scores], Fresh(x2), Fresh(u_dn), pair_rows, count_row, wide_d, base_gains, bias, wide_head],
        vmem=10, name="loss",
    )
    e2_sib = across(e2, 1)
    y_mine, y_send, g_f = call(
        functools.partial(ffn_back_kernel, rank),
        [Kept((rows, width + 128), F32)] * 2 + [Kept((2 * rows, own_hidden), BF16)],
        [Fresh(e2), Fresh(e2_sib), Fresh(slope), f_own, f_sib,
         Fresh(w_up), Fresh(w_down)],
        vmem=14, name="ffn_back",
    )
    y_other = across(y_send, 1)
    gf_mine, gf_send = call(
        functools.partial(hidden_kernel, rank),
        [Kept((2 * rank, own_hidden), F32)] * 2,
        [Fresh(x) for x in (e2, e2_sib, e1, e1_sib, a, g_f)],
        vmem=6, name="hidden",
    )
    mat_f, left_f = call(
        functools.partial(factor_kernel, rank, half),
        [Kept((2 * rank, hidden), F32), Kept((rank, hidden), F32)],
        [Fresh(gf_mine), Fresh(across(gf_send, 1)), err_f[0, 0].T, qstart_f[0].T],
        vmem=10, name="factor_f",
    )
    mat_d, left_d = call(
        functools.partial(rows_back_kernel, micro, rank),
        [Kept((2, 5 * rank, width), F32), Kept((2 * rank + 8, width), F32)],
        [Fresh(y_mine), Fresh(y_other), Fresh(g_end), Fresh(g_dn), Fresh(small),
         *[Fresh(x) for x in (x1, e1, u, o, q, p_t, kv, ukv_t, *hl, *h1)],
         wide_d, base_gains, err_d[0, 0].transpose(1, 2, 0), qstart_d[0].transpose(0, 2, 1), Fresh(w_out)],
        vmem=26, name="rows_back",
    )

    def rep_parts(x, order):
        part = jnp.zeros_like(x)
        bits = [1 << k for k in range(n.bit_length() - 1)][::order]
        for bit in bits:
            part = send(x, pairs_of(n, m, lambda r, s, bit=bit: (r ^ bit, s)))
            if bit != bits[-1]:
                x = x + part
        return Fresh(x), Fresh(part)

    ph_d, ph_f, total_head, note = call(
        functools.partial(ortho_kernel, rank),
        [Kept((2, rank, width), F32), Kept((rank, hidden), F32), Kept((1, width), F32),
         Kept((n * m, rank, 128), F32)],
        [*rep_parts(left_d, 1), *rep_parts(left_f, -1), Fresh(mat_d), Fresh(mat_f)],
        vmem=10, name="ortho",
    )
    notes = lax.all_to_all(note, AXES, 0, 0)
    own_ph_d = lax.dynamic_slice_in_dim(ph_d, rep * rd, rd, 2)
    own_ph_f = lax.dynamic_slice_in_dim(ph_f, rep * rf, rf, 1)
    own_head = lax.dynamic_slice_in_dim(total_head, rep * rd, rd, 1)
    nd, nf, nh, nmd, nmf, nmh, new_err_d, new_err_f, q_d, q_f, loss_sum, norm = call(
        functools.partial(final_kernel, rank, n, m),
        [shaped((2, 5 * rank, rd), F32), shaped((2 * rank, rf), F32), shaped((1, rd), F32)] * 2
        + [shaped((2, 5 * rank, width), F32), shaped((2 * rank, hidden), F32),
           shaped((2, rank, 5 * rank), F32), shaped((rank, 2 * rank), F32), shaped((1, 1), F32), shaped((1, 1), F32)],
        [Fresh(notes), Fresh(ph_d), Fresh(ph_f), Fresh(own_ph_d), Fresh(own_ph_f), Fresh(own_head),
         Fresh(mat_d), Fresh(mat_f), d_t, f_t, head, mom_d[0].transpose(1, 2, 0), mom_f[0].T, mom_head],
        vmem=16, name="final",
    )
    return (
        loss_sum[0, 0],
        count,
        norm[0, 0],
        nd.transpose(2, 0, 1)[None],
        nf.T[None],
        nh,
        nmd.transpose(2, 0, 1)[None],
        nmf.T[None],
        nmh,
        new_err_d.transpose(2, 0, 1)[None, None],
        new_err_f.T[None, None],
        q_d.transpose(0, 2, 1)[None],
        q_f.T[None],
    )


def solution(mesh):
    n, m = mesh.shape["rep"], mesh.shape["shard"]
    return jax.shard_map(
        functools.partial(on_device, n, m),
        mesh=mesh,
        in_specs=(
            P("rep", None),
            P("rep", None),
            P("rep", None),
            P("rep", None, None),
            P("shard", None),
            P(),
            P("rep", None),
            P("rep", None),
            P("rep", None),
            P("rep", None),
            P(),
            P(),
            P("shard", "rep", None, None),
            P("shard", "rep", None),
            P("shard", "rep"),
            P("shard", "rep", None, None),
            P("shard", "rep", None),
            P("shard", "rep"),
            P("shard", "rep", None, None, None),
            P("shard", "rep", None, None),
            P("shard", None, None, None),
            P("shard", None, None),
        ),
        out_specs=(
            P(),
            P(),
            P(),
            P("shard", "rep", None, None),
            P("shard", "rep", None),
            P("shard", "rep"),
            P("shard", "rep", None, None),
            P("shard", "rep", None),
            P("shard", "rep"),
            P("shard", "rep", None, None, None),
            P("shard", "rep", None, None),
            P("shard", None, None, None),
            P("shard", None, None),
        ),
        check_vma=False,
    )
```

```python
import functools
import math

import jax
import jax.numpy as jnp
import numpy as np
from jax import lax
from jax.experimental import pallas as pl
from jax.experimental.pallas import tpu as pltpu
from jax.sharding import PartitionSpec as P

HEAD_DIM = 64
F32 = jnp.float32
BF16 = jnp.bfloat16
EXACT = lax.Precision.HIGHEST
CLIP = 0.01
MOMENTUM = 0.9
RATE = 1000.0
SCALE = 2.0
AXES = ("rep", "shard")


def nn(a, b, precision=None):
    return lax.dot_general(
        a, b, (((1,), (0,)), ((), ())), precision=precision, preferred_element_type=F32
    )


def nt(a, b, precision=None):
    return lax.dot_general(
        a, b, (((1,), (1,)), ((), ())), precision=precision, preferred_element_type=F32
    )


def tn(a, b, precision=None):
    return lax.dot_general(
        a, b, (((0,), (0,)), ((), ())), precision=precision, preferred_element_type=F32
    )


def iota(shape, dim):
    return lax.broadcasted_iota(jnp.int32, shape, dim)


def lanes(x, low, high):
    at = iota(x.shape, x.ndim - 1)
    return jnp.where((at >= low) & (at < high), x, jnp.zeros_like(x))


def norm_parts(x):
    centered = x - jnp.mean(x, -1, keepdims=True)
    rstd = lax.rsqrt(jnp.mean(centered * centered, -1, keepdims=True) + 1e-05)
    return centered * rstd, rstd


def norm_back(grad, gain, unit, rstd):
    g = grad * gain
    return rstd * (
        g - jnp.mean(g, -1, keepdims=True) - unit * jnp.mean(g * unit, -1, keepdims=True)
    )


def load(pieces, spots, target, sems):
    copies = []
    for index, (piece, (row, column)) in enumerate(zip(pieces, spots, strict=True)):
        rows, columns = piece.shape
        if not isinstance(row, int):
            row = pl.multiple_of(row, rows)
        if not isinstance(column, int):
            column = pl.multiple_of(column, columns)
        place = target.at[pl.ds(row, rows), pl.ds(column, columns)]
        copies.append(pltpu.make_async_copy(piece, place, sems.at[index]))
    for copy in copies:
        copy.start()

    def wait():
        for copy in copies:
            copy.wait()

    return wait


def expand_heads(x, heads):
    rows, width = x.shape
    head_of = iota((rows, width), 1) // HEAD_DIM
    return jnp.concatenate(
        [jnp.where(head_of == h, x, jnp.zeros_like(x)) for h in range(heads)], 0
    )


def collapse_heads(x, heads):
    rows, width = x.shape[0] // heads, x.shape[1]
    head_of = iota((rows, width), 1) // HEAD_DIM
    total = jnp.zeros((rows, width), F32)
    for h in range(heads):
        total = total + jnp.where(head_of == h, x[h * rows : (h + 1) * rows], 0.0)
    return total


def column(row):
    return jnp.transpose(jnp.broadcast_to(row, (8, row.shape[1])))[:, :1]


def split_kernel(ready, d_t, f_t, head, live, qkv, out, up, down, left, right, up_part, down_part, sems):
    shard = lax.axis_index("shard")
    core = shard % 2
    rows, width = out.shape
    below = left.shape[0] - rows
    half = down_part.shape[0]
    blocks = up_part.shape[1] // half
    part = width // 2
    copies = []

    def move(piece, to):
        copies.append(pltpu.make_async_copy(piece, to, sems.at[len(copies)]))
        copies[-1].start()

    for j in range(4):
        at = pl.multiple_of(core * part, part)
        piece = out.at[:, pl.ds(at, part)] if j == 3 else qkv.at[:, pl.ds(at + j * width, part)]
        move(piece, (left, right)[j // 2].at[pl.ds(0, rows), pl.ds(j % 2 * part, part)])
    move(down.at[pl.ds(pl.multiple_of(core * half, half), half), :], down_part)
    for b in range(blocks):
        at = pl.multiple_of((2 * b + core) * half, half)
        move(up.at[:, pl.ds(at, half)], up_part.at[:, pl.ds(b * half, half)])
    ready()
    left[rows:, :] = jnp.zeros((below, width), BF16)
    right[rows:, :] = jnp.zeros((below, width), BF16)
    flat = jnp.concatenate([d_t[0], d_t[1]], 0).astype(BF16)
    count = flat.shape[0] // below
    for j in range(count):
        left[rows:, j * rows : (j + 1) * rows] = flat[j * below : (j + 1) * below]
    alive = jnp.sum((live[...] >= 0).astype(F32), keepdims=True)
    two = jnp.where(iota((below, rows), 0) == 0, head[...], alive)
    left[rows:, count * rows : (count + 1) * rows] = two.astype(BF16)
    right[rows:, : f_t.shape[1]] = f_t[...].astype(BF16)
    for copy in copies:
        copy.wait()


def assemble_kernel(column, ready, source, *refs):
    pieces, (mat, sems) = refs[:-2], refs[-2:]
    rep, core = lax.axis_index("rep"), lax.axis_index("shard") % 2
    rows, part = mat.shape[0] // len(pieces), mat.shape[1]
    tops = [piece.at[pl.ds(0, rows), pl.ds(column * part, part)] for piece in pieces]
    load(tops, [(source[rep, core, k] * rows, 0) for k in range(len(pieces))], mat, sems)()


def unpack_kernel(rank, rows, ready, source, *refs):
    pieces = refs[:-8]
    wide_d, own, other, head, count, flat, both, sems = refs[-8:]
    rep, core = lax.axis_index("rep"), lax.axis_index("shard") % 2
    n = len(pieces) // 2
    below, hidden = both.shape
    blocks = 10 * rank // below
    copies = []
    for k in range(n):
        r = source[rep, core, k]
        lanes_d = pl.ds(pl.multiple_of(r * rows, rows), rows)
        lanes_f = pl.ds(pl.multiple_of(r * (hidden // n), hidden // n), hidden // n)
        low = pl.ds(rows, below)
        for j in range(blocks + 1):
            place = flat.at[pl.ds(j * below, below), lanes_d]
            copies.append((pieces[k].at[low, pl.ds(j * rows, rows)], place))
        copies.append((pieces[n + k].at[low, pl.ds(0, hidden // n)], both.at[:, lanes_f]))
    copies = [pltpu.make_async_copy(a, b, sems.at[i]) for i, (a, b) in enumerate(copies)]
    for copy in copies:
        copy.start()
    for copy in copies:
        copy.wait()
    ready()
    wide_d[0] = flat[0 : 5 * rank, :]
    wide_d[1] = flat[5 * rank : 10 * rank, :]
    head[...] = flat[10 * rank : 10 * rank + 1, :].astype(F32)
    live = flat[10 * rank + 1 : 10 * rank + 2, :].astype(F32)
    count[...] = jnp.broadcast_to(jnp.sum(live, keepdims=True) / rows, count.shape)
    half = hidden // n // 2
    value = both[...]
    halves = [
        jnp.concatenate([value[:, (2 * r + c) * half : (2 * r + c + 1) * half] for r in range(n)], 1)
        for c in range(2)
    ]
    mine = (core == 0).astype(F32)
    zero, one = halves[0].astype(F32), halves[1].astype(F32)
    own[...] = (zero * mine + one * (1.0 - mine)).astype(BF16)
    other[...] = (zero * (1.0 - mine) + one * mine).astype(BF16)


def factors(ref, rank):
    value = ref[...]
    zero = jnp.zeros((4 * rank, value.shape[1]), value.dtype)
    return jnp.concatenate([zero, value[:rank]], 0), jnp.concatenate([zero, value[rank:]], 0)


def front_kernel(offset, ready, parts, pos_v, seg_v, table, gains, bias, h1, xl, hl, prow, tok):
    tokens, width = h1.shape
    slots = xl.shape[0]
    seq = (lax.axis_index("shard") + offset) % 2
    step = min(128, tokens)
    ready()
    position = pos_v[pl.ds(seq, 1), :]
    total = parts[0][...]
    for part in parts[1:]:
        total = total + part[...]
    tok[...] = total
    for i in range(tokens // step):
        rows = pl.ds(i * step, step)
        place = position[:, i * step : (i + 1) * step]
        onehot = (iota((tokens, step), 0) == place).astype(BF16)
        pos = tn(onehot, table[...])
        prow[rows, :] = pos.astype(BF16)
        unit, _ = norm_parts(tok[rows, :].astype(F32) + pos)
        h1[rows, :] = (unit * gains[0:1, :] + bias[0:1, :]).astype(BF16)
    segment = seg_v[pl.ds(seq, 1), :]
    after = pltpu.roll(jnp.broadcast_to(segment, (8, tokens)), tokens - 1, 1)[0:1]
    final = (segment != after) | (iota((1, tokens), 1) == tokens - 1)
    pick = ((segment == iota((slots, tokens), 0)) & final).astype(BF16)
    xl[...] = nn(pick, tok[...]) + nn(pick, prow[...])
    hl[...] = nn(pick, h1[...]).astype(BF16)


def kv_half(rank, h1, mat, at, u, ad, bias, kv):
    part = mat[0].shape[1]
    width = 2 * part
    cols = pl.ds(at, part)
    for j in range(2):
        to = pl.ds(pl.multiple_of(at + j * width, part), part)
        for b in range(len(h1)):
            total = nn(h1[b][...], mat[1 + j][...]) + bias[4 + j : 5 + j, cols]
            total = total + SCALE * nn(lanes(u[b], rank * (1 + j), rank * (2 + j)), ad[1, :, cols])
            kv[b, :, to] = total.astype(BF16)


def rows_kernel(micro, rank, ready, flush, *refs):
    seg_v, refs = refs[0], refs[1:]
    h1, hl, xl = refs[:micro], refs[micro : 2 * micro], refs[2 * micro : 3 * micro]
    ad, gains, bias = refs[3 * micro : 3 * micro + 3]
    mats = refs[3 * micro + 3 : 3 * micro + 11]
    kv, ukv_t, o, x1, q, p_t, u, w_out, e1, ukv = refs[3 * micro + 11 :]
    core = lax.axis_index("shard") % 2
    slots, width = hl[0].shape
    heads = width // HEAD_DIM
    tokens = h1[0].shape[0]
    part = width // 2
    places = [pl.multiple_of(core * part, part), pl.multiple_of((1 - core) * part, part)]
    mats = [(mats[:4], places[0]), (mats[4:], places[1])]
    ready(ad, *h1)
    down, up = ad[0], ad[1]
    for b in range(micro):
        ukv[b] = lanes(nt(h1[b][...], down).astype(BF16), rank, 3 * rank)
        ukv_t[b] = nt(down, h1[b][...]).astype(BF16)
    ready(*mats[0][0][1:3], bias)
    kv_half(rank, h1, *mats[0], ukv, ad, bias, kv)
    ready()
    kv_half(rank, h1, *mats[1], ukv, ad, bias, kv)
    flush(0)
    flush(1)
    for mat, at in mats:
        w_out[:, pl.ds(at, part)] = mat[3][...]
    flush(7)
    h_last = jnp.concatenate([h[...] for h in hl], 0)
    x_last = jnp.concatenate([x[...] for x in xl], 0)
    u_q = lanes(nt(h_last, down).astype(BF16), 0, rank)
    for mat, at in mats:
        cols = pl.ds(at, part)
        total = nn(h_last, mat[0][...]) + bias[3:4, cols] + SCALE * nn(u_q, ad[1, :, cols])
        q[:, cols] = total.astype(BF16)
    q_all = q[...]
    parts = []
    for b in range(micro):
        wide_q = expand_heads(q_all[b * slots : (b + 1) * slots], heads)
        scores = HEAD_DIM ** (-0.5) * nt(kv[b, :, :width], wide_q)
        segment = column(seg_v[pl.ds((core + b) % 2, 1), :])
        inside = segment == iota((tokens, heads * slots), 1) % slots
        scores = jnp.where(inside, scores, -1000000000.0)
        e = jnp.exp(scores - jnp.max(scores, 0, keepdims=True))
        probs = e / jnp.sum(e, 0, keepdims=True)
        p_t[b] = probs
        parts.append(collapse_heads(tn(probs.astype(BF16), kv[b, :, width:]), heads))
    flush(5)
    o_all = jnp.concatenate(parts, 0).astype(BF16)
    o[...] = o_all
    u_o = lanes(nt(o_all, down).astype(BF16), 3 * rank, 4 * rank)
    mid = x_last + nn(o_all, w_out[...]) + bias[6:7, :] + SCALE * nn(u_o, up)
    x1[...] = mid
    unit, _ = norm_parts(mid)
    h2 = (unit * gains[1:2, :] + bias[1:2, :]).astype(BF16)
    u_up = lanes(nt(h2, down).astype(BF16), 4 * rank, 5 * rank)
    e1[:, :width] = h2
    e1[:, width:] = jnp.zeros_like(e1[:, width:])
    e1[:, width : width + 5 * rank] = u_up
    u[...] = u_q + u_o + u_up


def preload_kernel(n, ready, source, _, *refs):
    w_up, w_down, sems = refs[-3:]
    rep, core = lax.axis_index("rep"), lax.axis_index("shard") % 2
    loads = []
    for index, wide in enumerate((w_up, w_down)):
        pieces = refs[index * n : (index + 1) * n]
        height = pieces[0].shape[0]
        spots = [(source[rep, core, k] * height, 0) for k in range(n)]
        loads.append(load(pieces, spots, wide, sems.at[index]))
    for wait in loads:
        wait()


def ffn_kernel(rank, last, ready, source, own, sib, f_own, f_sib, bias, *refs):
    up_last, down_last, _, _, f, a, w_up, w_down, mine, send, sems = refs
    width = w_up.shape[0]
    rep, core = lax.axis_index("rep"), lax.axis_index("shard") % 2
    loads = []
    for index, (piece, wide) in enumerate(((up_last, w_up), (down_last, w_down))):
        spots = [(source[rep, core, last] * piece.shape[0], 0)]
        loads.append(load([piece], spots, wide, sems.at[index]))
    ready()
    lane = 5 * rank
    rows = own.shape[0]
    h2 = jnp.concatenate([own[:, :width], sib[:, :width]], 0)
    pair_own, pair_sib = factors(f_own, rank), factors(f_sib, rank)
    extra = jnp.concatenate(
        [
            nn(own[:, width : width + lane], pair_own[1]),
            nn(sib[:, width : width + lane], pair_sib[1]),
        ],
        0,
    )
    loads[0]()
    total = nn(h2, w_up[...]) + bias[...] + SCALE * extra
    f[...] = total
    low = jax.nn.gelu(total, approximate=True).astype(BF16)
    a[...] = low
    for out, at, pair in ((mine, 0, pair_own), (send, rows, pair_sib)):
        out[:, width:] = jnp.zeros_like(out[:, width:])
        out[:, width : width + lane] = nt(low[at : at + rows], pair[0])
    loads[1]()
    y = nn(low, w_down[...])
    mine[:, :width] = y[:rows]
    send[:, :width] = y[rows:]


def score_kernel(rank, ready, x1, mine, recv, ad, gains, bias, head, x2, u_dn, score):
    ready()
    width = x1.shape[1]
    lane = 5 * rank
    u = (mine[:, width : width + lane] + recv[:, width : width + lane]).astype(BF16)
    u_dn[...] = u
    end = x1[...] + mine[:, :width] + recv[:, :width] + bias[11:12, :] + SCALE * nn(u, ad[1])
    x2[...] = end
    unit, _ = norm_parts(end)
    token = jnp.sum((unit * gains[2:3, :] + bias[2:3, :]) * head[...], -1, keepdims=True)
    score[...] = jnp.broadcast_to(token, score.shape)


def loss_kernel(rank, members, ready, *refs):
    scores = refs[:members]
    x2, u_dn, pairs, count, ad, gains, bias, head = refs[members : members + 8]
    e2, g_end, g_dn, small = refs[members + 8 :]
    ready()
    rows, width = x2.shape
    half = rows // 2

    def value(m):
        if m % 2 == 0:
            return scores[m][...]
        return jnp.concatenate([scores[m][half:, :], scores[m][:half, :]], 0)

    level = [value(m) for m in range(members)]
    while len(level) > 1:
        level = [level[i] + level[i + 1] for i in range(0, len(level), 2)]
    mean_reward = level[0][:, :1] / members
    at = iota((rows, pairs.shape[1]), 0)
    pick = (at == pairs[0:1, :]).astype(F32) - (at == pairs[1:2, :]).astype(F32)
    live = (pairs[0:1, :] >= 0).astype(F32)
    diff = jnp.sum(pick * mean_reward, 0, keepdims=True)
    terms = live * jax.nn.softplus(-diff)
    grad_diff = -live * jax.nn.sigmoid(-diff) / count[:, :1]
    grad_score = jnp.sum(pick * grad_diff, -1, keepdims=True) / members
    unit, rstd = norm_parts(x2[...])
    final = unit * gains[2:3, :] + bias[2:3, :]
    small[...] = jnp.zeros_like(small)
    small[0:1, :] = jnp.sum(final * grad_score, 0, keepdims=True)
    small[1:2, :] = jnp.broadcast_to(jnp.sum(terms, -1, keepdims=True), (1, width))
    end = norm_back(grad_score * head[...], gains[2:3, :], unit, rstd)
    g_end[...] = end
    g_ff = end.astype(BF16)
    left = lanes((SCALE * nt(g_ff, ad[1])).astype(BF16), 4 * rank, 5 * rank)
    g_dn[...] = SCALE * tn(u_dn[...], g_ff)
    e2[:, :width] = g_ff
    e2[:, width:] = jnp.zeros_like(e2[:, width:])
    e2[:, width : width + 5 * rank] = left


def slope_kernel(ready, f, _, out):
    x = f[...]
    c0, c1 = math.sqrt(2.0 / math.pi), 0.044715
    t = jnp.tanh(c0 * (x + c1 * x * x * x))
    out[...] = 0.5 * (1.0 + t) + 0.5 * x * (1.0 - t * t) * (c0 * (1.0 + 3.0 * c1 * x * x))


def ffn_back_kernel(rank, ready, own, sib, slope, f_own, f_sib, wide_u, wide_d,
                    mine, send, g_out):
    width = wide_u.shape[0]
    lane = 5 * rank
    ready()
    rows = own.shape[0]
    left_own, left_sib = own[:, width : width + lane], sib[:, width : width + lane]
    g_ff = jnp.concatenate([own[:, :width], sib[:, :width]], 0)
    pair_own, pair_sib = factors(f_own, rank), factors(f_sib, rank)
    extra = jnp.concatenate([nn(left_own, pair_own[0]), nn(left_sib, pair_sib[0])], 0)
    g_a = (nt(g_ff, wide_d[...]) + extra).astype(BF16)
    g_f = (g_a.astype(F32) * slope[...]).astype(BF16)
    g_h = nt(g_f, wide_u[...])
    for out, low, factor in ((mine, 0, pair_own), (send, rows, pair_sib)):
        out[:, :width] = g_h[low : low + rows]
        out[:, width:] = jnp.zeros_like(out[:, width:])
        out[:, width : width + lane] = SCALE * nt(g_f[low : low + rows], factor[1])
    g_out[...] = g_f


def hidden_kernel(rank, ready, own, sib, e1_own, e1_sib, a, g_f, mine, send):
    rows = own.shape[0]
    cut = slice(own.shape[1] - 128, own.shape[1] - 128 + 5 * rank)
    for out, low, left, u in ((mine, 0, own, e1_own), (send, rows, sib, e1_sib)):
        out[0:rank, :] = tn(left[:, cut], a[low : low + rows, :])[4 * rank :]
        out[rank:, :] = SCALE * tn(u[:, cut], g_f[low : low + rows, :])[4 * rank :]


def factor_kernel(rank, half, ready, mine, other, err, start, mat, left):
    ready()
    core = lax.axis_index("shard") % 2
    first = (core == 0).astype(F32)
    even = mine[...] * first + other[...] * (1.0 - first)
    odd = mine[...] * (1.0 - first) + other[...] * first
    parts = []
    for r in range(mine.shape[1] // half):
        cut = slice(r * half, (r + 1) * half)
        parts += [even[:, cut], odd[:, cut]]
    mat[...] = jnp.concatenate(parts, 1) + err[...]
    left[...] = nn(start[...], mat[...], EXACT)


def rows_back_kernel(micro, rank, ready, *refs):
    mine, recv, g_end, g_dn, small, x1, e1, u, o, q, p_t, kv, ukv_t = refs[:13]
    hl = refs[13 : 13 + micro]
    h1 = refs[13 + micro : 13 + 2 * micro]
    ad, gains, err, start, w_out, mat, left = refs[13 + 2 * micro :]
    ready(ad, gains)
    rows, width = x1.shape
    slots = rows // micro
    heads = width // HEAD_DIM
    lane = 5 * rank
    down, up = ad[0], ad[1]
    h2 = e1[:, :width]
    u_rows = u[...]
    g_u = (mine[:, width : width + lane] + recv[:, width : width + lane]).astype(BF16)
    g_h2 = (mine[:, :width] + recv[:, :width] + nn(g_u, down)).astype(BF16)
    grad_in = tn(g_u, h2)
    unit, rstd = norm_parts(x1[...])
    g_mid = g_end[...] + norm_back(g_h2.astype(F32), gains[1:2, :], unit, rstd)
    g_att = g_mid.astype(BF16)
    grad_out = g_dn[...] + SCALE * tn(lanes(u_rows, 3 * rank, 4 * rank), g_att)
    g_ol = lanes((SCALE * nt(g_att, up)).astype(BF16), 3 * rank, 4 * rank)
    grad_in = grad_in + tn(g_ol, o[...])
    g_o = (nt(g_att, w_out[...]) + nn(g_ol, down)).astype(BF16)
    ready()
    scale = HEAD_DIM ** (-0.5)

    both = (lane, 2 * heads * slots)
    group, side = iota(both, 0) // rank, iota(both, 1) // (heads * slots)
    keep = jnp.where(group == 1 + side, jnp.where(side == 0, scale, 1.0), 0.0)

    for b in range(micro):
        pick = slice(b * slots, (b + 1) * slots)
        wide_g = expand_heads(g_o[pick], heads)
        wide_q = expand_heads(q[pick, :], heads)
        probs = p_t[b]
        g_p = nt(kv[b, :, width:], wide_g)
        g_s = (probs * (g_p - jnp.sum(probs * g_p, 0, keepdims=True))).astype(BF16)
        g_q = (scale * collapse_heads(tn(g_s, kv[b, :, :width]), heads)).astype(BF16)
        u_q = lanes(u_rows[pick], 0, rank)
        tall = jnp.concatenate([g_s, probs.astype(BF16)], 1)
        flat = jnp.concatenate([wide_q, wide_g], 0)
        inner = (nn(ukv_t[b], tall) * keep).astype(BF16)
        grad_out = grad_out + SCALE * (tn(u_q, g_q) + nn(inner, flat))
        g_uq = lanes((SCALE * nt(g_q, up)).astype(BF16), 0, rank)
        inner = (nt(up, flat) * keep).astype(BF16)
        g_ukv = (SCALE * nt(inner, tall)).astype(BF16)
        grad_in = grad_in + tn(g_uq, hl[b][...]) + nn(g_ukv, h1[b][...])
    mat[0] = grad_in + err[0]
    mat[1] = grad_out + err[1]
    first = start.shape[1]
    left[0:first, :] = nn(start[0], mat[0], EXACT)
    left[first : 2 * first, :] = nn(start[1], mat[1], EXACT)
    left[2 * first :, :] = small[...]


def orthonormal_rows(refs):
    count = refs[0].shape[0]
    for k in range(count):
        for ref in refs:
            block = ref[...]
            row = block[k : k + 1, :]
            dots = jnp.sum(block * row, -1, keepdims=True)
            scale = lax.rsqrt(dots[k : k + 1] + 1e-06)
            row = row * scale
            at = iota(block.shape, 0)
            later = jnp.where(at > k, block - (dots * scale) * row, block)
            ref[...] = jnp.where(at == k, row, later)


def ortho_kernel(rank, ready, d_a, d_b, f_a, f_b, mat_d, mat_f, ph_d, ph_f, head, note):
    count = rank
    for j in range(2):
        part = slice(j * count, (j + 1) * count)
        ph_d[j] = d_a[part, :] + d_b[part, :]
    ph_f[...] = f_a[...] + f_b[...]
    rest = d_a[2 * count :, :] + d_b[2 * count :, :]
    refs = (ph_d.at[0], ph_d.at[1], ph_f)
    orthonormal_rows(refs)
    ready()
    grad = rest[0:1, :]
    head[...] = grad
    parts = []
    for ref, mat in zip(refs, (mat_d.at[0], mat_d.at[1], mat_f), strict=True):
        parts.append(nt(ref[...], mat[...], EXACT))
    for ref in refs:
        parts.append(nt(ref[...], ref[...], EXACT))
    parts.append(jnp.broadcast_to(jnp.sum(grad * grad, keepdims=True), (count, 1)))
    parts.append(jnp.broadcast_to(rest[1:2, :1], (count, 1)))
    used = sum(x.shape[1] for x in parts)
    parts.append(jnp.zeros((count, 128 - used), F32))
    own = jnp.concatenate(parts, 1)

    @pl.loop(0, note.shape[0])
    def _(i):
        note[i] = own


def final_kernel(rank, n, m, ready, notes, ph_d, ph_f, ph_do, ph_fo, ghead, mat_d, mat_f,
                 wd, wf, wh, md, mf, mh,
                 nd, nf, nh, nmd, nmf, nmh, err_d, err_f, q_d, q_f, mean_loss, norm):
    ready()
    shard = lax.axis_index("shard")
    count = rank
    sizes = (5 * rank, 5 * rank, 2 * rank)
    total = jnp.zeros((1, 1), F32)
    loss = jnp.zeros((1, 1), F32)
    own = jnp.zeros((count, 128), F32)
    for s in range(m):
        block = notes[s]
        for r in range(1, n):
            block = block + notes[r * m + s]
        own = jnp.where(shard == s, block, own)
        note = notes[s]
        at, gram = 0, sum(sizes)
        for size in sizes:
            right = block[:, at : at + size]
            inner = note[:, gram : gram + count]
            total = total + jnp.sum(right * nn(inner, right, EXACT), keepdims=True)
            at += size
            gram += count
        total = total + note[0:1, gram : gram + 1]
        loss = loss + note[0:1, gram + 1 : gram + 2]
    grad_norm = jnp.sqrt(total)
    clip = jnp.minimum(1.0, CLIP / (grad_norm + 1e-06))
    mean_loss[...] = loss / m
    norm[...] = grad_norm
    at = 0
    for j in range(2):
        right = own[:, at : at + sizes[j]]
        q_d[j] = right
        at += sizes[j]
        err_d[j] = mat_d[j] - tn(right, ph_d[j], EXACT) * (1.0 / n)
        fresh = MOMENTUM * md[j] + clip * tn(right, ph_do[j], EXACT)
        nmd[j] = fresh
        nd[j] = wd[j] - RATE * fresh
    right = own[:, at : at + sizes[2]]
    q_f[...] = right
    err_f[...] = mat_f[...] - tn(right, ph_f[...], EXACT) * (1.0 / n)
    fresh = MOMENTUM * mf[...] + clip * tn(right, ph_fo[...], EXACT)
    nmf[...] = fresh
    nf[...] = wf[...] - RATE * fresh
    fresh = MOMENTUM * mh[...] + clip * ghead[...]
    nmh[...] = fresh
    nh[...] = wh[...] - RATE * fresh


class Raw:
    def __init__(self, array):
        self.array = array


class Scalars(Raw):
    pass


class Far(Raw):
    pass


class Fresh(Raw):
    pass


class Part:
    def __init__(self, array, rows):
        self.array, self.rows = array, rows


class Kept:
    def __init__(self, shape, dtype):
        self.shape, self.dtype = tuple(shape), dtype


class Placed(Kept):
    pass


def call(body, outs, args, scratch=(), vmem=60, name=None, groups=None, aliases=None, flushes=False):
    arrays, specs, staged = [], [], []
    for arg in args:
        arrays.append(arg.array if isinstance(arg, Raw | Part) else arg)
        space = pl.ANY
        if isinstance(arg, Scalars):
            space = pltpu.SMEM
        elif isinstance(arg, Fresh):
            space = pltpu.VMEM
        elif isinstance(arg, Far):
            space = pltpu.HBM
        specs.append(pl.BlockSpec(memory_space=space))
        if isinstance(arg, Part):
            staged.append(pltpu.VMEM((arg.rows, *arg.array.shape[1:]), arg.array.dtype))
        elif not isinstance(arg, Raw):
            staged.append(pltpu.VMEM(arg.shape, arg.dtype))
    results = [pltpu.VMEM(o.shape, o.dtype) for o in outs if not isinstance(o, Kept)]

    def kernel(*refs):
        ins, refs = refs[: len(args)], refs[len(args) :]
        targets, refs = refs[: len(outs)], refs[len(outs) :]
        held, refs = refs[: len(staged)], refs[len(staged) :]
        buffers, refs = refs[: len(results)], refs[len(results) :]
        extra, sems = refs[:-1], refs[-1]
        copies, given, i = {}, [], 0
        for arg, ref in zip(args, ins, strict=True):
            if isinstance(arg, Raw):
                given.append(ref)
                continue
            origin = ref.at[pl.ds(0, arg.rows)] if isinstance(arg, Part) else ref
            copies[id(held[i])] = pltpu.make_async_copy(origin, held[i], sems.at[i])
            given.append(held[i])
            i += 1
        for copy in copies.values():
            copy.start()

        def ready(*some):
            for key in [id(r) for r in some] or list(copies):
                copies.pop(key).wait()

        local, back, i = [], {}, 0
        for j, out in enumerate(outs):
            if isinstance(out, Kept):
                local.append(targets[j])
                continue
            local.append(buffers[i])
            back[j] = pltpu.make_async_copy(buffers[i], targets[j], sems.at[len(staged) + i])
            i += 1
        def flush(j):
            back[j].start()
            begun.append(j)

        begun = []
        if groups:
            given = [given[:groups], *given[groups:]]
        body(ready, *((flush,) if flushes else ()), *given, *local, *extra)
        for j, copy in back.items():
            if j not in begun:
                copy.start()
        for copy in back.values():
            copy.wait()

    def place(out):
        if type(out) is Kept:
            return pltpu.VMEM
        return pl.ANY if isinstance(out, Kept) else pltpu.HBM

    return pl.pallas_call(
        kernel,
        out_shape=tuple(jax.ShapeDtypeStruct(o.shape, o.dtype) for o in outs),
        in_specs=specs,
        out_specs=tuple(pl.BlockSpec(memory_space=place(o)) for o in outs),
        scratch_shapes=[
            *staged, *results, *scratch, pltpu.SemaphoreType.DMA((max(1, len(staged) + len(results)),)),
        ],
        compiler_params=pltpu.CompilerParams(vmem_limit_bytes=vmem << 20),
        cost_estimate=pl.CostEstimate(flops=0, bytes_accessed=0, transcendentals=0),
        input_output_aliases=aliases or {},
        name=name,
    )(*arrays)


def shaped(shape, dtype):
    return jax.ShapeDtypeStruct(tuple(shape), dtype)


def ring_order(count):
    side = math.isqrt(count // 2)
    if side < 2 or 2 * side * side != count:
        return list(range(count))
    depth = 2 * side
    cells = []
    for z in range(depth):
        ys = range(1, side) if z % 2 == 0 else range(side - 1, 0, -1)
        cells += [(z, y) for y in ys]
    cells += [(z, 0) for z in range(depth - 1, -1, -1)]
    return [z * side + y for z, y in cells]


def pairs_of(n, m, move):
    return [(r * m + s, t[0] * m + t[1]) for r in range(n) for s in range(m) for t in [move(r, s)]]


def on_device(n, m, *args):
    (
        token_ids, positions, segment_ids, pair_index, embed_table, pos_table,
        base_qkv, base_out, base_up, base_down, base_gains, base_bias,
        adapt_d, adapt_f, head, mom_d, mom_f, mom_head, err_d, err_f, qstart_d, qstart_f,
    ) = args
    micro, tokens = token_ids.shape
    held, width = embed_table.shape
    pairs = pair_index.shape[1]
    slots = 2 * pairs
    rows = micro * slots
    hidden = base_up.shape[1]
    rank = adapt_f.shape[2] // 2
    heads = width // HEAD_DIM
    rd, rf = base_up.shape[0], base_down.shape[0]
    half = rf // 2
    own_hidden = hidden // 2
    rep, shard = lax.axis_index("rep"), lax.axis_index("shard")
    core = shard % 2

    order = ring_order(n)
    place = {r: i for i, r in enumerate(order)}
    around = pairs_of(
        n, m, lambda r, s: (order[(place[r] + (1 if s % 2 == 0 else -1)) % n], s)
    )
    turns = [
        [[order[(place[r] + (-k if c == 0 else k)) % n] for k in range(n)] for c in range(2)]
        for r in range(n)
    ]
    source = Scalars(jnp.asarray(np.array(turns, np.int32)))

    def send(x, perm):
        return lax.ppermute(x, AXES, perm)

    def across(x, mask):
        return send(x, pairs_of(n, m, lambda r, s: (r, s ^ mask)))

    def ring(x):
        out = []
        for _ in range(n - 1):
            x = send(x, around)
            out.append(x)
        return out

    def pick(x, index, axis):
        return lax.dynamic_index_in_dim(x, index, axis, keepdims=False)

    d_t = adapt_d[0].transpose(1, 2, 0)
    f_t = adapt_f[0].T
    below = 2 * rank
    live = pair_index[..., 0].reshape(1, micro * pairs)
    whole_blocks = rd % 128 == 0 and half % 128 == 0
    if whole_blocks:
        left, right, up_part, down_part = call(
            split_kernel,
            [shaped((rd + below, width), BF16), shaped((rd + below, width), BF16),
             shaped((rd, own_hidden), BF16), shaped((half, width), BF16)],
            [d_t, f_t, head, live, Raw(base_qkv), Raw(base_out), Raw(base_up), Raw(base_down)],
            [pltpu.SemaphoreType.DMA((n + 5,))],
            vmem=56, name="split",
        )
    else:
        two = jnp.concatenate([head, jnp.broadcast_to(jnp.sum((live >= 0).astype(F32)), (below - 1, rd))], 0)
        flat = [x for x in d_t.reshape(10 * rank // below, below, rd)]
        first = jnp.concatenate([base_qkv, base_out], 1).reshape(rd, 4, 2, width // 2)
        first = pick(first, core, 2).reshape(rd, 2, width)
        sides = []
        for side, extra in enumerate((jnp.concatenate([*flat, two], 1), f_t)):
            extra = jnp.pad(extra.astype(BF16), ((0, 0), (0, width - extra.shape[1])))
            sides.append(jnp.concatenate([first[:, side], extra], 0))
        left, right = sides
        up_part = pick(base_up.reshape(rd, n, 2, half), core, 2).reshape(rd, own_hidden)
        down_part = pick(base_down.reshape(2, half, width), core, 0)

    def after(x, *others):
        return pl.pallas_call(
            lambda *refs: None,
            out_shape=jax.ShapeDtypeStruct(x.shape, x.dtype),
            in_specs=[pl.BlockSpec(memory_space=pl.ANY)] * (1 + len(others)),
            out_specs=pl.BlockSpec(memory_space=pl.ANY),
            input_output_aliases={0: 0},
            cost_estimate=pl.CostEstimate(flops=0, bytes_accessed=0, transcendentals=0),
            name="after",
        )(x, *others)

    def lookup(*start):
        ids = jnp.stack([pick(token_ids, (core + b) % micro, 0) for b in range(micro)])
        near = ids - shard * held
        inside = (near >= 0) & (near < held)
        found = jnp.take(embed_table, after(jnp.clip(near, 0, held - 1), *start), axis=0)
        found = jnp.where(inside[..., None], found, jnp.zeros_like(found))
        return found[0], found[1]

    def shared(own, given, *others):
        own = own + across(after(given, *others), 1)
        mask = 2
        while mask < m // 2:
            own = own + across(own, mask)
            mask *= 2
        return own, across(own, mask) if m > 2 else own

    bias = base_bias.reshape(-1, width)
    bias_1 = pick(base_bias[7 * width : 7 * width + hidden].reshape(n, 2, half), core, 1)
    bias_1 = bias_1.reshape(1, own_hidden)
    local = (jnp.arange(micro) + core) % micro * slots
    pair_rows = jnp.where(pair_index >= 0, pair_index + local[:, None, None], -1)
    pair_rows = pair_rows.reshape(micro * pairs, 2).T

    pos_rows = pos_table[:tokens]

    lefts, rights, ups, downs = [left], [right], [up_part], [down_part]

    def behind(low, high, *gate):
        for k in range(low, min(high, n)):
            if gate:
                ups[-1], downs[-1] = after(ups[-1], *gate), after(downs[-1], *gate)
            gate = ()
            ups.append(send(ups[-1], around))
            downs.append(send(downs[-1], around))

    for k in range(1, n):
        gate = []
        if k == 9:
            gate = [ups[1], downs[1]]
        if k == 4:
            gate = [tok_own, bias, bias_1, pos_rows, pair_rows]
        if k == 9:
            gate = [tok_far]
        if gate:
            lefts[-1], rights[-1] = after(lefts[-1], *gate), after(rights[-1], *gate)
        lefts.append(send(lefts[-1], around))
        rights.append(send(rights[-1], around))
        if k == 1:
            ups[-1], downs[-1] = ups[-1], downs[-1]
            ups.append(send(ups[-1], around))
            downs.append(send(downs[-1], around))
            own, given = lookup(left)
        if k == 1:
            tok_own, tok_far = shared(own, given, lefts[1], rights[1], ups[1], downs[1])

    parts = [tok_own, tok_far] if m > 2 else [tok_own]
    both = tok_own + tok_far if m > 2 else tok_own
    toks = [parts, [across(both, 1)]]

    step_a = [*lefts, *rights]
    if whole_blocks:
        mats = []
        for k in range(4):
            mats += call(
                functools.partial(assemble_kernel, k % 2),
                [shaped((width, width // 2), BF16)],
                [source, *[Far(x) for x in (lefts, rights)[k // 2]]],
                [pltpu.SemaphoreType.DMA((n,))],
                vmem=8, name="assemble",
            )
        wide_d, f_own, f_other, wide_head, count_row = call(
            functools.partial(unpack_kernel, rank, rd),
            [shaped((2, 5 * rank, width), BF16), shaped((2 * rank, own_hidden), BF16),
             Kept((2 * rank, own_hidden), BF16), shaped((1, width), F32), shaped((1, 128), F32)],
            [source, *[Far(x) for x in step_a]],
            [pltpu.VMEM((10 * rank + below, width), BF16), pltpu.VMEM((below, hidden), BF16),
             pltpu.SemaphoreType.DMA((n * (10 * rank // below + 2),))],
            vmem=52, name="unpack",
        )
    else:
        turned = jnp.asarray(np.argsort(np.array(turns, np.int32), -1).astype(np.int32))
        place_at = lax.dynamic_slice(turned, (rep, core, 0), (1, 1, n)).reshape(n)
        steps_l, steps_r = [
            jnp.stack([pick(jnp.stack(x), place_at[r], 0) for r in range(n)]) for x in (lefts, rights)
        ]
        mats = [x[:, :rd].reshape(width, 2, width // 2) for x in (steps_l, steps_r)]
        mats = [x[:, j] for x in mats for j in range(2)]
        count_d = 10 * rank // below
        wide_d = steps_l[:, rd:, : count_d * rd].reshape(n, below, count_d, rd)
        wide_d = wide_d.transpose(2, 1, 0, 3).reshape(2, 5 * rank, width)
        wide_f = steps_r[:, rd:, :rf].reshape(n, 2 * rank, 2, half)
        wide_f = wide_f.transpose(2, 1, 0, 3).reshape(2, 2 * rank, own_hidden)
        f_own, f_other = pick(wide_f, core, 0), pick(wide_f, 1 - core, 0)
        last = steps_l[:, rd:, count_d * rd : (count_d + 1) * rd].astype(F32)
        wide_head = last[:, 0].reshape(1, width)
        count_row = jnp.broadcast_to(jnp.sum(last[:, 1, 0]), (1, 128))
    count = count_row[0, 0]
    f_sib = across(f_other, 1)
    mats += [across(x, 1) for x in mats]

    h1, xl, hl = [], [], []
    for b in range(micro):
        a, x, h = call(
            functools.partial(front_kernel, b),
            [shaped((tokens, width), BF16), shaped((slots, width), F32), shaped((slots, width), BF16)],
            [*toks[b], positions, segment_ids, pos_rows, base_gains, bias],
            [pltpu.VMEM((tokens, width), BF16), pltpu.VMEM((tokens, width), BF16)],
            groups=len(toks[b]), vmem=56, name="front",
        )
        h1.append(a)
        xl.append(x)
        hl.append(h)

    behind(2, 3, lefts[5])
    behind(3, 4, *mats[:2])
    behind(4, 5, *mats[2:4], hl[0])
    behind(5, 6, hl[1], wide_d)
    behind(6, 7)
    kv, ukv_t, o, x1, q, p_t, u, w_out, e1 = call(
        functools.partial(rows_kernel, micro, rank),
        [shaped((micro, tokens, 2 * width), BF16), shaped((micro, 5 * rank, tokens), BF16),
         shaped((rows, width), BF16), shaped((rows, width), F32), shaped((rows, width), BF16),
         shaped((micro, tokens, heads * slots), F32), shaped((rows, 5 * rank), BF16),
         shaped((width, width), BF16), shaped((rows, width + 128), BF16)],
        [segment_ids, *h1, *hl, *xl, wide_d, base_gains, bias, *mats],
        [pltpu.VMEM((micro, tokens, 5 * rank), BF16)],
        vmem=60, flushes=True, name="rows",
    )
    behind(7, n, o)
    ups, downs = [[Far(y) for y in x] for x in (ups, downs)]
    e1_sib = across(e1, 1)
    w_up, w_down = call(
        functools.partial(preload_kernel, n - 1),
        [Kept((width, own_hidden), BF16), Kept((own_hidden, width), BF16)],
        [source, Raw(o), *ups[:-1], *downs[:-1]],
        [pltpu.SemaphoreType.DMA((2, n - 1))],
        vmem=4, name="preload",
    )
    f, a, w_up, w_down, y_mine, y_send = call(
        functools.partial(ffn_kernel, rank, n - 1),
        [Kept((2 * rows, own_hidden), F32), Kept((2 * rows, own_hidden), BF16),
         Kept((width, own_hidden), BF16), Kept((own_hidden, width), BF16)]
        + [Kept((rows, width + 128), F32)] * 2,
        [source, Fresh(e1), Fresh(e1_sib), f_own, f_sib, bias_1, ups[-1], downs[-1], Fresh(w_up), Fresh(w_down)],
        [pltpu.SemaphoreType.DMA((2, 1))],
        aliases={8: 2, 9: 3}, vmem=10, name="ffn",
    )
    x2, u_dn, score = call(
        functools.partial(score_kernel, rank),
        [Kept((rows, width), F32), Kept((rows, 5 * rank), BF16), Kept((rows, 128), F32)],
        [Fresh(x1), Fresh(y_mine), Fresh(across(y_send, 1)), wide_d, base_gains, bias, wide_head],
        vmem=10, name="score",
    )
    scores = [score] + [across(score, k) for k in range(1, m)]
    (slope,) = call(
        slope_kernel,
        [Kept((2 * rows, own_hidden), F32)],
        [Fresh(f), Fresh(score)],
        vmem=6, name="slope",
    )
    e2, g_end, g_dn, small = call(
        functools.partial(loss_kernel, rank, m),
        [Kept((rows, width + 128), BF16), Kept((rows, width), F32), Kept((5 * rank, width), F32),
         Kept((8, width), F32)],
        [*[Fresh(x) for x in scores], Fresh(x2), Fresh(u_dn), pair_rows, count_row, wide_d, base_gains, bias, wide_head],
        vmem=10, name="loss",
    )
    e2_sib = across(e2, 1)
    y_mine, y_send, g_f = call(
        functools.partial(ffn_back_kernel, rank),
        [Kept((rows, width + 128), F32)] * 2 + [Kept((2 * rows, own_hidden), BF16)],
        [Fresh(e2), Fresh(e2_sib), Fresh(slope), f_own, f_sib,
         Fresh(w_up), Fresh(w_down)],
        vmem=14, name="ffn_back",
    )
    y_other = across(y_send, 1)
    gf_mine, gf_send = call(
        functools.partial(hidden_kernel, rank),
        [Kept((2 * rank, own_hidden), F32)] * 2,
        [Fresh(x) for x in (e2, e2_sib, e1, e1_sib, a, g_f)],
        vmem=6, name="hidden",
    )
    mat_f, left_f = call(
        functools.partial(factor_kernel, rank, half),
        [Kept((2 * rank, hidden), F32), Kept((rank, hidden), F32)],
        [Fresh(gf_mine), Fresh(across(gf_send, 1)), err_f[0, 0].T, qstart_f[0].T],
        vmem=10, name="factor_f",
    )
    mat_d, left_d = call(
        functools.partial(rows_back_kernel, micro, rank),
        [Kept((2, 5 * rank, width), F32), Kept((2 * rank + 8, width), F32)],
        [Fresh(y_mine), Fresh(y_other), Fresh(g_end), Fresh(g_dn), Fresh(small),
         *[Fresh(x) for x in (x1, e1, u, o, q, p_t, kv, ukv_t, *hl, *h1)],
         wide_d, base_gains, err_d[0, 0].transpose(1, 2, 0), qstart_d[0].transpose(0, 2, 1), Fresh(w_out)],
        vmem=26, name="rows_back",
    )

    def rep_parts(x, order):
        part = jnp.zeros_like(x)
        bits = [1 << k for k in range(n.bit_length() - 1)][::order]
        for bit in bits:
            part = send(x, pairs_of(n, m, lambda r, s, bit=bit: (r ^ bit, s)))
            if bit != bits[-1]:
                x = x + part
        return Fresh(x), Fresh(part)

    ph_d, ph_f, total_head, note = call(
        functools.partial(ortho_kernel, rank),
        [Kept((2, rank, width), F32), Kept((rank, hidden), F32), Kept((1, width), F32),
         Kept((n * m, rank, 128), F32)],
        [*rep_parts(left_d, 1), *rep_parts(left_f, -1), Fresh(mat_d), Fresh(mat_f)],
        vmem=10, name="ortho",
    )
    notes = lax.all_to_all(note, AXES, 0, 0)
    own_ph_d = lax.dynamic_slice_in_dim(ph_d, rep * rd, rd, 2)
    own_ph_f = lax.dynamic_slice_in_dim(ph_f, rep * rf, rf, 1)
    own_head = lax.dynamic_slice_in_dim(total_head, rep * rd, rd, 1)
    nd, nf, nh, nmd, nmf, nmh, new_err_d, new_err_f, q_d, q_f, loss_sum, norm = call(
        functools.partial(final_kernel, rank, n, m),
        [shaped((2, 5 * rank, rd), F32), shaped((2 * rank, rf), F32), shaped((1, rd), F32)] * 2
        + [shaped((2, 5 * rank, width), F32), shaped((2 * rank, hidden), F32),
           shaped((2, rank, 5 * rank), F32), shaped((rank, 2 * rank), F32), shaped((1, 1), F32), shaped((1, 1), F32)],
        [Fresh(notes), Fresh(ph_d), Fresh(ph_f), Fresh(own_ph_d), Fresh(own_ph_f), Fresh(own_head),
         Fresh(mat_d), Fresh(mat_f), d_t, f_t, head, mom_d[0].transpose(1, 2, 0), mom_f[0].T, mom_head],
        vmem=16, name="final",
    )
    return (
        loss_sum[0, 0],
        count,
        norm[0, 0],
        nd.transpose(2, 0, 1)[None],
        nf.T[None],
        nh,
        nmd.transpose(2, 0, 1)[None],
        nmf.T[None],
        nmh,
        new_err_d.transpose(2, 0, 1)[None, None],
        new_err_f.T[None, None],
        q_d.transpose(0, 2, 1)[None],
        q_f.T[None],
    )


def solution(mesh):
    n, m = mesh.shape["rep"], mesh.shape["shard"]
    return jax.shard_map(
        functools.partial(on_device, n, m),
        mesh=mesh,
        in_specs=(
            P("rep", None),
            P("rep", None),
            P("rep", None),
            P("rep", None, None),
            P("shard", None),
            P(),
            P("rep", None),
            P("rep", None),
            P("rep", None),
            P("rep", None),
            P(),
            P(),
            P("shard", "rep", None, None),
            P("shard", "rep", None),
            P("shard", "rep"),
            P("shard", "rep", None, None),
            P("shard", "rep", None),
            P("shard", "rep"),
            P("shard", "rep", None, None, None),
            P("shard", "rep", None, None),
            P("shard", None, None, None),
            P("shard", None, None),
        ),
        out_specs=(
            P(),
            P(),
            P(),
            P("shard", "rep", None, None),
            P("shard", "rep", None),
            P("shard", "rep"),
            P("shard", "rep", None, None),
            P("shard", "rep", None),
            P("shard", "rep"),
            P("shard", "rep", None, None, None),
            P("shard", "rep", None, None),
            P("shard", None, None, None),
            P("shard", None, None),
        ),
        check_vma=False,
    )
```

```python
import functools
import math

import jax
import jax.numpy as jnp
import numpy as np
from jax import lax
from jax.experimental import pallas as pl
from jax.experimental.pallas import tpu as pltpu
from jax.sharding import PartitionSpec as P

HEAD_DIM = 64
F32 = jnp.float32
BF16 = jnp.bfloat16
EXACT = lax.Precision.HIGHEST
CLIP = 0.01
MOMENTUM = 0.9
RATE = 1000.0
SCALE = 2.0
AXES = ("rep", "shard")


def nn(a, b, precision=None):
    return lax.dot_general(
        a, b, (((1,), (0,)), ((), ())), precision=precision, preferred_element_type=F32
    )


def nt(a, b, precision=None):
    return lax.dot_general(
        a, b, (((1,), (1,)), ((), ())), precision=precision, preferred_element_type=F32
    )


def tn(a, b, precision=None):
    return lax.dot_general(
        a, b, (((0,), (0,)), ((), ())), precision=precision, preferred_element_type=F32
    )


def iota(shape, dim):
    return lax.broadcasted_iota(jnp.int32, shape, dim)


def lanes(x, low, high):
    at = iota(x.shape, x.ndim - 1)
    return jnp.where((at >= low) & (at < high), x, jnp.zeros_like(x))


def norm_parts(x):
    centered = x - jnp.mean(x, -1, keepdims=True)
    rstd = lax.rsqrt(jnp.mean(centered * centered, -1, keepdims=True) + 1e-05)
    return centered * rstd, rstd


def norm_back(grad, gain, unit, rstd):
    g = grad * gain
    return rstd * (
        g - jnp.mean(g, -1, keepdims=True) - unit * jnp.mean(g * unit, -1, keepdims=True)
    )


def load(pieces, spots, target, sems):
    copies = []
    for index, (piece, (row, column)) in enumerate(zip(pieces, spots, strict=True)):
        rows, columns = piece.shape
        if not isinstance(row, int):
            row = pl.multiple_of(row, rows)
        if not isinstance(column, int):
            column = pl.multiple_of(column, columns)
        place = target.at[pl.ds(row, rows), pl.ds(column, columns)]
        copies.append(pltpu.make_async_copy(piece, place, sems.at[index]))
    for copy in copies:
        copy.start()

    def wait():
        for copy in copies:
            copy.wait()

    return wait


def expand_heads(x, heads):
    rows, width = x.shape
    head_of = iota((rows, width), 1) // HEAD_DIM
    return jnp.concatenate(
        [jnp.where(head_of == h, x, jnp.zeros_like(x)) for h in range(heads)], 0
    )


def collapse_heads(x, heads):
    rows, width = x.shape[0] // heads, x.shape[1]
    head_of = iota((rows, width), 1) // HEAD_DIM
    total = jnp.zeros((rows, width), F32)
    for h in range(heads):
        total = total + jnp.where(head_of == h, x[h * rows : (h + 1) * rows], 0.0)
    return total


def column(row):
    return jnp.transpose(jnp.broadcast_to(row, (8, row.shape[1])))[:, :1]


def split_kernel(ready, d_t, f_t, head, live, qkv, out, up, down, left, right, up_part, down_part, sems):
    shard = lax.axis_index("shard")
    core = shard % 2
    rows, width = out.shape
    below = left.shape[0] - rows
    half = down_part.shape[0]
    blocks = up_part.shape[1] // half
    part = width // 2
    copies = []

    def move(piece, to):
        copies.append(pltpu.make_async_copy(piece, to, sems.at[len(copies)]))
        copies[-1].start()

    for j in range(4):
        at = pl.multiple_of(core * part, part)
        piece = out.at[:, pl.ds(at, part)] if j == 3 else qkv.at[:, pl.ds(at + j * width, part)]
        move(piece, (left, right)[j // 2].at[pl.ds(0, rows), pl.ds(j % 2 * part, part)])
    move(down.at[pl.ds(pl.multiple_of(core * half, half), half), :], down_part)
    for b in range(blocks):
        at = pl.multiple_of((2 * b + core) * half, half)
        move(up.at[:, pl.ds(at, half)], up_part.at[:, pl.ds(b * half, half)])
    ready()
    left[rows:, :] = jnp.zeros((below, width), BF16)
    right[rows:, :] = jnp.zeros((below, width), BF16)
    flat = jnp.concatenate([d_t[0], d_t[1]], 0).astype(BF16)
    count = flat.shape[0] // below
    for j in range(count):
        left[rows:, j * rows : (j + 1) * rows] = flat[j * below : (j + 1) * below]
    alive = jnp.sum((live[...] >= 0).astype(F32), keepdims=True)
    two = jnp.where(iota((below, rows), 0) == 0, head[...], alive)
    left[rows:, count * rows : (count + 1) * rows] = two.astype(BF16)
    right[rows:, : f_t.shape[1]] = f_t[...].astype(BF16)
    for copy in copies:
        copy.wait()


def assemble_kernel(column, ready, source, *refs):
    pieces, (mat, sems) = refs[:-2], refs[-2:]
    rep, core = lax.axis_index("rep"), lax.axis_index("shard") % 2
    rows, part = mat.shape[0] // len(pieces), mat.shape[1]
    tops = [piece.at[pl.ds(0, rows), pl.ds(column * part, part)] for piece in pieces]
    load(tops, [(source[rep, core, k] * rows, 0) for k in range(len(pieces))], mat, sems)()


def unpack_kernel(rank, rows, ready, source, *refs):
    pieces = refs[:-8]
    wide_d, own, other, head, count, flat, both, sems = refs[-8:]
    rep, core = lax.axis_index("rep"), lax.axis_index("shard") % 2
    n = len(pieces) // 2
    below, hidden = both.shape
    blocks = 10 * rank // below
    copies = []
    for k in range(n):
        r = source[rep, core, k]
        lanes_d = pl.ds(pl.multiple_of(r * rows, rows), rows)
        lanes_f = pl.ds(pl.multiple_of(r * (hidden // n), hidden // n), hidden // n)
        low = pl.ds(rows, below)
        for j in range(blocks + 1):
            place = flat.at[pl.ds(j * below, below), lanes_d]
            copies.append((pieces[k].at[low, pl.ds(j * rows, rows)], place))
        copies.append((pieces[n + k].at[low, pl.ds(0, hidden // n)], both.at[:, lanes_f]))
    copies = [pltpu.make_async_copy(a, b, sems.at[i]) for i, (a, b) in enumerate(copies)]
    for copy in copies:
        copy.start()
    for copy in copies:
        copy.wait()
    ready()
    wide_d[0] = flat[0 : 5 * rank, :]
    wide_d[1] = flat[5 * rank : 10 * rank, :]
    head[...] = flat[10 * rank : 10 * rank + 1, :].astype(F32)
    live = flat[10 * rank + 1 : 10 * rank + 2, :].astype(F32)
    count[...] = jnp.broadcast_to(jnp.sum(live, keepdims=True) / rows, count.shape)
    half = hidden // n // 2
    value = both[...]
    halves = [
        jnp.concatenate([value[:, (2 * r + c) * half : (2 * r + c + 1) * half] for r in range(n)], 1)
        for c in range(2)
    ]
    mine = (core == 0).astype(F32)
    zero, one = halves[0].astype(F32), halves[1].astype(F32)
    own[...] = (zero * mine + one * (1.0 - mine)).astype(BF16)
    other[...] = (zero * (1.0 - mine) + one * mine).astype(BF16)


def factors(ref, rank):
    value = ref[...]
    zero = jnp.zeros((4 * rank, value.shape[1]), value.dtype)
    return jnp.concatenate([zero, value[:rank]], 0), jnp.concatenate([zero, value[rank:]], 0)


def front_kernel(offset, ready, parts, pos_v, seg_v, table, gains, bias, h1, xl, hl, prow, tok):
    tokens, width = h1.shape
    slots = xl.shape[0]
    seq = (lax.axis_index("shard") + offset) % 2
    step = min(128, tokens)
    ready()
    position = pos_v[pl.ds(seq, 1), :]
    total = parts[0][...]
    for part in parts[1:]:
        total = total + part[...]
    tok[...] = total
    for i in range(tokens // step):
        rows = pl.ds(i * step, step)
        place = position[:, i * step : (i + 1) * step]
        onehot = (iota((tokens, step), 0) == place).astype(BF16)
        pos = tn(onehot, table[...])
        prow[rows, :] = pos.astype(BF16)
        unit, _ = norm_parts(tok[rows, :].astype(F32) + pos)
        h1[rows, :] = (unit * gains[0:1, :] + bias[0:1, :]).astype(BF16)
    segment = seg_v[pl.ds(seq, 1), :]
    after = pltpu.roll(jnp.broadcast_to(segment, (8, tokens)), tokens - 1, 1)[0:1]
    final = (segment != after) | (iota((1, tokens), 1) == tokens - 1)
    pick = ((segment == iota((slots, tokens), 0)) & final).astype(BF16)
    xl[...] = nn(pick, tok[...]) + nn(pick, prow[...])
    hl[...] = nn(pick, h1[...]).astype(BF16)


def kv_half(rank, h1, mat, at, u, ad, bias, kv):
    part = mat[0].shape[1]
    width = 2 * part
    cols = pl.ds(at, part)
    for j in range(2):
        to = pl.ds(pl.multiple_of(at + j * width, part), part)
        for b in range(len(h1)):
            total = nn(h1[b][...], mat[1 + j][...]) + bias[4 + j : 5 + j, cols]
            total = total + SCALE * nn(lanes(u[b], rank * (1 + j), rank * (2 + j)), ad[1, :, cols])
            kv[b, :, to] = total.astype(BF16)


def rows_kernel(micro, rank, ready, flush, *refs):
    seg_v, refs = refs[0], refs[1:]
    h1, hl, xl = refs[:micro], refs[micro : 2 * micro], refs[2 * micro : 3 * micro]
    ad, gains, bias = refs[3 * micro : 3 * micro + 3]
    mats = refs[3 * micro + 3 : 3 * micro + 11]
    kv, ukv_t, o, x1, q, p_t, u, w_out, e1, ukv = refs[3 * micro + 11 :]
    core = lax.axis_index("shard") % 2
    slots, width = hl[0].shape
    heads = width // HEAD_DIM
    tokens = h1[0].shape[0]
    part = width // 2
    places = [pl.multiple_of(core * part, part), pl.multiple_of((1 - core) * part, part)]
    mats = [(mats[:4], places[0]), (mats[4:], places[1])]
    ready(ad, *h1)
    down, up = ad[0], ad[1]
    for b in range(micro):
        ukv[b] = lanes(nt(h1[b][...], down).astype(BF16), rank, 3 * rank)
        ukv_t[b] = nt(down, h1[b][...]).astype(BF16)
    ready(*mats[0][0][1:3], bias)
    kv_half(rank, h1, *mats[0], ukv, ad, bias, kv)
    ready()
    kv_half(rank, h1, *mats[1], ukv, ad, bias, kv)
    flush(0)
    flush(1)
    for mat, at in mats:
        w_out[:, pl.ds(at, part)] = mat[3][...]
    flush(7)
    h_last = jnp.concatenate([h[...] for h in hl], 0)
    x_last = jnp.concatenate([x[...] for x in xl], 0)
    u_q = lanes(nt(h_last, down).astype(BF16), 0, rank)
    for mat, at in mats:
        cols = pl.ds(at, part)
        total = nn(h_last, mat[0][...]) + bias[3:4, cols] + SCALE * nn(u_q, ad[1, :, cols])
        q[:, cols] = total.astype(BF16)
    q_all = q[...]
    parts = []
    for b in range(micro):
        wide_q = expand_heads(q_all[b * slots : (b + 1) * slots], heads)
        scores = HEAD_DIM ** (-0.5) * nt(kv[b, :, :width], wide_q)
        segment = column(seg_v[pl.ds((core + b) % 2, 1), :])
        inside = segment == iota((tokens, heads * slots), 1) % slots
        scores = jnp.where(inside, scores, -1000000000.0)
        e = jnp.exp(scores - jnp.max(scores, 0, keepdims=True))
        probs = e / jnp.sum(e, 0, keepdims=True)
        p_t[b] = probs
        parts.append(collapse_heads(tn(probs.astype(BF16), kv[b, :, width:]), heads))
    flush(5)
    o_all = jnp.concatenate(parts, 0).astype(BF16)
    o[...] = o_all
    u_o = lanes(nt(o_all, down).astype(BF16), 3 * rank, 4 * rank)
    mid = x_last + nn(o_all, w_out[...]) + bias[6:7, :] + SCALE * nn(u_o, up)
    x1[...] = mid
    unit, _ = norm_parts(mid)
    h2 = (unit * gains[1:2, :] + bias[1:2, :]).astype(BF16)
    u_up = lanes(nt(h2, down).astype(BF16), 4 * rank, 5 * rank)
    e1[:, :width] = h2
    e1[:, width:] = jnp.zeros_like(e1[:, width:])
    e1[:, width : width + 5 * rank] = u_up
    u[...] = u_q + u_o + u_up


def preload_kernel(n, ready, source, _, *refs):
    w_up, w_down, sems = refs[-3:]
    rep, core = lax.axis_index("rep"), lax.axis_index("shard") % 2
    loads = []
    for index, wide in enumerate((w_up, w_down)):
        pieces = refs[index * n : (index + 1) * n]
        height = pieces[0].shape[0]
        spots = [(source[rep, core, k] * height, 0) for k in range(n)]
        loads.append(load(pieces, spots, wide, sems.at[index]))
    for wait in loads:
        wait()


def ffn_kernel(rank, last, ready, source, own, sib, f_own, f_sib, bias, *refs):
    up_last, down_last, _, _, f, a, w_up, w_down, mine, send, sems = refs
    width = w_up.shape[0]
    rep, core = lax.axis_index("rep"), lax.axis_index("shard") % 2
    loads = []
    for index, (piece, wide) in enumerate(((up_last, w_up), (down_last, w_down))):
        spots = [(source[rep, core, last] * piece.shape[0], 0)]
        loads.append(load([piece], spots, wide, sems.at[index]))
    ready()
    lane = 5 * rank
    rows = own.shape[0]
    h2 = jnp.concatenate([own[:, :width], sib[:, :width]], 0)
    pair_own, pair_sib = factors(f_own, rank), factors(f_sib, rank)
    extra = jnp.concatenate(
        [
            nn(own[:, width : width + lane], pair_own[1]),
            nn(sib[:, width : width + lane], pair_sib[1]),
        ],
        0,
    )
    loads[0]()
    total = nn(h2, w_up[...]) + bias[...] + SCALE * extra
    f[...] = total
    low = jax.nn.gelu(total, approximate=True).astype(BF16)
    a[...] = low
    for out, at, pair in ((mine, 0, pair_own), (send, rows, pair_sib)):
        out[:, width:] = jnp.zeros_like(out[:, width:])
        out[:, width : width + lane] = nt(low[at : at + rows], pair[0])
    loads[1]()
    y = nn(low, w_down[...])
    mine[:, :width] = y[:rows]
    send[:, :width] = y[rows:]


def score_kernel(rank, ready, x1, mine, recv, ad, gains, bias, head, x2, u_dn, score):
    ready()
    width = x1.shape[1]
    lane = 5 * rank
    u = (mine[:, width : width + lane] + recv[:, width : width + lane]).astype(BF16)
    u_dn[...] = u
    end = x1[...] + mine[:, :width] + recv[:, :width] + bias[11:12, :] + SCALE * nn(u, ad[1])
    x2[...] = end
    unit, _ = norm_parts(end)
    token = jnp.sum((unit * gains[2:3, :] + bias[2:3, :]) * head[...], -1, keepdims=True)
    score[...] = jnp.broadcast_to(token, score.shape)


def loss_kernel(rank, members, ready, *refs):
    scores = refs[:members]
    x2, u_dn, pairs, count, ad, gains, bias, head = refs[members : members + 8]
    e2, g_end, g_dn, small = refs[members + 8 :]
    ready()
    rows, width = x2.shape
    half = rows // 2

    def value(m):
        if m % 2 == 0:
            return scores[m][...]
        return jnp.concatenate([scores[m][half:, :], scores[m][:half, :]], 0)

    level = [value(m) for m in range(members)]
    while len(level) > 1:
        level = [level[i] + level[i + 1] for i in range(0, len(level), 2)]
    mean_reward = level[0][:, :1] / members
    at = iota((rows, pairs.shape[1]), 0)
    pick = (at == pairs[0:1, :]).astype(F32) - (at == pairs[1:2, :]).astype(F32)
    live = (pairs[0:1, :] >= 0).astype(F32)
    diff = jnp.sum(pick * mean_reward, 0, keepdims=True)
    terms = live * jax.nn.softplus(-diff)
    grad_diff = -live * jax.nn.sigmoid(-diff) / count[:, :1]
    grad_score = jnp.sum(pick * grad_diff, -1, keepdims=True) / members
    unit, rstd = norm_parts(x2[...])
    final = unit * gains[2:3, :] + bias[2:3, :]
    small[...] = jnp.zeros_like(small)
    small[0:1, :] = jnp.sum(final * grad_score, 0, keepdims=True)
    small[1:2, :] = jnp.broadcast_to(jnp.sum(terms, -1, keepdims=True), (1, width))
    end = norm_back(grad_score * head[...], gains[2:3, :], unit, rstd)
    g_end[...] = end
    g_ff = end.astype(BF16)
    left = lanes((SCALE * nt(g_ff, ad[1])).astype(BF16), 4 * rank, 5 * rank)
    g_dn[...] = SCALE * tn(u_dn[...], g_ff)
    e2[:, :width] = g_ff
    e2[:, width:] = jnp.zeros_like(e2[:, width:])
    e2[:, width : width + 5 * rank] = left


def slope_kernel(ready, f, _, out):
    x = f[...]
    c0, c1 = math.sqrt(2.0 / math.pi), 0.044715
    t = jnp.tanh(c0 * (x + c1 * x * x * x))
    out[...] = 0.5 * (1.0 + t) + 0.5 * x * (1.0 - t * t) * (c0 * (1.0 + 3.0 * c1 * x * x))


def ffn_back_kernel(rank, ready, own, sib, slope, f_own, f_sib, wide_u, wide_d,
                    mine, send, g_out):
    width = wide_u.shape[0]
    lane = 5 * rank
    ready()
    rows = own.shape[0]
    left_own, left_sib = own[:, width : width + lane], sib[:, width : width + lane]
    g_ff = jnp.concatenate([own[:, :width], sib[:, :width]], 0)
    pair_own, pair_sib = factors(f_own, rank), factors(f_sib, rank)
    extra = jnp.concatenate([nn(left_own, pair_own[0]), nn(left_sib, pair_sib[0])], 0)
    g_a = (nt(g_ff, wide_d[...]) + extra).astype(BF16)
    g_f = (g_a.astype(F32) * slope[...]).astype(BF16)
    g_h = nt(g_f, wide_u[...])
    for out, low, factor in ((mine, 0, pair_own), (send, rows, pair_sib)):
        out[:, :width] = g_h[low : low + rows]
        out[:, width:] = jnp.zeros_like(out[:, width:])
        out[:, width : width + lane] = SCALE * nt(g_f[low : low + rows], factor[1])
    g_out[...] = g_f


def hidden_kernel(rank, ready, own, sib, e1_own, e1_sib, a, g_f, mine, send):
    rows = own.shape[0]
    cut = slice(own.shape[1] - 128, own.shape[1] - 128 + 5 * rank)
    for out, low, left, u in ((mine, 0, own, e1_own), (send, rows, sib, e1_sib)):
        out[0:rank, :] = tn(left[:, cut], a[low : low + rows, :])[4 * rank :]
        out[rank:, :] = SCALE * tn(u[:, cut], g_f[low : low + rows, :])[4 * rank :]


def factor_kernel(rank, half, ready, mine, other, err, start, mat, left):
    ready()
    core = lax.axis_index("shard") % 2
    first = (core == 0).astype(F32)
    even = mine[...] * first + other[...] * (1.0 - first)
    odd = mine[...] * (1.0 - first) + other[...] * first
    parts = []
    for r in range(mine.shape[1] // half):
        cut = slice(r * half, (r + 1) * half)
        parts += [even[:, cut], odd[:, cut]]
    mat[...] = jnp.concatenate(parts, 1) + err[...]
    left[...] = nn(start[...], mat[...], EXACT)


def rows_back_kernel(micro, rank, ready, *refs):
    mine, recv, g_end, g_dn, small, x1, e1, u, o, q, p_t, kv, ukv_t = refs[:13]
    hl = refs[13 : 13 + micro]
    h1 = refs[13 + micro : 13 + 2 * micro]
    ad, gains, err, start, w_out, mat, left = refs[13 + 2 * micro :]
    rows, width = x1.shape
    slots = rows // micro
    heads = width // HEAD_DIM
    lane = 5 * rank
    down, up = ad[0], ad[1]
    h2 = e1[:, :width]
    u_rows = u[...]
    g_u = (mine[:, width : width + lane] + recv[:, width : width + lane]).astype(BF16)
    g_h2 = (mine[:, :width] + recv[:, :width] + nn(g_u, down)).astype(BF16)
    grad_in = tn(g_u, h2)
    unit, rstd = norm_parts(x1[...])
    g_mid = g_end[...] + norm_back(g_h2.astype(F32), gains[1:2, :], unit, rstd)
    g_att = g_mid.astype(BF16)
    grad_out = g_dn[...] + SCALE * tn(lanes(u_rows, 3 * rank, 4 * rank), g_att)
    g_ol = lanes((SCALE * nt(g_att, up)).astype(BF16), 3 * rank, 4 * rank)
    grad_in = grad_in + tn(g_ol, o[...])
    g_o = (nt(g_att, w_out[...]) + nn(g_ol, down)).astype(BF16)
    ready()
    scale = HEAD_DIM ** (-0.5)

    both = (lane, 2 * heads * slots)
    group, side = iota(both, 0) // rank, iota(both, 1) // (heads * slots)
    keep = jnp.where(group == 1 + side, jnp.where(side == 0, scale, 1.0), 0.0)

    for b in range(micro):
        pick = slice(b * slots, (b + 1) * slots)
        wide_g = expand_heads(g_o[pick], heads)
        wide_q = expand_heads(q[pick, :], heads)
        probs = p_t[b]
        g_p = nt(kv[b, :, width:], wide_g)
        g_s = (probs * (g_p - jnp.sum(probs * g_p, 0, keepdims=True))).astype(BF16)
        g_q = (scale * collapse_heads(tn(g_s, kv[b, :, :width]), heads)).astype(BF16)
        u_q = lanes(u_rows[pick], 0, rank)
        tall = jnp.concatenate([g_s, probs.astype(BF16)], 1)
        flat = jnp.concatenate([wide_q, wide_g], 0)
        inner = (nn(ukv_t[b], tall) * keep).astype(BF16)
        grad_out = grad_out + SCALE * (tn(u_q, g_q) + nn(inner, flat))
        g_uq = lanes((SCALE * nt(g_q, up)).astype(BF16), 0, rank)
        inner = (nt(up, flat) * keep).astype(BF16)
        g_ukv = (SCALE * nt(inner, tall)).astype(BF16)
        grad_in = grad_in + tn(g_uq, hl[b][...]) + nn(g_ukv, h1[b][...])
    mat[0] = grad_in + err[0]
    mat[1] = grad_out + err[1]
    first = start.shape[1]
    left[0:first, :] = nn(start[0], mat[0], EXACT)
    left[first : 2 * first, :] = nn(start[1], mat[1], EXACT)
    left[2 * first :, :] = small[...]


def orthonormal_rows(refs):
    count = refs[0].shape[0]
    for k in range(count):
        for ref in refs:
            block = ref[...]
            row = block[k : k + 1, :]
            dots = jnp.sum(block * row, -1, keepdims=True)
            scale = lax.rsqrt(dots[k : k + 1] + 1e-06)
            row = row * scale
            at = iota(block.shape, 0)
            later = jnp.where(at > k, block - (dots * scale) * row, block)
            ref[...] = jnp.where(at == k, row, later)


def ortho_kernel(rank, ready, d_a, d_b, f_a, f_b, mat_d, mat_f, ph_d, ph_f, head, note):
    count = rank
    for j in range(2):
        part = slice(j * count, (j + 1) * count)
        ph_d[j] = d_a[part, :] + d_b[part, :]
    ph_f[...] = f_a[...] + f_b[...]
    rest = d_a[2 * count :, :] + d_b[2 * count :, :]
    refs = (ph_d.at[0], ph_d.at[1], ph_f)
    orthonormal_rows(refs)
    ready()
    grad = rest[0:1, :]
    head[...] = grad
    parts = []
    for ref, mat in zip(refs, (mat_d.at[0], mat_d.at[1], mat_f), strict=True):
        parts.append(nt(ref[...], mat[...], EXACT))
    for ref in refs:
        parts.append(nt(ref[...], ref[...], EXACT))
    parts.append(jnp.broadcast_to(jnp.sum(grad * grad, keepdims=True), (count, 1)))
    parts.append(jnp.broadcast_to(rest[1:2, :1], (count, 1)))
    used = sum(x.shape[1] for x in parts)
    parts.append(jnp.zeros((count, 128 - used), F32))
    own = jnp.concatenate(parts, 1)

    @pl.loop(0, note.shape[0])
    def _(i):
        note[i] = own


def final_kernel(rank, n, m, ready, notes, ph_d, ph_f, ph_do, ph_fo, ghead, mat_d, mat_f,
                 wd, wf, wh, md, mf, mh,
                 nd, nf, nh, nmd, nmf, nmh, err_d, err_f, q_d, q_f, mean_loss, norm):
    ready()
    shard = lax.axis_index("shard")
    count = rank
    sizes = (5 * rank, 5 * rank, 2 * rank)
    total = jnp.zeros((1, 1), F32)
    loss = jnp.zeros((1, 1), F32)
    own = jnp.zeros((count, 128), F32)
    for s in range(m):
        block = notes[s]
        for r in range(1, n):
            block = block + notes[r * m + s]
        own = jnp.where(shard == s, block, own)
        note = notes[s]
        at, gram = 0, sum(sizes)
        for size in sizes:
            right = block[:, at : at + size]
            inner = note[:, gram : gram + count]
            total = total + jnp.sum(right * nn(inner, right, EXACT), keepdims=True)
            at += size
            gram += count
        total = total + note[0:1, gram : gram + 1]
        loss = loss + note[0:1, gram + 1 : gram + 2]
    grad_norm = jnp.sqrt(total)
    clip = jnp.minimum(1.0, CLIP / (grad_norm + 1e-06))
    mean_loss[...] = loss / m
    norm[...] = grad_norm
    at = 0
    for j in range(2):
        right = own[:, at : at + sizes[j]]
        q_d[j] = right
        at += sizes[j]
        err_d[j] = mat_d[j] - tn(right, ph_d[j], EXACT) * (1.0 / n)
        fresh = MOMENTUM * md[j] + clip * tn(right, ph_do[j], EXACT)
        nmd[j] = fresh
        nd[j] = wd[j] - RATE * fresh
    right = own[:, at : at + sizes[2]]
    q_f[...] = right
    err_f[...] = mat_f[...] - tn(right, ph_f[...], EXACT) * (1.0 / n)
    fresh = MOMENTUM * mf[...] + clip * tn(right, ph_fo[...], EXACT)
    nmf[...] = fresh
    nf[...] = wf[...] - RATE * fresh
    fresh = MOMENTUM * mh[...] + clip * ghead[...]
    nmh[...] = fresh
    nh[...] = wh[...] - RATE * fresh


class Raw:
    def __init__(self, array):
        self.array = array


class Scalars(Raw):
    pass


class Far(Raw):
    pass


class Fresh(Raw):
    pass


class Part:
    def __init__(self, array, rows):
        self.array, self.rows = array, rows


class Kept:
    def __init__(self, shape, dtype):
        self.shape, self.dtype = tuple(shape), dtype


class Placed(Kept):
    pass


def call(body, outs, args, scratch=(), vmem=60, name=None, groups=None, aliases=None, flushes=False):
    arrays, specs, staged = [], [], []
    for arg in args:
        arrays.append(arg.array if isinstance(arg, Raw | Part) else arg)
        space = pl.ANY
        if isinstance(arg, Scalars):
            space = pltpu.SMEM
        elif isinstance(arg, Fresh):
            space = pltpu.VMEM
        elif isinstance(arg, Far):
            space = pltpu.HBM
        specs.append(pl.BlockSpec(memory_space=space))
        if isinstance(arg, Part):
            staged.append(pltpu.VMEM((arg.rows, *arg.array.shape[1:]), arg.array.dtype))
        elif not isinstance(arg, Raw):
            staged.append(pltpu.VMEM(arg.shape, arg.dtype))
    results = [pltpu.VMEM(o.shape, o.dtype) for o in outs if not isinstance(o, Kept)]

    def kernel(*refs):
        ins, refs = refs[: len(args)], refs[len(args) :]
        targets, refs = refs[: len(outs)], refs[len(outs) :]
        held, refs = refs[: len(staged)], refs[len(staged) :]
        buffers, refs = refs[: len(results)], refs[len(results) :]
        extra, sems = refs[:-1], refs[-1]
        copies, given, i = {}, [], 0
        for arg, ref in zip(args, ins, strict=True):
            if isinstance(arg, Raw):
                given.append(ref)
                continue
            origin = ref.at[pl.ds(0, arg.rows)] if isinstance(arg, Part) else ref
            copies[id(held[i])] = pltpu.make_async_copy(origin, held[i], sems.at[i])
            given.append(held[i])
            i += 1
        for copy in copies.values():
            copy.start()

        def ready(*some):
            for key in [id(r) for r in some] or list(copies):
                copies.pop(key).wait()

        local, back, i = [], {}, 0
        for j, out in enumerate(outs):
            if isinstance(out, Kept):
                local.append(targets[j])
                continue
            local.append(buffers[i])
            back[j] = pltpu.make_async_copy(buffers[i], targets[j], sems.at[len(staged) + i])
            i += 1
        def flush(j):
            back[j].start()
            begun.append(j)

        begun = []
        if groups:
            given = [given[:groups], *given[groups:]]
        body(ready, *((flush,) if flushes else ()), *given, *local, *extra)
        for j, copy in back.items():
            if j not in begun:
                copy.start()
        for copy in back.values():
            copy.wait()

    def place(out):
        if type(out) is Kept:
            return pltpu.VMEM
        return pl.ANY if isinstance(out, Kept) else pltpu.HBM

    return pl.pallas_call(
        kernel,
        out_shape=tuple(jax.ShapeDtypeStruct(o.shape, o.dtype) for o in outs),
        in_specs=specs,
        out_specs=tuple(pl.BlockSpec(memory_space=place(o)) for o in outs),
        scratch_shapes=[
            *staged, *results, *scratch, pltpu.SemaphoreType.DMA((max(1, len(staged) + len(results)),)),
        ],
        compiler_params=pltpu.CompilerParams(vmem_limit_bytes=vmem << 20),
        cost_estimate=pl.CostEstimate(flops=0, bytes_accessed=0, transcendentals=0),
        input_output_aliases=aliases or {},
        name=name,
    )(*arrays)


def shaped(shape, dtype):
    return jax.ShapeDtypeStruct(tuple(shape), dtype)


def ring_order(count):
    side = math.isqrt(count // 2)
    if side < 2 or 2 * side * side != count:
        return list(range(count))
    depth = 2 * side
    cells = []
    for z in range(depth):
        ys = range(1, side) if z % 2 == 0 else range(side - 1, 0, -1)
        cells += [(z, y) for y in ys]
    cells += [(z, 0) for z in range(depth - 1, -1, -1)]
    return [z * side + y for z, y in cells]


def pairs_of(n, m, move):
    return [(r * m + s, t[0] * m + t[1]) for r in range(n) for s in range(m) for t in [move(r, s)]]


def on_device(n, m, *args):
    (
        token_ids, positions, segment_ids, pair_index, embed_table, pos_table,
        base_qkv, base_out, base_up, base_down, base_gains, base_bias,
        adapt_d, adapt_f, head, mom_d, mom_f, mom_head, err_d, err_f, qstart_d, qstart_f,
    ) = args
    micro, tokens = token_ids.shape
    held, width = embed_table.shape
    pairs = pair_index.shape[1]
    slots = 2 * pairs
    rows = micro * slots
    hidden = base_up.shape[1]
    rank = adapt_f.shape[2] // 2
    heads = width // HEAD_DIM
    rd, rf = base_up.shape[0], base_down.shape[0]
    half = rf // 2
    own_hidden = hidden // 2
    rep, shard = lax.axis_index("rep"), lax.axis_index("shard")
    core = shard % 2

    order = ring_order(n)
    place = {r: i for i, r in enumerate(order)}
    around = pairs_of(
        n, m, lambda r, s: (order[(place[r] + (1 if s % 2 == 0 else -1)) % n], s)
    )
    turns = [
        [[order[(place[r] + (-k if c == 0 else k)) % n] for k in range(n)] for c in range(2)]
        for r in range(n)
    ]
    source = Scalars(jnp.asarray(np.array(turns, np.int32)))

    def send(x, perm):
        return lax.ppermute(x, AXES, perm)

    def across(x, mask):
        return send(x, pairs_of(n, m, lambda r, s: (r, s ^ mask)))

    def ring(x):
        out = []
        for _ in range(n - 1):
            x = send(x, around)
            out.append(x)
        return out

    def pick(x, index, axis):
        return lax.dynamic_index_in_dim(x, index, axis, keepdims=False)

    d_t = adapt_d[0].transpose(1, 2, 0)
    f_t = adapt_f[0].T
    below = 2 * rank
    live = pair_index[..., 0].reshape(1, micro * pairs)
    whole_blocks = rd % 128 == 0 and half % 128 == 0
    if whole_blocks:
        left, right, up_part, down_part = call(
            split_kernel,
            [shaped((rd + below, width), BF16), shaped((rd + below, width), BF16),
             shaped((rd, own_hidden), BF16), shaped((half, width), BF16)],
            [d_t, f_t, head, live, Raw(base_qkv), Raw(base_out), Raw(base_up), Raw(base_down)],
            [pltpu.SemaphoreType.DMA((n + 5,))],
            vmem=56, name="split",
        )
    else:
        two = jnp.concatenate([head, jnp.broadcast_to(jnp.sum((live >= 0).astype(F32)), (below - 1, rd))], 0)
        flat = [x for x in d_t.reshape(10 * rank // below, below, rd)]
        first = jnp.concatenate([base_qkv, base_out], 1).reshape(rd, 4, 2, width // 2)
        first = pick(first, core, 2).reshape(rd, 2, width)
        sides = []
        for side, extra in enumerate((jnp.concatenate([*flat, two], 1), f_t)):
            extra = jnp.pad(extra.astype(BF16), ((0, 0), (0, width - extra.shape[1])))
            sides.append(jnp.concatenate([first[:, side], extra], 0))
        left, right = sides
        up_part = pick(base_up.reshape(rd, n, 2, half), core, 2).reshape(rd, own_hidden)
        down_part = pick(base_down.reshape(2, half, width), core, 0)

    def after(x, *others):
        return pl.pallas_call(
            lambda *refs: None,
            out_shape=jax.ShapeDtypeStruct(x.shape, x.dtype),
            in_specs=[pl.BlockSpec(memory_space=pl.ANY)] * (1 + len(others)),
            out_specs=pl.BlockSpec(memory_space=pl.ANY),
            input_output_aliases={0: 0},
            cost_estimate=pl.CostEstimate(flops=0, bytes_accessed=0, transcendentals=0),
            name="after",
        )(x, *others)

    def lookup(*start):
        ids = jnp.stack([pick(token_ids, (core + b) % micro, 0) for b in range(micro)])
        near = ids - shard * held
        inside = (near >= 0) & (near < held)
        found = jnp.take(embed_table, after(jnp.clip(near, 0, held - 1), *start), axis=0)
        found = jnp.where(inside[..., None], found, jnp.zeros_like(found))
        return found[0], found[1]

    def shared(own, given, *others):
        own = own + across(after(given, *others), 1)
        mask = 2
        while mask < m // 2:
            own = own + across(own, mask)
            mask *= 2
        return own, across(own, mask) if m > 2 else own

    bias = base_bias.reshape(-1, width)
    bias_1 = pick(base_bias[7 * width : 7 * width + hidden].reshape(n, 2, half), core, 1)
    bias_1 = bias_1.reshape(1, own_hidden)
    local = (jnp.arange(micro) + core) % micro * slots
    pair_rows = jnp.where(pair_index >= 0, pair_index + local[:, None, None], -1)
    pair_rows = pair_rows.reshape(micro * pairs, 2).T

    pos_rows = pos_table[:tokens]

    lefts, rights, ups, downs = [left], [right], [up_part], [down_part]

    def behind(low, high, *gate):
        for k in range(low, min(high, n)):
            if gate:
                ups[-1], downs[-1] = after(ups[-1], *gate), after(downs[-1], *gate)
            gate = ()
            ups.append(send(ups[-1], around))
            downs.append(send(downs[-1], around))

    for k in range(1, n):
        gate = []
        if k == 9:
            gate = [ups[1], downs[1]]
        if k == 4:
            gate = [tok_own, bias, bias_1, pos_rows, pair_rows]
        if k == 9:
            gate = [tok_far]
        if gate:
            lefts[-1], rights[-1] = after(lefts[-1], *gate), after(rights[-1], *gate)
        lefts.append(send(lefts[-1], around))
        rights.append(send(rights[-1], around))
        if k == 1:
            ups[-1], downs[-1] = ups[-1], downs[-1]
            ups.append(send(ups[-1], around))
            downs.append(send(downs[-1], around))
            own, given = lookup(left)
        if k == 1:
            tok_own, tok_far = shared(own, given, lefts[1], rights[1], ups[1], downs[1])

    parts = [tok_own, tok_far] if m > 2 else [tok_own]
    both = tok_own + tok_far if m > 2 else tok_own
    toks = [parts, [across(both, 1)]]

    step_a = [*lefts, *rights]
    if whole_blocks:
        mats = []
        for k in range(4):
            mats += call(
                functools.partial(assemble_kernel, k % 2),
                [shaped((width, width // 2), BF16)],
                [source, *[Far(x) for x in (lefts, rights)[k // 2]]],
                [pltpu.SemaphoreType.DMA((n,))],
                vmem=8, name="assemble",
            )
        wide_d, f_own, f_other, wide_head, count_row = call(
            functools.partial(unpack_kernel, rank, rd),
            [shaped((2, 5 * rank, width), BF16), shaped((2 * rank, own_hidden), BF16),
             Kept((2 * rank, own_hidden), BF16), shaped((1, width), F32), shaped((1, 128), F32)],
            [source, *[Far(x) for x in step_a]],
            [pltpu.VMEM((10 * rank + below, width), BF16), pltpu.VMEM((below, hidden), BF16),
             pltpu.SemaphoreType.DMA((n * (10 * rank // below + 2),))],
            vmem=52, name="unpack",
        )
    else:
        turned = jnp.asarray(np.argsort(np.array(turns, np.int32), -1).astype(np.int32))
        place_at = lax.dynamic_slice(turned, (rep, core, 0), (1, 1, n)).reshape(n)
        steps_l, steps_r = [
            jnp.stack([pick(jnp.stack(x), place_at[r], 0) for r in range(n)]) for x in (lefts, rights)
        ]
        mats = [x[:, :rd].reshape(width, 2, width // 2) for x in (steps_l, steps_r)]
        mats = [x[:, j] for x in mats for j in range(2)]
        count_d = 10 * rank // below
        wide_d = steps_l[:, rd:, : count_d * rd].reshape(n, below, count_d, rd)
        wide_d = wide_d.transpose(2, 1, 0, 3).reshape(2, 5 * rank, width)
        wide_f = steps_r[:, rd:, :rf].reshape(n, 2 * rank, 2, half)
        wide_f = wide_f.transpose(2, 1, 0, 3).reshape(2, 2 * rank, own_hidden)
        f_own, f_other = pick(wide_f, core, 0), pick(wide_f, 1 - core, 0)
        last = steps_l[:, rd:, count_d * rd : (count_d + 1) * rd].astype(F32)
        wide_head = last[:, 0].reshape(1, width)
        count_row = jnp.broadcast_to(jnp.sum(last[:, 1, 0]), (1, 128))
    count = count_row[0, 0]
    f_sib = across(f_other, 1)
    mats += [across(x, 1) for x in mats]

    h1, xl, hl = [], [], []
    for b in range(micro):
        a, x, h = call(
            functools.partial(front_kernel, b),
            [shaped((tokens, width), BF16), shaped((slots, width), F32), shaped((slots, width), BF16)],
            [*toks[b], positions, segment_ids, pos_rows, base_gains, bias],
            [pltpu.VMEM((tokens, width), BF16), pltpu.VMEM((tokens, width), BF16)],
            groups=len(toks[b]), vmem=56, name="front",
        )
        h1.append(a)
        xl.append(x)
        hl.append(h)

    behind(2, 3, lefts[5])
    behind(3, 4, *mats[:2])
    behind(4, 5, *mats[2:4], hl[0])
    behind(5, 6, hl[1], wide_d)
    behind(6, 7)
    kv, ukv_t, o, x1, q, p_t, u, w_out, e1 = call(
        functools.partial(rows_kernel, micro, rank),
        [shaped((micro, tokens, 2 * width), BF16), shaped((micro, 5 * rank, tokens), BF16),
         shaped((rows, width), BF16), shaped((rows, width), F32), shaped((rows, width), BF16),
         shaped((micro, tokens, heads * slots), F32), shaped((rows, 5 * rank), BF16),
         shaped((width, width), BF16), shaped((rows, width + 128), BF16)],
        [segment_ids, *h1, *hl, *xl, wide_d, base_gains, bias, *mats],
        [pltpu.VMEM((micro, tokens, 5 * rank), BF16)],
        vmem=60, flushes=True, name="rows",
    )
    behind(7, n, o)
    ups, downs = [[Far(y) for y in x] for x in (ups, downs)]
    e1_sib = across(e1, 1)
    w_up, w_down = call(
        functools.partial(preload_kernel, n - 1),
        [Kept((width, own_hidden), BF16), Kept((own_hidden, width), BF16)],
        [source, Raw(o), *ups[:-1], *downs[:-1]],
        [pltpu.SemaphoreType.DMA((2, n - 1))],
        vmem=4, name="preload",
    )
    f, a, w_up, w_down, y_mine, y_send = call(
        functools.partial(ffn_kernel, rank, n - 1),
        [Kept((2 * rows, own_hidden), F32), Kept((2 * rows, own_hidden), BF16),
         Kept((width, own_hidden), BF16), Kept((own_hidden, width), BF16)]
        + [Kept((rows, width + 128), F32)] * 2,
        [source, Fresh(e1), Fresh(e1_sib), f_own, f_sib, bias_1, ups[-1], downs[-1], Fresh(w_up), Fresh(w_down)],
        [pltpu.SemaphoreType.DMA((2, 1))],
        aliases={8: 2, 9: 3}, vmem=10, name="ffn",
    )
    x2, u_dn, score = call(
        functools.partial(score_kernel, rank),
        [Kept((rows, width), F32), Kept((rows, 5 * rank), BF16), Kept((rows, 128), F32)],
        [Fresh(x1), Fresh(y_mine), Fresh(across(y_send, 1)), wide_d, base_gains, bias, wide_head],
        vmem=10, name="score",
    )
    scores = [score] + [across(score, k) for k in range(1, m)]
    (slope,) = call(
        slope_kernel,
        [Kept((2 * rows, own_hidden), F32)],
        [Fresh(f), Fresh(score)],
        vmem=6, name="slope",
    )
    e2, g_end, g_dn, small = call(
        functools.partial(loss_kernel, rank, m),
        [Kept((rows, width + 128), BF16), Kept((rows, width), F32), Kept((5 * rank, width), F32),
         Kept((8, width), F32)],
        [*[Fresh(x) for x in scores], Fresh(x2), Fresh(u_dn), pair_rows, count_row, wide_d, base_gains, bias, wide_head],
        vmem=10, name="loss",
    )
    e2_sib = across(e2, 1)
    y_mine, y_send, g_f = call(
        functools.partial(ffn_back_kernel, rank),
        [Kept((rows, width + 128), F32)] * 2 + [Kept((2 * rows, own_hidden), BF16)],
        [Fresh(e2), Fresh(e2_sib), Fresh(slope), Fresh(f_own), Fresh(f_sib),
         Fresh(w_up), Fresh(w_down)],
        vmem=14, name="ffn_back",
    )
    y_other = across(y_send, 1)
    gf_mine, gf_send = call(
        functools.partial(hidden_kernel, rank),
        [Kept((2 * rank, own_hidden), F32)] * 2,
        [Fresh(x) for x in (e2, e2_sib, e1, e1_sib, a, g_f)],
        vmem=6, name="hidden",
    )
    mat_f, left_f = call(
        functools.partial(factor_kernel, rank, half),
        [Kept((2 * rank, hidden), F32), Kept((rank, hidden), F32)],
        [Fresh(gf_mine), Fresh(across(gf_send, 1)), err_f[0, 0].T, qstart_f[0].T],
        vmem=10, name="factor_f",
    )
    mat_d, left_d = call(
        functools.partial(rows_back_kernel, micro, rank),
        [Kept((2, 5 * rank, width), F32), Kept((2 * rank + 8, width), F32)],
        [Fresh(y_mine), Fresh(y_other), Fresh(g_end), Fresh(g_dn), Fresh(small),
         *[Fresh(x) for x in (x1, e1, u, o, q, p_t, kv, ukv_t, *hl, *h1)],
         Fresh(wide_d), Fresh(base_gains), err_d[0, 0].transpose(1, 2, 0), qstart_d[0].transpose(0, 2, 1), Fresh(w_out)],
        vmem=26, name="rows_back",
    )

    def rep_parts(x, order):
        part = jnp.zeros_like(x)
        bits = [1 << k for k in range(n.bit_length() - 1)][::order]
        for bit in bits:
            part = send(x, pairs_of(n, m, lambda r, s, bit=bit: (r ^ bit, s)))
            if bit != bits[-1]:
                x = x + part
        return Fresh(x), Fresh(part)

    ph_d, ph_f, total_head, note = call(
        functools.partial(ortho_kernel, rank),
        [Kept((2, rank, width), F32), Kept((rank, hidden), F32), Kept((1, width), F32),
         Kept((n * m, rank, 128), F32)],
        [*rep_parts(left_d, 1), *rep_parts(left_f, -1), Fresh(mat_d), Fresh(mat_f)],
        vmem=10, name="ortho",
    )
    notes = lax.all_to_all(note, AXES, 0, 0)
    own_ph_d = lax.dynamic_slice_in_dim(ph_d, rep * rd, rd, 2)
    own_ph_f = lax.dynamic_slice_in_dim(ph_f, rep * rf, rf, 1)
    own_head = lax.dynamic_slice_in_dim(total_head, rep * rd, rd, 1)
    nd, nf, nh, nmd, nmf, nmh, new_err_d, new_err_f, q_d, q_f, loss_sum, norm = call(
        functools.partial(final_kernel, rank, n, m),
        [shaped((2, 5 * rank, rd), F32), shaped((2 * rank, rf), F32), shaped((1, rd), F32)] * 2
        + [shaped((2, 5 * rank, width), F32), shaped((2 * rank, hidden), F32),
           shaped((2, rank, 5 * rank), F32), shaped((rank, 2 * rank), F32), shaped((1, 1), F32), shaped((1, 1), F32)],
        [Fresh(notes), Fresh(ph_d), Fresh(ph_f), Fresh(own_ph_d), Fresh(own_ph_f), Fresh(own_head),
         Fresh(mat_d), Fresh(mat_f), d_t, f_t, head, mom_d[0].transpose(1, 2, 0), mom_f[0].T, mom_head],
        vmem=16, name="final",
    )
    return (
        loss_sum[0, 0],
        count,
        norm[0, 0],
        nd.transpose(2, 0, 1)[None],
        nf.T[None],
        nh,
        nmd.transpose(2, 0, 1)[None],
        nmf.T[None],
        nmh,
        new_err_d.transpose(2, 0, 1)[None, None],
        new_err_f.T[None, None],
        q_d.transpose(0, 2, 1)[None],
        q_f.T[None],
    )


def solution(mesh):
    n, m = mesh.shape["rep"], mesh.shape["shard"]
    return jax.shard_map(
        functools.partial(on_device, n, m),
        mesh=mesh,
        in_specs=(
            P("rep", None),
            P("rep", None),
            P("rep", None),
            P("rep", None, None),
            P("shard", None),
            P(),
            P("rep", None),
            P("rep", None),
            P("rep", None),
            P("rep", None),
            P(),
            P(),
            P("shard", "rep", None, None),
            P("shard", "rep", None),
            P("shard", "rep"),
            P("shard", "rep", None, None),
            P("shard", "rep", None),
            P("shard", "rep"),
            P("shard", "rep", None, None, None),
            P("shard", "rep", None, None),
            P("shard", None, None, None),
            P("shard", None, None),
        ),
        out_specs=(
            P(),
            P(),
            P(),
            P("shard", "rep", None, None),
            P("shard", "rep", None),
            P("shard", "rep"),
            P("shard", "rep", None, None),
            P("shard", "rep", None),
            P("shard", "rep"),
            P("shard", "rep", None, None, None),
            P("shard", "rep", None, None),
            P("shard", None, None, None),
            P("shard", None, None),
        ),
        check_vma=False,
    )
```
